128 devices in a mesh: sec: 2 (over core), row: 8 (over x, z_lo), nest: 8 (over y, z_hi).
Axes of the slice: x: 4, y: 4, z: 4 (z_hi: 2, z_lo: 2; z = z_hi * 2 + z_lo), core: 2. Of those that a mesh axis runs over, the one named last changes fastest.
Arguments:
- ocean_state: float32 [2, 3, 512, 1024], P('sec', None, 'row', 'nest'), may hold values from -1.2 to 1.2
- face_depth: float32 [2, 2, 512, 1024], P('sec', None, 'row', 'nest'), may hold values from 2 to 4
- face_open: int32 [2, 2, 512, 1024], P('sec', None, 'row', 'nest'), may hold values 0 or 1
- nest_place: int32 [64], replicated, may hold values from 0 to 383, as said below
- nest_host: int32 [64], replicated, may hold values from 0 to 127, as said below
Outputs:
- final_state: float32 [2, 3, 512, 1024], P('sec', None, 'row', 'nest')
The draws below stay inside these ranges and needn't reach their ends.
Inputs may be any that keep to these rules, and one draw needn't show every extreme that they name: `nest_place`: distinct positions; the first and the last position are always covered. `nest_host`: distinct slots; both slots of some device hold a nest; the nest at the first position lives in the last slot and the nest at the last position in the first slot.
All inputs are finite; a program needn't handle non-finite values. No bound on the sum of `face_open` on one device may be relied on, other than what follows from the above.
Results may differ from the reference program's by a relative error of at most 0.00013.
Values sent between devices are 32-bit elements; how exact they have to be, the bound alone decides.
No kernel may reach another device: no remote copies, remote signals or barrier semaphores. Data moves between devices by JAX's collectives and lax.ppermute only.
A program may use at most 64 MiB of HBM per device.

```python
import math
import jax
import jax.numpy as jnp
from jax import lax

PH = 8
PW = 32
RR = 4
K = 2
STEPS = 4
NT = 64
SLOTS = 128
NPOS = 6
NESTS = 64
OH = 512
OW = 1024
N_ROW = 8
N_NEST = 8


def draw_nest_place(key, part):
    total = NT * NPOS
    inner = jax.random.permutation(jax.random.fold_in(key, 11), total - 2).astype(jnp.int32) + 1
    chosen = jnp.concatenate([jnp.array([0, total - 1], jnp.int32), inner[:NESTS - 2]])
    shuffle = jax.random.permutation(jax.random.fold_in(key, 12), NESTS)
    return chosen[shuffle].astype(jnp.int32)


def draw_nest_host(key, part):
    base_key = jax.random.fold_in(key, 23)
    chosen = jax.random.randint(jax.random.fold_in(base_key, 1), (), 0, NT)
    ordering = jax.random.permutation(jax.random.fold_in(base_key, 2), SLOTS).astype(jnp.int32)
    flagged = (ordering // K == chosen).astype(jnp.int32)
    counter = jnp.arange(SLOTS, dtype=jnp.int32)
    scores = jnp.where(ordering == SLOTS - 1, 0, jnp.where(ordering == 0, 1, (3 - flagged) * SLOTS + counter)).astype(jnp.int32)
    assigned = ordering[jnp.argsort(scores)][:NESTS]
    shuffle = jax.random.permutation(jax.random.fold_in(key, 12), NESTS)
    return assigned[shuffle].astype(jnp.int32)


def plant(values, own_key, least, largest):
    dims = values.shape
    spot = [jax.random.randint(jax.random.fold_in(own_key, axis), (), 0, dims[axis]) for axis in range(len(dims))]
    values = values.at[tuple(spot)].set(least)
    longest = dims.index(max(dims))
    spot[longest] = (spot[longest] + 1) % dims[longest]
    return values.at[tuple(spot)].set(largest)


def block_levels(stream_key, dims, pieces, least, largest):
    gain, own = 1.0, jax.random.fold_in(stream_key, 6)
    for dim, blocks in pieces:
        draws = jnp.exp(jax.random.uniform(jax.random.fold_in(own, dim), (blocks,), jnp.float32, least / len(pieces), largest / len(pieces)))
        gain = gain * jnp.repeat(draws, dims[dim] // blocks).reshape([-1 if axis == dim else 1 for axis in range(len(dims))])
    return gain


def normal_values(stream_key, dims, spread, reach, shards=(), kind=jnp.bfloat16):
    gain = block_levels(stream_key, dims, shards, -0.22, 0.18) if shards else 1.0
    values = jax.random.normal(stream_key, dims, jnp.float32) * spread * gain
    return jnp.minimum(jnp.maximum(values, -reach), reach).astype(kind)


def setup_inputs(seed: int = 0) -> dict:
    keys = jax.random.split(jax.random.key(seed), 6)
    return {
        "ocean_state": normal_values(keys[0], (2, 3, OH, OW), 0.3, 1.2, ((0, 2), (2, 8), (3, 8)), jnp.float32),
        "face_depth": jnp.clip(jnp.exp(math.log(4.0) - 0.6931472 * jax.random.uniform(keys[1], (2, 2, OH, OW), jnp.float32) ** block_levels(keys[1], (2, 2, OH, OW), ((0, 2), (2, 8), (3, 8)), -0.2, 0.2)), 2.0, 4.0),
        "face_open": plant((jax.random.randint(keys[2], (2, 2, OH, OW), 0, 8) < 7).astype(jnp.int32), jax.random.fold_in(keys[2], 1), 0, 1),
        "nest_place": draw_nest_place(jax.random.fold_in(keys[5], 71), 0),
        "nest_host": draw_nest_host(jax.random.fold_in(keys[5], 71), 0),
    }


COURANT = 0.3


def surface_update(surface, eastward, southward, west_ghost, north_ghost):
    east_behind = jnp.concatenate([west_ghost, eastward[..., :-1]], axis=-1)
    south_behind = jnp.concatenate([north_ghost, southward[..., :-1, :]], axis=-2)
    return surface - COURANT * ((eastward - east_behind) + (southward - south_behind))


def flux_update(eastward, southward, new_surface, surface_east, surface_south, depth_east, depth_south, open_east, open_south):
    new_eastward = open_east * (eastward - COURANT * (depth_east + 0.5 * (new_surface + surface_east)) * (surface_east - new_surface))
    new_southward = open_south * (southward - COURANT * (depth_south + 0.5 * (new_surface + surface_south)) * (surface_south - new_surface))
    return new_eastward, new_southward


def restrict(surface, eastward, southward):
    leading = surface.shape[:-2]
    coarse_surface = surface.reshape(leading + (PH, RR, PW, RR)).mean(axis=(-3, -1))
    coarse_east = eastward[..., RR - 1::RR].reshape(leading + (PH, RR, PW)).mean(axis=-2)
    coarse_south = southward[..., RR - 1::RR, :].reshape(leading + (PH, PW, RR)).mean(axis=-1)
    return jnp.stack([coarse_surface, coarse_east, coarse_south], axis=-3)


def to_slots(grid):
    channels = grid.shape[0]
    reshaped = grid.reshape(channels, N_ROW, K, RR * PH, N_NEST, RR * PW).transpose(1, 4, 2, 0, 3, 5)
    return reshaped.reshape(N_ROW * N_NEST * K, channels, RR * PH, RR * PW)


def from_slots(slot_states):
    channels = slot_states.shape[1]
    reshaped = slot_states.reshape(N_ROW, N_NEST, K, channels, RR * PH, RR * PW).transpose(3, 0, 2, 4, 1, 5)
    return reshaped.reshape(channels, N_ROW * K * RR * PH, N_NEST * RR * PW)


def nest_anchors(nest_place):
    positions = K * (RR - 1)
    tile_number = nest_place // positions
    within = nest_place % positions
    band_number = within // (RR - 1)
    column_number = within % (RR - 1)
    first_rows = (tile_number // N_NEST) * (K * RR * PH) + band_number * (RR * PH) + (RR - 1) * PH // 2
    first_cols = (tile_number % N_NEST) * (RR * PW) + PW // 2 + column_number * PW
    return first_rows.astype(jnp.int32), first_cols.astype(jnp.int32)


def gather_strips(outer_grid, first_rows, first_cols):
    def one_nest(row_start, col_start):
        west_flux = lax.dynamic_slice(outer_grid[1], (row_start, col_start - 1), (PH, 1))[:, 0]
        east_level = lax.dynamic_slice(outer_grid[0], (row_start, col_start + PW), (PH, 1))[:, 0]
        north_flux = lax.dynamic_slice(outer_grid[2], (row_start - 1, col_start), (1, PW))[0]
        south_level = lax.dynamic_slice(outer_grid[0], (row_start + PH, col_start), (1, PW))[0]
        return jnp.stack([jnp.concatenate([west_flux, north_flux]), jnp.concatenate([east_level, south_level])])
    return jax.vmap(one_nest)(first_rows, first_cols)


def outer_advance(outer_grid, depth_outer, open_outer):
    grid_rows = outer_grid.shape[1]
    grid_cols = outer_grid.shape[2]
    zero_column = jnp.zeros((grid_rows, 1), jnp.float32)
    zero_row = jnp.zeros((1, grid_cols), jnp.float32)
    new_surface = surface_update(outer_grid[0], outer_grid[1], outer_grid[2], zero_column, zero_row)
    surface_east = jnp.concatenate([new_surface[:, 1:], zero_column], axis=1)
    surface_south = jnp.concatenate([new_surface[1:, :], zero_row], axis=0)
    new_eastward, new_southward = flux_update(outer_grid[1], outer_grid[2], new_surface, surface_east, surface_south, depth_outer[0], depth_outer[1], open_outer[0], open_outer[1])
    return jnp.stack([new_surface, new_eastward, new_southward])


def nest_advance(nest_states, depth_fine, open_fine, old_strips, new_strips):
    surface, eastward, southward = nest_states[:, 0], nest_states[:, 1], nest_states[:, 2]
    for substep in range(1, RR + 1):
        ghost_vals = old_strips + (substep / RR) * (new_strips - old_strips)
        west_ghost = jnp.repeat(ghost_vals[:, 0, :PH], RR, axis=1)[:, :, None]
        north_ghost = jnp.repeat(ghost_vals[:, 0, PH:], RR, axis=1)[:, None, :]
        east_ghost = jnp.repeat(ghost_vals[:, 1, :PH], RR, axis=1)[:, :, None]
        south_ghost = jnp.repeat(ghost_vals[:, 1, PH:], RR, axis=1)[:, None, :]
        new_surface = surface_update(surface, eastward, southward, west_ghost, north_ghost)
        surface_east = jnp.concatenate([new_surface[..., 1:], east_ghost], axis=-1)
        surface_south = jnp.concatenate([new_surface[..., 1:, :], south_ghost], axis=-2)
        eastward, southward = flux_update(eastward, southward, new_surface, surface_east, surface_south, depth_fine[:, 0], depth_fine[:, 1], open_fine[:, 0], open_fine[:, 1])
        surface = new_surface
    return jnp.stack([surface, eastward, southward], axis=1)


def write_back(outer_grid, coarse, first_rows, first_cols):
    def place_one(index, grid):
        return lax.dynamic_update_slice(grid, coarse[index], (jnp.zeros((), jnp.int32), first_rows[index], first_cols[index]))
    return lax.fori_loop(0, coarse.shape[0], place_one, outer_grid)


def reference(ocean_state, face_depth, face_open, nest_place, nest_host):
    outer_grid = ocean_state[0]
    depth_outer = face_depth[0]
    open_outer = face_open[0].astype(jnp.float32)
    slot_states = to_slots(ocean_state[1])
    slot_depth = to_slots(face_depth[1])
    slot_open = to_slots(face_open[1].astype(jnp.float32))
    nest_states = slot_states[nest_host]
    depth_fine = slot_depth[nest_host]
    open_fine = slot_open[nest_host]
    first_rows, first_cols = nest_anchors(nest_place)
    old_strips = gather_strips(outer_grid, first_rows, first_cols)
    for timestep in range(STEPS):
        outer_grid = outer_advance(outer_grid, depth_outer, open_outer)
        new_strips = gather_strips(outer_grid, first_rows, first_cols)
        nest_states = nest_advance(nest_states, depth_fine, open_fine, old_strips, new_strips)
        coarse = restrict(nest_states[:, 0], nest_states[:, 1], nest_states[:, 2])
        outer_grid = write_back(outer_grid, coarse, first_rows, first_cols)
        old_strips = new_strips
    slot_states = slot_states.at[nest_host].set(nest_states)
    return jnp.stack([outer_grid, from_slots(slot_states)])
```

```python
import jax
import jax.numpy as jnp
from jax import lax
from jax.experimental import pallas as pl
from jax.experimental.pallas import tpu as pltpu
from jax.sharding import PartitionSpec as P

PH = 8
PW = 32
RR = 4
K = 2
STEPS = 4
NESTS = 64
COURANT = 0.3

ROWS = 64
COLS = 128
FR = RR * PH
SPOTS = RR - 1
PEERS = 64
HALO = 4
EXT = ROWS + 2 * HALO
TOP = (RR - 1) * PH // 2
LEFT = PW // 2
CHAN = 7
UNIT = 4
UNITS = 8
BLOCK = UNIT * UNITS
HALO_ROW = 6 * UNIT
EDGE_ROW = 7 * UNIT

VMEM = pl.BlockSpec(memory_space=pltpu.VMEM)
SMEM = pl.BlockSpec(memory_space=pltpu.SMEM)


def div6(p):
    return (p * 10923) >> 16


def div3(p):
    return (p * 21846) >> 16


def channel(state_ref, depth_ref, open_ref, k, rows):
    if k < 3:
        return state_ref[0, k, rows, :]
    if k < 5:
        return depth_ref[0, k - 3, rows, :]
    return open_ref[0, k - 5, rows, :].astype(jnp.float32)


def pack_kernel(state_ref, depth_ref, open_ref, out_ref):
    for b in range(K):
        rows = pl.ds(b * FR, FR)
        for k in range(8):
            start = (k // UNIT) * FR * 8 + b * UNIT + k % UNIT
            if k < CHAN:
                value = channel(state_ref, depth_ref, open_ref, k, rows)
            else:
                value = jnp.zeros((FR, COLS), jnp.float32)
            out_ref[pl.ds(start, FR, stride=8), :] = value


def compact_kernel(place_ref, host_ref, own_ref, other_ref, out_ref, table_ref):
    sec = lax.axis_index("sec")
    me = lax.axis_index("row") * lax.axis_size("nest") + lax.axis_index("nest")
    upper = lax.broadcasted_iota(jnp.int32, (8, COLS), 0) >= UNIT

    def copy(source_ref, unit_from, dest, unit_to):
        piece = source_ref[pl.ds(pl.multiple_of((unit_from >> 1) * 8, 8), 8), :]
        swap = (unit_from & 1) != (unit_to & 1)
        piece = jnp.where(swap, pltpu.roll(piece, UNIT, 0), piece)
        spot = pl.ds(pl.multiple_of(dest * BLOCK + (unit_to >> 1) * 8, 8), 8)
        out_ref[spot, :] = jnp.where(upper == ((unit_to & 1) == 1), piece, out_ref[spot, :])

    out_ref[...] = jnp.zeros_like(out_ref)

    @pl.when(sec == 0)
    def _():
        def place_one(n, carry):
            p = place_ref[n]
            t = div6(p)
            copy(other_ref, host_ref[n], t, p - 6 * t)
            return carry

        lax.fori_loop(0, NESTS, place_one, 0, unroll=4)

        tile = lax.broadcasted_iota(jnp.int32, (PEERS, COLS), 0)
        lane = lax.broadcasted_iota(jnp.int32, (PEERS, COLS), 1)
        tile_col = tile & 7
        from_right = (lane < HALO) & (tile_col < 7)
        from_left = (lane >= COLS - HALO) & (tile_col > 0)

        def edges(x):
            right = pltpu.roll(x, PEERS - 1, 0)
            left = pltpu.roll(x, 1, 0)
            return jnp.where(from_right, right, jnp.where(from_left, left, 0.0))

        below = (me & (FR - 1)) < FR // 2
        packed = jnp.zeros((PEERS, COLS), jnp.float32)
        for c in range(UNIT):
            band0 = own_ref[pl.ds(c, PEERS, stride=8), :]
            band1 = own_ref[pl.ds(UNIT + c, PEERS, stride=8), :]
            packed += pltpu.roll(edges(band0), HALO + 8 * c, 1)
            packed += pltpu.roll(edges(band1), HALO + 8 * (UNIT + c), 1)
            down = jnp.where(tile < PEERS - 8, pltpu.roll(band0, PEERS - 8, 0), 0.0)
            up = jnp.where(tile >= 8, pltpu.roll(band1, 8, 0), 0.0)
            vertical = jnp.where(below, down, up)
            packed += pltpu.roll(edges(vertical), HALO + 8 * (2 * UNIT + c), 1)
            out_ref[pl.ds(HALO_ROW + c, PEERS, stride=BLOCK), :] = vertical
        out_ref[pl.ds(EDGE_ROW, PEERS, stride=BLOCK), :] = packed

    @pl.when(sec == 1)
    def _():
        def clear(n, carry):
            base = 3 * div3(place_ref[n])
            for j in range(SPOTS):
                table_ref[base + j] = 0
            return carry

        def note(n, carry):
            table_ref[place_ref[n]] = host_ref[n]
            return carry

        def gather_band(n, carry):
            p = place_ref[n]
            h = host_ref[n]
            dest = h >> 1
            unit = (h & 1) * UNIT
            band = div3(p)
            copy(other_ref, band, dest, unit)
            for j in range(SPOTS):
                copy(own_ref, table_ref[3 * band + j], dest, unit + 1 + j)
            return carry

        lax.fori_loop(0, NESTS, clear, 0, unroll=4)
        lax.fori_loop(0, NESTS, note, 0, unroll=4)
        lax.fori_loop(0, NESTS, gather_band, 0, unroll=2)


def window_kernel(
    place_ref, host_ref, state_ref, depth_ref, open_ref, got_ref, out_ref,
    outer_ref, fine_ref, rep_ref, cov_ref, at_ref,
):
    sec = lax.axis_index("sec")
    row = lax.axis_index("row")
    col = lax.axis_index("nest")
    row_count = lax.axis_size("row")
    col_count = lax.axis_size("nest")
    me = row * col_count + col

    def got(k, unit_row, rows=FR, first=0):
        start = ((k // UNIT) * FR + first) * BLOCK + unit_row + k % UNIT
        return got_ref[pl.ds(start, rows, stride=BLOCK), :]

    for u in range(6):
        cov_ref[u] = 0
    at_ref[0] = -1
    at_ref[1] = -1

    @pl.when(sec == 0)
    def _():
        def scan(n, carry):
            p = place_ref[n]
            t = div6(p)

            @pl.when(t == me)
            def _():
                cov_ref[p - 6 * t] = 1

            return carry

        lax.fori_loop(0, NESTS, scan, 0, unroll=4)
        lane = lax.broadcasted_iota(jnp.int32, (FR, COLS), 1)
        keep = (lane < HALO) | (lane >= COLS - HALO)
        for k in range(CHAN):
            for b in range(K):
                for j in range(SPOTS):
                    fine_ref[3 * b + j, k] = got(k, UNIT * (3 * b + j))
                outer_ref[k, pl.ds(HALO + b * FR, FR), 0:COLS] = channel(
                    state_ref, depth_ref, open_ref, k, pl.ds(b * FR, FR)
                )
            outer_ref[k, 0:HALO, 0:COLS] = got(k, HALO_ROW, HALO, FR - HALO)
            outer_ref[k, EXT - HALO : EXT, 0:COLS] = got(k, HALO_ROW, HALO, 0)
        for g in range(2):
            start = g * FR * BLOCK + EDGE_ROW
            packed = got_ref[pl.ds(start, FR, stride=BLOCK), :]
            for c in range(UNIT):
                k = g * UNIT + c
                if k >= CHAN:
                    continue
                for b in range(K):
                    shift = HALO + 8 * (b * UNIT + c)
                    side = jnp.where(keep, pltpu.roll(packed, COLS - shift, 1), 0.0)
                    outer_ref[k, pl.ds(HALO + b * FR, FR), COLS : 2 * COLS] = side
                shift = HALO + 8 * (2 * UNIT + c)
                side = jnp.where(keep, pltpu.roll(packed, COLS - shift, 1), 0.0)
                outer_ref[k, 0:HALO, COLS : 2 * COLS] = side[FR - HALO :]
                outer_ref[k, EXT - HALO : EXT, COLS : 2 * COLS] = side[:HALO]

    @pl.when(sec == 1)
    def _():
        def find(n, carry):
            h = host_ref[n]

            @pl.when((h >> 1) == me)
            def _():
                at_ref[h & 1] = place_ref[n]

            return carry

        lax.fori_loop(0, NESTS, find, 0, unroll=4)
        bands = [div3(at_ref[s]) for s in range(K)]

        def scan(n, carry):
            p = place_ref[n]
            band = div3(p)
            for s in range(K):

                @pl.when((at_ref[s] >= 0) & (band == bands[s]))
                def _():
                    cov_ref[3 * s + p - 3 * band] = 1

            return carry

        lax.fori_loop(0, NESTS, scan, 0, unroll=4)
        for k in range(CHAN):
            outer_ref[k] = jnp.zeros((EXT, 2 * COLS), jnp.float32)
            for s in range(K):
                outer_ref[k, pl.ds(HALO + s * FR, FR), 0:COLS] = got(k, UNIT * UNIT * s)
                for j in range(SPOTS):
                    fine_ref[3 * s + j, k] = got(k, UNIT * (UNIT * s + 1 + j))

    ext_row = lax.broadcasted_iota(jnp.int32, (EXT, 2 * COLS), 0)
    ext_lane = lax.broadcasted_iota(jnp.int32, (EXT, 2 * COLS), 1)
    row_low = jnp.where((sec == 0) & (row == 0), HALO, 0)
    row_high = jnp.where((sec == 0) & (row == row_count - 1), EXT - HALO, EXT)
    right_end = jnp.where((sec == 0) & (col < col_count - 1), COLS + HALO, COLS)
    left_start = jnp.where((sec == 0) & (col > 0), 2 * COLS - HALO, 2 * COLS)
    inside = (
        (ext_row >= row_low)
        & (ext_row < row_high)
        & ((ext_lane < right_end) | (ext_lane >= left_start))
    )

    small_lane = lax.broadcasted_iota(jnp.int32, (PH, COLS), 1)
    lane = lax.broadcasted_iota(jnp.int32, (FR, COLS), 1)
    fine_row = lax.broadcasted_iota(jnp.int32, (FR, COLS), 0)
    spread = [LEFT + PW * j + (small_lane >> 2) for j in range(SPOTS)]
    gathered = [
        jnp.clip(RR * (small_lane - LEFT - PW * j), 0, COLS - RR) for j in range(SPOTS)
    ]
    mine = [
        (small_lane >= LEFT + PW * j) & (small_lane < LEFT + PW * (j + 1)) for j in range(SPOTS)
    ]

    def take(x, index):
        return jnp.take_along_axis(x, index, axis=1, mode="promise_in_bounds")

    def ghosts(surface, eastward, southward, slot):
        ends = []
        for b in range(K):
            r0 = HALO + TOP + b * FR
            e_rows = eastward[r0 : r0 + PH, :COLS]
            s_rows = surface[r0 : r0 + PH, :COLS]
            north = jnp.broadcast_to(southward[r0 - 1 : r0, :COLS], (PH, COLS))
            south = jnp.broadcast_to(surface[r0 + PH : r0 + PH + 1, :COLS], (PH, COLS))
            for j in range(SPOTS):
                c0 = LEFT + PW * j
                west = pltpu.roll(e_rows, COLS - (c0 - 1), 1)
                east = pltpu.roll(s_rows, COLS - 1 - (c0 + PW), 1)
                side = jnp.where(small_lane == 0, west, east)
                for i in range(RR):
                    rep_ref[slot, 3 * b + j, pl.ds(i, PH, stride=RR), :] = side
                ends.append((take(north, spread[j]), take(south, spread[j])))
        return ends

    def tall(x):
        return jnp.concatenate([x] * RR, axis=0)

    old_ends = ghosts(outer_ref[0], outer_ref[1], outer_ref[2], 0)
    for step in range(STEPS):
        old, new = step % 2, (step + 1) % 2
        surface, eastward, southward = outer_ref[0], outer_ref[1], outer_ref[2]
        flow = (eastward - pltpu.roll(eastward, 1, 1)) + (southward - pltpu.roll(southward, 1, 0))
        surface = jnp.where(inside, surface - COURANT * flow, 0.0)
        to_east = pltpu.roll(surface, 2 * COLS - 1, 1)
        to_south = pltpu.roll(surface, EXT - 1, 0)
        eastward = outer_ref[5] * (
            eastward - COURANT * (outer_ref[3] + 0.5 * (surface + to_east)) * (to_east - surface)
        )
        southward = outer_ref[6] * (
            southward - COURANT * (outer_ref[4] + 0.5 * (surface + to_south)) * (to_south - surface)
        )
        outer_ref[0] = surface
        outer_ref[1] = eastward
        outer_ref[2] = southward
        new_ends = ghosts(surface, eastward, southward, new)
        for nest in range(K * SPOTS):
            b, j = nest // SPOTS, nest % SPOTS
            level, east_flux, south_flux = (fine_ref[nest, k] for k in range(3))
            old_side, new_side = rep_ref[old, nest], rep_ref[new, nest]
            (old_north, old_south), (new_north, new_south) = old_ends[nest], new_ends[nest]
            for m in range(1, RR + 1):
                part = m / RR
                side = old_side + part * (new_side - old_side)
                north = tall(old_north + part * (new_north - old_north))
                south = tall(old_south + part * (new_south - old_south))
                west_of = jnp.where(lane == 0, side, pltpu.roll(east_flux, 1, 1))
                north_of = jnp.where(fine_row == 0, north, pltpu.roll(south_flux, 1, 0))
                level = level - COURANT * ((east_flux - west_of) + (south_flux - north_of))
                east_of = jnp.where(lane == COLS - 1, side, pltpu.roll(level, COLS - 1, 1))
                south_of = jnp.where(fine_row == FR - 1, south, pltpu.roll(level, FR - 1, 0))
                east_flux = fine_ref[nest, 5] * (
                    east_flux
                    - COURANT * (fine_ref[nest, 3] + 0.5 * (level + east_of)) * (east_of - level)
                )
                south_flux = fine_ref[nest, 6] * (
                    south_flux
                    - COURANT * (fine_ref[nest, 4] + 0.5 * (level + south_of)) * (south_of - level)
                )
            for k, value in enumerate((level, east_flux, south_flux)):
                fine_ref[nest, k] = value

            def every(k, i):
                return fine_ref[nest, k, pl.ds(i, PH, stride=RR), :]

            def quads(x):
                x = x + pltpu.roll(x, COLS - 1, 1)
                return x + pltpu.roll(x, COLS - 2, 1)

            mean_level = quads((every(0, 0) + every(0, 1)) + (every(0, 2) + every(0, 3)))
            mean_east = (every(1, 0) + every(1, 1)) + (every(1, 2) + every(1, 3))
            mean_south = quads(every(2, RR - 1))
            back = (
                take(mean_level, gathered[j]) * (1.0 / (RR * RR)),
                take(mean_east, gathered[j] + (RR - 1)) * (1.0 / RR),
                take(mean_south, gathered[j]) * (1.0 / RR),
            )
            here = mine[j] & (cov_ref[nest] == 1)
            rows = pl.ds(HALO + TOP + b * FR, PH)
            for k in range(3):
                outer_ref[k, rows, 0:COLS] = jnp.where(here, back[k], outer_ref[k, rows, 0:COLS])
        old_ends = new_ends

    @pl.when(sec == 0)
    def _():
        for k in range(3):
            out_ref[0, k] = outer_ref[k, HALO : HALO + ROWS, 0:COLS]

    @pl.when(sec == 1)
    def _():
        for s in range(K):
            p = at_ref[s]
            j = jnp.where(p >= 0, p - 3 * div3(p), 0)
            for k in range(3):
                rows = pl.ds(s * FR, FR)
                out_ref[0, k, rows, :] = jnp.where(
                    p >= 0, fine_ref[3 * s + j, k], state_ref[0, k, rows, :]
                )


def on_device(ocean_state, face_depth, face_open, nest_place, nest_host):
    tiles = ("row", "nest")
    packed = pl.pallas_call(
        pack_kernel,
        out_shape=jax.ShapeDtypeStruct((PEERS * 8, COLS), jnp.float32),
        in_specs=[VMEM, VMEM, VMEM],
        out_specs=VMEM,
        name="pack",
    )(ocean_state, face_depth, face_open)
    pieces = lax.all_to_all(
        packed.reshape(PEERS, 8, COLS), tiles, split_axis=0, concat_axis=0, tiled=True
    )
    others = lax.ppermute(pieces, "sec", [(0, 1), (1, 0)])
    blocks = pl.pallas_call(
        compact_kernel,
        out_shape=jax.ShapeDtypeStruct((PEERS * BLOCK, COLS), jnp.float32),
        in_specs=[SMEM, SMEM, VMEM, VMEM],
        out_specs=VMEM,
        scratch_shapes=[pltpu.SMEM((PEERS * K * SPOTS,), jnp.int32)],
        name="compact",
    )(nest_place, nest_host, pieces.reshape(-1, COLS), others.reshape(-1, COLS))
    got = lax.all_to_all(
        blocks.reshape(PEERS, BLOCK, COLS), tiles, split_axis=0, concat_axis=0, tiled=True
    )
    return pl.pallas_call(
        window_kernel,
        out_shape=jax.ShapeDtypeStruct(ocean_state.shape, jnp.float32),
        in_specs=[SMEM, SMEM, VMEM, VMEM, VMEM, VMEM],
        out_specs=VMEM,
        scratch_shapes=[
            pltpu.VMEM((CHAN, EXT, 2 * COLS), jnp.float32),
            pltpu.VMEM((K * SPOTS, CHAN, FR, COLS), jnp.float32),
            pltpu.VMEM((2, K * SPOTS, FR, COLS), jnp.float32),
            pltpu.SMEM((K * SPOTS,), jnp.int32),
            pltpu.SMEM((K,), jnp.int32),
        ],
        compiler_params=pltpu.CompilerParams(vmem_limit_bytes=32 * 1024 * 1024),
        name="window",
    )(nest_place, nest_host, ocean_state, face_depth, face_open, got.reshape(-1, COLS))


def solution(mesh):
    placed = (
        P("sec", None, "row", "nest"),
        P("sec", None, "row", "nest"),
        P("sec", None, "row", "nest"),
        P(),
        P(),
    )
    return jax.shard_map(
        on_device,
        mesh=mesh,
        in_specs=placed,
        out_specs=P("sec", None, "row", "nest"),
        check_vma=False,
    )
```

```python
import jax
import jax.numpy as jnp
from jax import lax
from jax.experimental import pallas as pl
from jax.experimental.pallas import tpu as pltpu
from jax.sharding import PartitionSpec as P

PH = 8
PW = 32
RR = 4
K = 2
STEPS = 4
NESTS = 64
COURANT = 0.3

ROWS = 64
COLS = 128
FR = RR * PH
SPOTS = RR - 1
PEERS = 64
HALO = 4
EXT = ROWS + 2 * HALO
TOP = (RR - 1) * PH // 2
LEFT = PW // 2
CHAN = 7
UNIT = 4
UNITS = 6
BLOCK = UNIT * UNITS
HALF = COLS // 2
LAST = CHAN - 1
PART = LAST // 2

VMEM = pl.BlockSpec(memory_space=pltpu.VMEM)
SMEM = pl.BlockSpec(memory_space=pltpu.SMEM)


def div6(p):
    return (p * 10923) >> 16


def div3(p):
    return (p * 21846) >> 16


def pack_kernel(
    place_in, host_in, state_in, depth_in, open_in,
    out_ref, place_ref, host_ref, state_ref, depth_ref, open_ref, sems,
):
    moves = [
        pltpu.make_async_copy(source, target, sems.at[i])
        for i, (source, target) in enumerate(
            (
                (state_in, state_ref), (depth_in, depth_ref), (open_in, open_ref),
                (place_in, place_ref), (host_in, host_ref),
            )
        )
    ]
    for move in moves:
        move.start()
    for move in moves:
        move.wait()

    def channel(k, rows):
        if k < 3:
            return state_ref[0, k, rows, :]
        if k < 5:
            return depth_ref[0, k - 3, rows, :]
        return open_ref[0, k - 5, rows, :].astype(jnp.float32)

    first = lax.broadcasted_iota(jnp.int32, (8, COLS), 0) < HALO
    rims = [
        jnp.where(first, channel(k, pl.ds(0, 8)), channel(k, pl.ds(ROWS - 8, 8)))
        for k in range(CHAN)
    ]
    rims = jnp.concatenate(rims + [jnp.zeros((8, COLS), jnp.float32)], axis=0)
    left = lax.broadcasted_iota(jnp.int32, (FR, COLS), 1) < HALF
    for b in range(K):
        rows = pl.ds(b * FR, FR)
        for g in range(2):
            base = g * FR * 8 + b * UNIT
            for c in range(PART):
                out_ref[pl.ds(base + c, FR, stride=8), :] = channel(PART * g + c, rows)
            half = channel(LAST, rows)
            rim = rims[g * FR : (g + 1) * FR]
            if g == 1:
                half = pltpu.roll(half, HALF, 1)
            if b == 0:
                rim = pltpu.roll(rim, HALF, 1)
            out_ref[pl.ds(base + PART, FR, stride=8), :] = jnp.where(left, half, rim)


def compact_kernel(place_ref, host_ref, own_ref, other_ref, out_ref, table_ref):
    sec = lax.axis_index("sec")
    me = lax.axis_index("row") * lax.axis_size("nest") + lax.axis_index("nest")
    sub = lax.broadcasted_iota(jnp.int32, (8, COLS), 0)
    sub_lane = lax.broadcasted_iota(jnp.int32, (8, COLS), 1)
    used = (sub_lane < HALF) | ((sub & (UNIT - 1)) < PART)
    halves = (used & (sub < UNIT), used & (sub >= UNIT))

    def copy(source_ref, unit_from, dest, unit_to):
        piece = source_ref[pl.ds(pl.multiple_of((unit_from >> 1) * 8, 8), 8), :]
        swap = (unit_from & 1) != (unit_to & 1)
        piece = jnp.where(swap, pltpu.roll(piece, UNIT, 0), piece)
        spot = pl.ds(pl.multiple_of(dest * BLOCK + (unit_to >> 1) * 8, 8), 8)
        mask = jnp.where((unit_to & 1) == 1, halves[1].astype(jnp.int32), halves[0].astype(jnp.int32))
        pltpu.store(out_ref.at[spot, :], piece, mask=mask == 1)

    out_ref[...] = jnp.zeros_like(out_ref)

    @pl.when(sec == 0)
    def _():
        def place_one(n, carry):
            p = place_ref[n]
            t = div6(p)
            copy(other_ref, host_ref[n], t, p - 6 * t)
            return carry

        lax.fori_loop(0, NESTS, place_one, 0, unroll=8)

        tile = lax.broadcasted_iota(jnp.int32, (PEERS, COLS), 0)
        lane = lax.broadcasted_iota(jnp.int32, (PEERS, COLS), 1)
        tile_col = tile & 7
        has_right, has_left = tile_col < 7, tile_col > 0
        lower_half = me < FR
        to_above = ((me >> 2) & 1) == 0

        def right_of(x):
            return pltpu.roll(x, PEERS - 1, 0)

        def left_of(x):
            return pltpu.roll(x, 1, 0)

        def row_of(i):
            return own_ref[pl.ds(i, PEERS, stride=8), :]

        packed = jnp.zeros((PEERS, COLS), jnp.float32)
        rims = []
        for b in range(K):
            for c in range(PART):
                x = row_of(UNIT * b + c)
                side = jnp.where(
                    has_right & (lane < HALO),
                    right_of(x),
                    jnp.where(has_left & (lane >= COLS - HALO), left_of(x), 0.0),
                )
                packed += pltpu.roll(side, HALF + HALO + 8 * (PART * b + c), 1)
            x = row_of(UNIT * b + PART)
            right = jnp.where(has_right & (lane < HALO), right_of(x), 0.0)
            left = jnp.where(
                has_left & (lane >= HALF - HALO) & (lane < HALF), left_of(x), 0.0
            )
            spot = HALF + 8 * PART * K + HALO * b
            packed += jnp.where(
                lower_half, pltpu.roll(right, spot, 1), pltpu.roll(left, spot - HALF + HALO, 1)
            )
            rims.append(
                jnp.where(
                    to_above,
                    jnp.where(tile < PEERS - 8, pltpu.roll(x, PEERS - 8, 0), 0.0),
                    jnp.where(tile >= 8, pltpu.roll(x, 8, 0), 0.0),
                )
            )
        right = jnp.where(
            has_right & (lane >= HALF) & (lane < HALF + HALO), right_of(rims[0]), 0.0
        )
        left = jnp.where(has_left & (lane >= COLS - HALO), left_of(rims[1]), 0.0)
        packed += pltpu.roll(right, HALF - HALO, 1) + pltpu.roll(left, COLS - HALO, 1)
        for u, value in enumerate([packed] + rims):
            spot = pl.ds(UNIT * u + PART, PEERS, stride=BLOCK)
            out_ref[spot, :] = jnp.where(lane >= HALF, value, out_ref[spot, :])

    @pl.when(sec == 1)
    def _():
        def clear(n, carry):
            base = 3 * div3(place_ref[n])
            for j in range(SPOTS):
                table_ref[base + j] = 0
            return carry

        def note(n, carry):
            table_ref[place_ref[n]] = host_ref[n]
            return carry

        def gather_band(n, carry):
            p = place_ref[n]
            h = host_ref[n]
            dest = h >> 1
            unit = (h & 1) * SPOTS
            band = div3(p)
            j = p - 3 * band
            copy(other_ref, band, dest, unit)
            copy(own_ref, table_ref[3 * band + jnp.where(j == 0, 1, 0)], dest, unit + 1)
            copy(own_ref, table_ref[3 * band + jnp.where(j == 2, 1, 2)], dest, unit + 2)
            return carry

        lax.fori_loop(0, NESTS, clear, 0, unroll=8)
        lax.fori_loop(0, NESTS, note, 0, unroll=8)
        lax.fori_loop(0, NESTS, gather_band, 0, unroll=4)


def window_kernel(
    place_ref, host_ref, state_ref, depth_ref, open_ref, got_ref, out_ref,
    outer_ref, fine_ref, rep_ref, cov_ref, at_ref,
):
    sec = lax.axis_index("sec")
    row = lax.axis_index("row")
    col = lax.axis_index("nest")
    row_count = lax.axis_size("row")
    col_count = lax.axis_size("nest")
    me = row * col_count + col
    lane = lax.broadcasted_iota(jnp.int32, (FR, COLS), 1)
    small_lane = lax.broadcasted_iota(jnp.int32, (PH, COLS), 1)

    def own(k, rows):
        if k < 3:
            return state_ref[0, k, rows, :]
        if k < 5:
            return depth_ref[0, k - 3, rows, :]
        return open_ref[0, k - 5, rows, :].astype(jnp.float32)

    def rows_of(peer, row, count):
        return got_ref[pl.ds(peer * BLOCK + row, count, stride=BLOCK), :]

    def got(k, unit):
        if k < LAST:
            return rows_of((k // PART) * FR, UNIT * unit + k % PART, FR)
        left, right = (rows_of(g * FR, UNIT * unit + PART, FR) for g in range(2))
        return jnp.where(lane < HALF, left, pltpu.roll(right, HALF, 1))

    for u in range(6):
        cov_ref[u] = 0
    at_ref[0] = -1
    at_ref[1] = -1

    @pl.when(sec == 0)
    def _():
        def scan(n, carry):
            p = place_ref[n]
            t = div6(p)

            @pl.when(t == me)
            def _():
                cov_ref[p - 6 * t] = 1

            return carry

        lax.fori_loop(0, NESTS, scan, 0, unroll=4)
        keep = (lane < HALO) | (lane >= COLS - HALO)
        small_keep = (small_lane < HALO) | (small_lane >= COLS - HALO)
        beside = [rows_of(g * FR, PART, FR) for g in range(2)]
        for k in range(CHAN):
            for b in range(K):
                rows = pl.ds(HALO + b * FR, FR)
                for j in range(SPOTS):
                    fine_ref[3 * b + j, k] = got(k, 3 * b + j)
                outer_ref[k, rows, 0:COLS] = own(k, pl.ds(b * FR, FR))
                if k < LAST:
                    shift = HALF + HALO + 8 * (PART * b + k % PART)
                    side = pltpu.roll(beside[k // PART], COLS - shift, 1)
                else:
                    shift = HALF + 8 * PART * K + HALO * b
                    side = jnp.where(
                        lane < HALO,
                        pltpu.roll(beside[0], COLS - shift, 1),
                        pltpu.roll(beside[1], COLS - HALO - shift, 1),
                    )
                outer_ref[k, rows, COLS : 2 * COLS] = jnp.where(keep, side, 0.0)
            rim = jnp.where(
                small_lane < HALF,
                pltpu.roll(rows_of(8 * k, UNIT + PART, 8), HALF, 1),
                rows_of(8 * k, 2 * UNIT + PART, 8),
            )
            corner = jnp.where(small_keep, pltpu.roll(rows_of(8 * k, PART, 8), HALO, 1), 0.0)
            for columns, value in ((pl.ds(0, COLS), rim), (pl.ds(COLS, COLS), corner)):
                outer_ref[k, EXT - HALO : EXT, columns] = value[:HALO]
                outer_ref[k, 0:HALO, columns] = value[HALO:]

    @pl.when(sec == 1)
    def _():
        def find(n, carry):
            h = host_ref[n]

            @pl.when((h >> 1) == me)
            def _():
                at_ref[h & 1] = place_ref[n]

            return carry

        lax.fori_loop(0, NESTS, find, 0, unroll=4)
        bands = [div3(at_ref[s]) for s in range(K)]

        def scan(n, carry):
            p = place_ref[n]
            band = div3(p)
            for s in range(K):

                @pl.when((at_ref[s] >= 0) & (band == bands[s]))
                def _():
                    cov_ref[3 * s + p - 3 * band] = 1

            return carry

        lax.fori_loop(0, NESTS, scan, 0, unroll=4)
        for s in range(K):
            j = jnp.where(at_ref[s] >= 0, at_ref[s] - 3 * bands[s], 0)
            spots = (j, jnp.where(j == 0, 1, 0), jnp.where(j == 2, 1, 2))
            for k in range(CHAN):
                outer_ref[k, pl.ds(HALO + s * FR, FR), 0:COLS] = got(k, SPOTS * s)
                fine_ref[3 * s + spots[0], k] = own(k, pl.ds(s * FR, FR))
                fine_ref[3 * s + spots[1], k] = got(k, SPOTS * s + 1)
                fine_ref[3 * s + spots[2], k] = got(k, SPOTS * s + 2)
        for k in range(CHAN):
            outer_ref[k, 0:HALO, 0:COLS] = jnp.zeros((HALO, COLS), jnp.float32)
            outer_ref[k, EXT - HALO : EXT, 0:COLS] = jnp.zeros((HALO, COLS), jnp.float32)
            outer_ref[k, :, COLS : 2 * COLS] = jnp.zeros((EXT, COLS), jnp.float32)

    ext_row = lax.broadcasted_iota(jnp.int32, (EXT, 2 * COLS), 0)
    ext_lane = lax.broadcasted_iota(jnp.int32, (EXT, 2 * COLS), 1)
    row_low = jnp.where((sec == 0) & (row == 0), HALO, 0)
    row_high = jnp.where((sec == 0) & (row == row_count - 1), EXT - HALO, EXT)
    right_end = jnp.where((sec == 0) & (col < col_count - 1), COLS + HALO, COLS)
    left_start = jnp.where((sec == 0) & (col > 0), 2 * COLS - HALO, 2 * COLS)
    inside = (
        (ext_row >= row_low)
        & (ext_row < row_high)
        & ((ext_lane < right_end) | (ext_lane >= left_start))
    )

    fine_row = lax.broadcasted_iota(jnp.int32, (FR, COLS), 0)
    spread = [LEFT + PW * j + (small_lane >> 2) for j in range(SPOTS)]
    gathered = [
        jnp.clip(RR * (small_lane - LEFT - PW * j), 0, COLS - RR) for j in range(SPOTS)
    ]
    mine = [
        (small_lane >= LEFT + PW * j) & (small_lane < LEFT + PW * (j + 1)) for j in range(SPOTS)
    ]

    def take(x, index):
        return jnp.take_along_axis(x, index, axis=1, mode="promise_in_bounds")

    def ghosts(surface, eastward, southward, slot):
        ends = []
        for b in range(K):
            r0 = HALO + TOP + b * FR
            e_rows = eastward[r0 : r0 + PH, :COLS]
            s_rows = surface[r0 : r0 + PH, :COLS]
            north = jnp.broadcast_to(southward[r0 - 1 : r0, :COLS], (PH, COLS))
            south = jnp.broadcast_to(surface[r0 + PH : r0 + PH + 1, :COLS], (PH, COLS))
            for j in range(SPOTS):
                c0 = LEFT + PW * j
                west = pltpu.roll(e_rows, COLS - (c0 - 1), 1)
                east = pltpu.roll(s_rows, COLS - 1 - (c0 + PW), 1)
                side = jnp.where(small_lane == 0, west, east)
                for i in range(RR):
                    rep_ref[slot, 3 * b + j, pl.ds(i, PH, stride=RR), :] = side
                ends.append((take(north, spread[j]), take(south, spread[j])))
        return ends

    def tall(x):
        return jnp.concatenate([x] * RR, axis=0)

    old_ends = ghosts(outer_ref[0], outer_ref[1], outer_ref[2], 0)
    for step in range(STEPS):
        old, new = step % 2, (step + 1) % 2
        surface, eastward, southward = outer_ref[0], outer_ref[1], outer_ref[2]
        flow = (eastward - pltpu.roll(eastward, 1, 1)) + (southward - pltpu.roll(southward, 1, 0))
        surface = jnp.where(inside, surface - COURANT * flow, 0.0)
        to_east = pltpu.roll(surface, 2 * COLS - 1, 1)
        to_south = pltpu.roll(surface, EXT - 1, 0)
        eastward = outer_ref[5] * (
            eastward - COURANT * (outer_ref[3] + 0.5 * (surface + to_east)) * (to_east - surface)
        )
        southward = outer_ref[6] * (
            southward - COURANT * (outer_ref[4] + 0.5 * (surface + to_south)) * (to_south - surface)
        )
        outer_ref[0] = surface
        outer_ref[1] = eastward
        outer_ref[2] = southward
        new_ends = ghosts(surface, eastward, southward, new)
        for nest in range(K * SPOTS):
            b, j = nest // SPOTS, nest % SPOTS
            level, east_flux, south_flux = (fine_ref[nest, k] for k in range(3))
            old_side, new_side = rep_ref[old, nest], rep_ref[new, nest]
            (old_north, old_south), (new_north, new_south) = old_ends[nest], new_ends[nest]
            for m in range(1, RR + 1):
                part = m / RR
                side = old_side + part * (new_side - old_side)
                north = tall(old_north + part * (new_north - old_north))
                south = tall(old_south + part * (new_south - old_south))
                west_of = jnp.where(lane == 0, side, pltpu.roll(east_flux, 1, 1))
                north_of = jnp.where(fine_row == 0, north, pltpu.roll(south_flux, 1, 0))
                level = level - COURANT * ((east_flux - west_of) + (south_flux - north_of))
                east_of = jnp.where(lane == COLS - 1, side, pltpu.roll(level, COLS - 1, 1))
                south_of = jnp.where(fine_row == FR - 1, south, pltpu.roll(level, FR - 1, 0))
                east_flux = fine_ref[nest, 5] * (
                    east_flux
                    - COURANT * (fine_ref[nest, 3] + 0.5 * (level + east_of)) * (east_of - level)
                )
                south_flux = fine_ref[nest, 6] * (
                    south_flux
                    - COURANT * (fine_ref[nest, 4] + 0.5 * (level + south_of)) * (south_of - level)
                )
            for k, value in enumerate((level, east_flux, south_flux)):
                fine_ref[nest, k] = value

            def every(k, i):
                return fine_ref[nest, k, pl.ds(i, PH, stride=RR), :]

            def quads(x):
                x = x + pltpu.roll(x, COLS - 1, 1)
                return x + pltpu.roll(x, COLS - 2, 1)

            mean_level = quads((every(0, 0) + every(0, 1)) + (every(0, 2) + every(0, 3)))
            mean_east = (every(1, 0) + every(1, 1)) + (every(1, 2) + every(1, 3))
            mean_south = quads(every(2, RR - 1))
            back = (
                take(mean_level, gathered[j]) * (1.0 / (RR * RR)),
                take(mean_east, gathered[j] + (RR - 1)) * (1.0 / RR),
                take(mean_south, gathered[j]) * (1.0 / RR),
            )
            here = mine[j] & (cov_ref[nest] == 1)
            rows = pl.ds(HALO + TOP + b * FR, PH)
            for k in range(3):
                outer_ref[k, rows, 0:COLS] = jnp.where(here, back[k], outer_ref[k, rows, 0:COLS])
        old_ends = new_ends

    @pl.when(sec == 0)
    def _():
        for k in range(3):
            out_ref[0, k] = outer_ref[k, HALO : HALO + ROWS, 0:COLS]

    @pl.when(sec == 1)
    def _():
        for s in range(K):
            p = at_ref[s]
            j = jnp.where(p >= 0, p - 3 * div3(p), 0)
            for k in range(3):
                rows = pl.ds(s * FR, FR)
                out_ref[0, k, rows, :] = jnp.where(
                    p >= 0, fine_ref[3 * s + j, k], state_ref[0, k, rows, :]
                )


def on_device(ocean_state, face_depth, face_open, nest_place, nest_host):
    tiles = ("row", "nest")
    packed, place, host = pl.pallas_call(
        pack_kernel,
        out_shape=(
            jax.ShapeDtypeStruct((PEERS * 8, COLS), jnp.float32),
            jax.ShapeDtypeStruct(nest_place.shape, jnp.int32),
            jax.ShapeDtypeStruct(nest_host.shape, jnp.int32),
        ),
        in_specs=[pl.BlockSpec(memory_space=pltpu.HBM)] * 5,
        out_specs=(VMEM, VMEM, VMEM),
        scratch_shapes=[
            pltpu.VMEM(ocean_state.shape, jnp.float32),
            pltpu.VMEM(face_depth.shape, jnp.float32),
            pltpu.VMEM(face_open.shape, jnp.int32),
            pltpu.SemaphoreType.DMA((5,)),
        ],
        compiler_params=pltpu.CompilerParams(vmem_limit_bytes=4 * 1024 * 1024),
        name="pack",
    )(*(
        pltpu.with_memory_space_constraint(x, pltpu.HBM)
        for x in (nest_place, nest_host, ocean_state, face_depth, face_open)
    ))
    pieces = lax.all_to_all(
        packed.reshape(PEERS, 8, COLS), tiles, split_axis=0, concat_axis=0, tiled=True
    )
    others = lax.ppermute(pieces, "sec", [(0, 1), (1, 0)])
    blocks = pl.pallas_call(
        compact_kernel,
        out_shape=jax.ShapeDtypeStruct((PEERS * BLOCK, COLS), jnp.float32),
        in_specs=[SMEM, SMEM, VMEM, VMEM],
        out_specs=VMEM,
        scratch_shapes=[pltpu.SMEM((PEERS * K * SPOTS,), jnp.int32)],
        compiler_params=pltpu.CompilerParams(vmem_limit_bytes=8 * 1024 * 1024),
        name="compact",
    )(place, host, pieces.reshape(-1, COLS), others.reshape(-1, COLS))
    got = lax.all_to_all(
        blocks.reshape(PEERS, BLOCK, COLS), tiles, split_axis=0, concat_axis=0, tiled=True
    )
    return pl.pallas_call(
        window_kernel,
        out_shape=jax.ShapeDtypeStruct(ocean_state.shape, jnp.float32),
        in_specs=[SMEM, SMEM, VMEM, VMEM, VMEM, VMEM],
        out_specs=VMEM,
        scratch_shapes=[
            pltpu.VMEM((CHAN, EXT, 2 * COLS), jnp.float32),
            pltpu.VMEM((K * SPOTS, CHAN, FR, COLS), jnp.float32),
            pltpu.VMEM((2, K * SPOTS, FR, COLS), jnp.float32),
            pltpu.SMEM((K * SPOTS,), jnp.int32),
            pltpu.SMEM((K,), jnp.int32),
        ],
        compiler_params=pltpu.CompilerParams(vmem_limit_bytes=32 * 1024 * 1024),
        name="window",
    )(place, host, ocean_state, face_depth, face_open, got.reshape(-1, COLS))


def solution(mesh):
    placed = (
        P("sec", None, "row", "nest"),
        P("sec", None, "row", "nest"),
        P("sec", None, "row", "nest"),
        P(),
        P(),
    )
    return jax.shard_map(
        on_device,
        mesh=mesh,
        in_specs=placed,
        out_specs=P("sec", None, "row", "nest"),
        check_vma=False,
    )
```

```python
import functools

import jax
import jax.numpy as jnp
from jax import lax
from jax.experimental import pallas as pl
from jax.experimental.pallas import tpu as pltpu
from jax.sharding import PartitionSpec as P

PH = 8
PW = 32
RR = 4
K = 2
STEPS = 4
NESTS = 64
COURANT = 0.3

ROWS = 64
COLS = 128
FR = RR * PH
SPOTS = RR - 1
PEERS = 64
HALO = 4
EXT = ROWS + 2 * HALO
TOP = (RR - 1) * PH // 2
LEFT = PW // 2
CHAN = 7
UNIT = 4
TILE_BLOCK = UNIT * K * SPOTS
SLOT_BLOCK = UNIT * K * 2
HALF = COLS // 2
LAST = CHAN - 1
PART = LAST // 2

VMEM = pl.BlockSpec(memory_space=pltpu.VMEM)
SMEM = pl.BlockSpec(memory_space=pltpu.SMEM)


def div6(p):
    return (p * 10923) >> 16


def div3(p):
    return (p * 21846) >> 16


def pack_kernel(
    place_in, host_in, state_in, depth_in, open_in,
    out_ref, place_ref, host_ref, state_ref, depth_ref, open_ref, sems,
):
    moves = [
        pltpu.make_async_copy(source, target, sems.at[i])
        for i, (source, target) in enumerate(
            (
                (state_in, state_ref), (depth_in, depth_ref), (open_in, open_ref),
                (place_in, place_ref), (host_in, host_ref),
            )
        )
    ]
    for move in moves:
        move.start()
    for move in moves:
        move.wait()

    def channel(k, rows):
        if k < 3:
            return state_ref[0, k, rows, :]
        if k < 5:
            return depth_ref[0, k - 3, rows, :]
        return open_ref[0, k - 5, rows, :].astype(jnp.float32)

    first = lax.broadcasted_iota(jnp.int32, (8, COLS), 0) < HALO
    rims = [
        jnp.where(first, channel(k, pl.ds(0, 8)), channel(k, pl.ds(ROWS - 8, 8)))
        for k in range(CHAN)
    ]
    rims = jnp.concatenate(rims + [jnp.zeros((8, COLS), jnp.float32)], axis=0)
    left = lax.broadcasted_iota(jnp.int32, (FR, COLS), 1) < HALF
    for b in range(K):
        rows = pl.ds(b * FR, FR)
        for g in range(2):
            base = g * FR * 8 + b * UNIT
            for c in range(PART):
                out_ref[pl.ds(base + c, FR, stride=8), :] = channel(PART * g + c, rows)
            half = channel(LAST, rows)
            rim = rims[g * FR : (g + 1) * FR]
            if g == 1:
                half = pltpu.roll(half, HALF, 1)
            if b == 0:
                rim = pltpu.roll(rim, HALF, 1)
            out_ref[pl.ds(base + PART, FR, stride=8), :] = jnp.where(left, half, rim)


def clear_table(table_ref, first, count):
    for i in range(count):
        table_ref[first + i] = -1


def compact_tiles_kernel(place_ref, host_ref, own_ref, other_ref, out_ref):
    me = lax.axis_index("row") * lax.axis_size("nest") + lax.axis_index("nest")
    sub = lax.broadcasted_iota(jnp.int32, (8, COLS), 0)
    sub_lane = lax.broadcasted_iota(jnp.int32, (8, COLS), 1)
    used = (sub_lane < HALF) | ((sub & (UNIT - 1)) < PART)
    half_of = jnp.where(used, jnp.where(sub < UNIT, 0, 1), 2)

    out_ref[...] = jnp.zeros_like(out_ref)

    def place_one(n, carry):
        p = place_ref[n]
        h = host_ref[n]
        t = div6(p)
        u = p - 6 * t
        piece = other_ref[pl.ds(pl.multiple_of((h >> 1) * 8, 8), 8), :]
        piece = jnp.where((h & 1) != (u & 1), pltpu.roll(piece, UNIT, 0), piece)
        spot = pl.ds(pl.multiple_of(t * TILE_BLOCK + (u >> 1) * 8, 8), 8)
        pltpu.store(out_ref.at[spot, :], piece, mask=half_of == (u & 1))
        return carry

    lax.fori_loop(0, NESTS, place_one, 0, unroll=8)

    tile = lax.broadcasted_iota(jnp.int32, (PEERS, COLS), 0)
    lane = lax.broadcasted_iota(jnp.int32, (PEERS, COLS), 1)
    tile_col = tile & 7
    has_right, has_left = tile_col < 7, tile_col > 0
    lower_half = me < FR
    to_above = ((me >> 2) & 1) == 0

    def right_of(x):
        return pltpu.roll(x, PEERS - 1, 0)

    def left_of(x):
        return pltpu.roll(x, 1, 0)

    def row_of(i):
        return own_ref[pl.ds(i, PEERS, stride=8), :]

    packed = jnp.zeros((PEERS, COLS), jnp.float32)
    rims = []
    for b in range(K):
        for c in range(PART):
            x = row_of(UNIT * b + c)
            side = jnp.where(
                has_right & (lane < HALO),
                right_of(x),
                jnp.where(has_left & (lane >= COLS - HALO), left_of(x), 0.0),
            )
            packed += pltpu.roll(side, HALF + HALO + 8 * (PART * b + c), 1)
        x = row_of(UNIT * b + PART)
        right = jnp.where(has_right & (lane < HALO), right_of(x), 0.0)
        left = jnp.where(has_left & (lane >= HALF - HALO) & (lane < HALF), left_of(x), 0.0)
        spot = HALF + 8 * PART * K + HALO * b
        packed += jnp.where(
            lower_half, pltpu.roll(right, spot, 1), pltpu.roll(left, spot - HALF + HALO, 1)
        )
        rims.append(
            jnp.where(
                to_above,
                jnp.where(tile < PEERS - 8, pltpu.roll(x, PEERS - 8, 0), 0.0),
                jnp.where(tile >= 8, pltpu.roll(x, 8, 0), 0.0),
            )
        )
    right = jnp.where(has_right & (lane >= HALF) & (lane < HALF + HALO), right_of(rims[0]), 0.0)
    left = jnp.where(has_left & (lane >= COLS - HALO), left_of(rims[1]), 0.0)
    packed += pltpu.roll(right, HALF - HALO, 1) + pltpu.roll(left, COLS - HALO, 1)
    for u, value in enumerate([packed] + rims):
        spot = pl.ds(UNIT * u + PART, PEERS, stride=TILE_BLOCK)
        out_ref[spot, :] = jnp.where(lane >= HALF, value, out_ref[spot, :])


def compact_slots_kernel(place_ref, host_ref, own_ref, other_ref, out_ref, table_ref):
    me = lax.axis_index("row") * lax.axis_size("nest") + lax.axis_index("nest")
    sub = lax.broadcasted_iota(jnp.int32, (UNIT, COLS), 0)
    lane = lax.broadcasted_iota(jnp.int32, (UNIT, COLS), 1)
    from_east = jnp.where(sub < PART, (lane < HALF).astype(jnp.int32), (me < FR).astype(jnp.int32))

    def unit(source_ref, i):
        piece = source_ref[pl.ds(pl.multiple_of((i >> 1) * 8, 8), 8), :]
        return jnp.where((i & 1) == 1, piece[UNIT:], piece[:UNIT])

    def clear(n, carry):
        clear_table(table_ref, 3 * div3(place_ref[n]), SPOTS)
        return carry

    def note(n, carry):
        table_ref[place_ref[n]] = host_ref[n]
        return carry

    def gather_band(n, carry):
        p = place_ref[n]
        h = host_ref[n]
        band = div3(p)
        j = p - 3 * band
        west = table_ref[3 * band + jnp.where(j == 0, 0, j - 1)]
        east = table_ref[3 * band + jnp.where(j == SPOTS - 1, SPOTS - 1, j + 1)]
        west = jnp.where(west < 0, 0, west)
        east = jnp.where(east < 0, 0, east)
        beside = jnp.where(from_east == 1, unit(own_ref, east), unit(own_ref, west))
        block = jnp.concatenate([unit(other_ref, band), beside], axis=0)
        out_ref[pl.ds(pl.multiple_of(h * 8, 8), 8), :] = block
        return carry

    out_ref[...] = jnp.zeros_like(out_ref)
    lax.fori_loop(0, NESTS, clear, 0, unroll=8)
    lax.fori_loop(0, NESTS, note, 0, unroll=8)
    lax.fori_loop(0, NESTS, gather_band, 0, unroll=4)


def window_kernel(
    tile_side, place_ref, host_ref, state_ref, depth_ref, open_ref, got_ref, out_ref,
    outer_ref, fine_ref, rep_ref, table_ref,
):
    row = lax.axis_index("row")
    col = lax.axis_index("nest")
    row_count = lax.axis_size("row")
    col_count = lax.axis_size("nest")
    me = row * col_count + col
    block = TILE_BLOCK if tile_side else SLOT_BLOCK
    lane = lax.broadcasted_iota(jnp.int32, (FR, COLS), 1)
    fine_row = lax.broadcasted_iota(jnp.int32, (FR, COLS), 0)
    small_lane = lax.broadcasted_iota(jnp.int32, (PH, COLS), 1)

    def own(k, rows):
        if k < 3:
            return state_ref[0, k, rows, :]
        if k < 5:
            return depth_ref[0, k - 3, rows, :]
        return open_ref[0, k - 5, rows, :].astype(jnp.float32)

    def rows_of(peer, row, count):
        return got_ref[pl.ds(peer * block + row, count, stride=block), :]

    def got(k, unit):
        if k < LAST:
            return rows_of((k // PART) * FR, UNIT * unit + k % PART, FR)
        left, right = (rows_of(g * FR, UNIT * unit + PART, FR) for g in range(2))
        return jnp.where(lane < HALF, left, pltpu.roll(right, HALF, 1))

    def set_fine(nest, values):
        level, east_flux, south_flux, depth_east, depth_south, open_east, open_south = values
        fine_ref[nest, 0] = level
        fine_ref[nest, 1] = COURANT * east_flux
        fine_ref[nest, 2] = COURANT * south_flux
        fine_ref[nest, 3] = (COURANT * COURANT) * open_east * depth_east
        fine_ref[nest, 4] = (COURANT * COURANT) * open_south * depth_south
        fine_ref[nest, 5] = open_east
        fine_ref[nest, 6] = open_south

    def note_place(n, carry):
        table_ref[place_ref[n]] = 1
        return carry

    def note_host(n, carry):
        table_ref[host_ref[n]] = place_ref[n]
        return carry

    if tile_side:
        clear_table(table_ref, 6 * me, K * SPOTS)
        lax.fori_loop(0, NESTS, note_place, 0, unroll=16)
        covered = [table_ref[6 * me + u] == 1 for u in range(K * SPOTS)]
        keep = (lane < HALO) | (lane >= COLS - HALO)
        small_keep = (small_lane < HALO) | (small_lane >= COLS - HALO)
        beside = [rows_of(g * FR, PART, FR) for g in range(2)]
        for k in range(CHAN):
            for b in range(K):
                rows = pl.ds(HALO + b * FR, FR)
                outer_ref[k, rows, 0:COLS] = own(k, pl.ds(b * FR, FR))
                if k < LAST:
                    shift = HALF + HALO + 8 * (PART * b + k % PART)
                    side = pltpu.roll(beside[k // PART], COLS - shift, 1)
                else:
                    shift = HALF + 8 * PART * K + HALO * b
                    side = jnp.where(
                        lane < HALO,
                        pltpu.roll(beside[0], COLS - shift, 1),
                        pltpu.roll(beside[1], COLS - HALO - shift, 1),
                    )
                outer_ref[k, rows, COLS : 2 * COLS] = jnp.where(keep, side, 0.0)
            rim = jnp.where(
                small_lane < HALF,
                pltpu.roll(rows_of(8 * k, UNIT + PART, 8), HALF, 1),
                rows_of(8 * k, 2 * UNIT + PART, 8),
            )
            corner = jnp.where(small_keep, pltpu.roll(rows_of(8 * k, PART, 8), HALO, 1), 0.0)
            for columns, value in ((pl.ds(0, COLS), rim), (pl.ds(COLS, COLS), corner)):
                outer_ref[k, EXT - HALO : EXT, columns] = value[:HALO]
                outer_ref[k, 0:HALO, columns] = value[HALO:]
        for u in range(K * SPOTS):
            set_fine(u, [got(k, u) for k in range(CHAN)])
    else:
        clear_table(table_ref, K * me, K)
        lax.fori_loop(0, NESTS, note_host, 0, unroll=16)
        at = [table_ref[K * me + s] for s in range(K)]
        live = [p >= 0 for p in at]
        bands = [3 * div3(jnp.where(live[s], at[s], 0)) for s in range(K)]
        spots = [jnp.where(live[s], at[s] - bands[s], 0) for s in range(K)]
        for s in range(K):
            clear_table(table_ref, bands[s], SPOTS)
        lax.fori_loop(0, NESTS, note_place, 0, unroll=16)
        covered = [table_ref[bands[s] + j] == 1 for s in range(K) for j in range(SPOTS)]
        for s in range(K):
            beside = [got(k, 2 * s + 1) for k in range(CHAN)]
            for j in range(SPOTS):
                set_fine(SPOTS * s + j, beside)
            set_fine(SPOTS * s + spots[s], [own(k, pl.ds(s * FR, FR)) for k in range(CHAN)])
            for k in range(CHAN):
                outer_ref[k, pl.ds(HALO + s * FR, FR), 0:COLS] = got(k, 2 * s)
        for k in range(CHAN):
            outer_ref[k, 0:HALO, 0:COLS] = jnp.zeros((HALO, COLS), jnp.float32)
            outer_ref[k, EXT - HALO : EXT, 0:COLS] = jnp.zeros((HALO, COLS), jnp.float32)
            outer_ref[k, :, COLS : 2 * COLS] = jnp.zeros((EXT, COLS), jnp.float32)

    for flux in (1, 2):
        outer_ref[flux] = COURANT * outer_ref[flux]
        outer_ref[flux + 2] = (COURANT * COURANT) * outer_ref[flux + 4] * outer_ref[flux + 2]

    inside = None
    if tile_side:
        ext_row = lax.broadcasted_iota(jnp.int32, (EXT, 2 * COLS), 0)
        ext_lane = lax.broadcasted_iota(jnp.int32, (EXT, 2 * COLS), 1)
        row_low = jnp.where(row == 0, HALO, 0)
        row_high = jnp.where(row == row_count - 1, EXT - HALO, EXT)
        right_end = jnp.where(col < col_count - 1, COLS + HALO, COLS)
        left_start = jnp.where(col > 0, 2 * COLS - HALO, 2 * COLS)
        inside = (
            (ext_row >= row_low)
            & (ext_row < row_high)
            & ((ext_lane < right_end) | (ext_lane >= left_start))
        )

    spread = [LEFT + PW * j + (small_lane >> 2) for j in range(SPOTS)]
    gathered = [
        jnp.clip(RR * (small_lane - LEFT - PW * j), 0, COLS - RR) for j in range(SPOTS)
    ]
    mine = [
        (small_lane >= LEFT + PW * j) & (small_lane < LEFT + PW * (j + 1)) for j in range(SPOTS)
    ]
    half_square = 0.5 * COURANT * COURANT

    def take(x, index):
        return jnp.take_along_axis(x, index, axis=1, mode="promise_in_bounds")

    def ghosts(surface, eastward, southward, slot):
        ends = []
        for b in range(K):
            r0 = HALO + TOP + b * FR
            e_rows = eastward[r0 : r0 + PH, :COLS]
            s_rows = surface[r0 : r0 + PH, :COLS]
            north = jnp.broadcast_to(southward[r0 - 1 : r0, :COLS], (PH, COLS))
            south = jnp.broadcast_to(surface[r0 + PH : r0 + PH + 1, :COLS], (PH, COLS))
            for j in range(SPOTS):
                c0 = LEFT + PW * j
                west = pltpu.roll(e_rows, COLS - (c0 - 1), 1)
                east = pltpu.roll(s_rows, COLS - 1 - (c0 + PW), 1)
                side = jnp.where(small_lane == 0, west, east)
                for i in range(RR):
                    rep_ref[slot, 3 * b + j, pl.ds(i, PH, stride=RR), :] = side
                ends.append((take(north, spread[j]), take(south, spread[j])))
        return ends

    def tall(x):
        return jnp.concatenate([x] * RR, axis=0)

    old_ends = ghosts(outer_ref[0], outer_ref[1], outer_ref[2], 0)
    for step in range(STEPS):
        old, new = step % 2, (step + 1) % 2
        surface, eastward, southward = outer_ref[0], outer_ref[1], outer_ref[2]
        flow = (eastward - pltpu.roll(eastward, 1, 1)) + (southward - pltpu.roll(southward, 1, 0))
        surface = surface - flow
        if inside is not None:
            surface = jnp.where(inside, surface, 0.0)
        to_east = pltpu.roll(surface, 2 * COLS - 1, 1)
        to_south = pltpu.roll(surface, EXT - 1, 0)
        eastward = outer_ref[5] * (
            eastward - half_square * (surface + to_east) * (to_east - surface)
        ) - outer_ref[3] * (to_east - surface)
        southward = outer_ref[6] * (
            southward - half_square * (surface + to_south) * (to_south - surface)
        ) - outer_ref[4] * (to_south - surface)
        outer_ref[0] = surface
        outer_ref[1] = eastward
        outer_ref[2] = southward
        new_ends = ghosts(surface, eastward, southward, new)
        for nest in range(K * SPOTS):
            b, j = nest // SPOTS, nest % SPOTS
            level, east_flux, south_flux = (fine_ref[nest, k] for k in range(3))
            old_side, new_side = rep_ref[old, nest], rep_ref[new, nest]
            (old_north, old_south), (new_north, new_south) = old_ends[nest], new_ends[nest]
            for m in range(1, RR + 1):
                part = m / RR
                side = old_side + part * (new_side - old_side)
                north = tall(old_north + part * (new_north - old_north))
                south = tall(old_south + part * (new_south - old_south))
                west_of = jnp.where(lane == 0, side, pltpu.roll(east_flux, 1, 1))
                north_of = jnp.where(fine_row == 0, north, pltpu.roll(south_flux, 1, 0))
                level = level - ((east_flux - west_of) + (south_flux - north_of))
                east_of = jnp.where(lane == COLS - 1, side, pltpu.roll(level, COLS - 1, 1))
                south_of = jnp.where(fine_row == FR - 1, south, pltpu.roll(level, FR - 1, 0))
                open_east, open_south = fine_ref[nest, 5], fine_ref[nest, 6]
                if step == 0 and m == 1:
                    east_flux = open_east * east_flux
                    south_flux = open_south * south_flux
                east_flux = east_flux - (
                    fine_ref[nest, 3] + (half_square * open_east) * (level + east_of)
                ) * (east_of - level)
                south_flux = south_flux - (
                    fine_ref[nest, 4] + (half_square * open_south) * (level + south_of)
                ) * (south_of - level)
            for k, value in enumerate((level, east_flux, south_flux)):
                fine_ref[nest, k] = value

            def every(k, i):
                return fine_ref[nest, k, pl.ds(i, PH, stride=RR), :]

            def quads(x):
                x = x + pltpu.roll(x, COLS - 1, 1)
                return x + pltpu.roll(x, COLS - 2, 1)

            mean_level = quads((every(0, 0) + every(0, 1)) + (every(0, 2) + every(0, 3)))
            mean_east = (every(1, 0) + every(1, 1)) + (every(1, 2) + every(1, 3))
            mean_south = quads(every(2, RR - 1))
            back = (
                take(mean_level, gathered[j]) * (1.0 / (RR * RR)),
                take(mean_east, gathered[j] + (RR - 1)) * (1.0 / RR),
                take(mean_south, gathered[j]) * (1.0 / RR),
            )
            here = mine[j] & covered[nest]
            rows = pl.ds(HALO + TOP + b * FR, PH)
            for k in range(3):
                outer_ref[k, rows, 0:COLS] = jnp.where(here, back[k], outer_ref[k, rows, 0:COLS])
        old_ends = new_ends

    for k in range(3):
        scale = 1.0 if k == 0 else 1.0 / COURANT
        if tile_side:
            out_ref[0, k] = outer_ref[k, HALO : HALO + ROWS, 0:COLS] * scale
        else:
            for s in range(K):
                rows = pl.ds(s * FR, FR)
                out_ref[0, k, rows, :] = jnp.where(
                    live[s], fine_ref[SPOTS * s + spots[s], k] * scale, state_ref[0, k, rows, :]
                )


def window(tile_side, place, host, pieces, others, state, depth, opening):
    block = TILE_BLOCK if tile_side else SLOT_BLOCK
    table = pltpu.SMEM((PEERS * K * SPOTS,), jnp.int32)
    blocks = pl.pallas_call(
        compact_tiles_kernel if tile_side else compact_slots_kernel,
        out_shape=jax.ShapeDtypeStruct((PEERS * block, COLS), jnp.float32),
        in_specs=[SMEM, SMEM, VMEM, VMEM],
        out_specs=VMEM,
        scratch_shapes=[] if tile_side else [table],
        compiler_params=pltpu.CompilerParams(vmem_limit_bytes=8 * 1024 * 1024),
        name="compact_tiles" if tile_side else "compact_slots",
    )(place, host, pieces.reshape(-1, COLS), others.reshape(-1, COLS))
    got = lax.all_to_all(
        blocks.reshape(PEERS, block, COLS),
        ("row", "nest"),
        split_axis=0,
        concat_axis=0,
        tiled=True,
    )
    return pl.pallas_call(
        functools.partial(window_kernel, tile_side),
        out_shape=jax.ShapeDtypeStruct(state.shape, jnp.float32),
        in_specs=[SMEM, SMEM, VMEM, VMEM, VMEM, VMEM],
        out_specs=VMEM,
        scratch_shapes=[
            pltpu.VMEM((CHAN, EXT, 2 * COLS), jnp.float32),
            pltpu.VMEM((K * SPOTS, CHAN, FR, COLS), jnp.float32),
            pltpu.VMEM((2, K * SPOTS, FR, COLS), jnp.float32),
            table,
        ],
        compiler_params=pltpu.CompilerParams(vmem_limit_bytes=32 * 1024 * 1024),
        name="window_tiles" if tile_side else "window_slots",
    )(place, host, state, depth, opening, got.reshape(-1, COLS))


def on_device(ocean_state, face_depth, face_open, nest_place, nest_host):
    tiles = ("row", "nest")
    packed, place, host = pl.pallas_call(
        pack_kernel,
        out_shape=(
            jax.ShapeDtypeStruct((PEERS * 8, COLS), jnp.float32),
            jax.ShapeDtypeStruct(nest_place.shape, jnp.int32),
            jax.ShapeDtypeStruct(nest_host.shape, jnp.int32),
        ),
        in_specs=[pl.BlockSpec(memory_space=pltpu.HBM)] * 5,
        out_specs=(VMEM, VMEM, VMEM),
        scratch_shapes=[
            pltpu.VMEM(ocean_state.shape, jnp.float32),
            pltpu.VMEM(face_depth.shape, jnp.float32),
            pltpu.VMEM(face_open.shape, jnp.int32),
            pltpu.SemaphoreType.DMA((5,)),
        ],
        compiler_params=pltpu.CompilerParams(vmem_limit_bytes=4 * 1024 * 1024),
        name="pack",
    )(*(
        pltpu.with_memory_space_constraint(x, pltpu.HBM)
        for x in (nest_place, nest_host, ocean_state, face_depth, face_open)
    ))
    pieces = lax.all_to_all(
        packed.reshape(PEERS, 8, COLS), tiles, split_axis=0, concat_axis=0, tiled=True
    )
    others = lax.ppermute(pieces, "sec", [(0, 1), (1, 0)])
    return lax.cond(
        lax.axis_index("sec") == 0,
        functools.partial(window, True),
        functools.partial(window, False),
        place, host, pieces, others, ocean_state, face_depth, face_open,
    )


def solution(mesh):
    placed = (
        P("sec", None, "row", "nest"),
        P("sec", None, "row", "nest"),
        P("sec", None, "row", "nest"),
        P(),
        P(),
    )
    return jax.shard_map(
        on_device,
        mesh=mesh,
        in_specs=placed,
        out_specs=P("sec", None, "row", "nest"),
        check_vma=False,
    )
```

```python
import functools
from typing import NamedTuple

import jax
import jax.numpy as jnp
from jax import lax
from jax.experimental import pallas as pl
from jax.experimental.pallas import tpu as pltpu
from jax.sharding import PartitionSpec as P

PH = 8
PW = 32
RR = 4
K = 2
STEPS = 4
NESTS = 64
COURANT = 0.3

ROWS = 64
COLS = 128
FR = RR * PH
SPOTS = RR - 1
PEERS = 64
HALO = 4
EXT = ROWS + 2 * HALO
TOP = (RR - 1) * PH // 2
LEFT = PW // 2
CHAN = 7
UNIT = 4
FEW = 4
MANY = K * SPOTS
SLOT_UNITS = K
HALF = COLS // 2
LAST = CHAN - 1
PART = LAST // 2
HALF_SQUARE = 0.5 * COURANT * COURANT

VMEM = pl.BlockSpec(memory_space=pltpu.VMEM)
SMEM = pl.BlockSpec(memory_space=pltpu.SMEM)


def div6(p):
    return (p * 10923) >> 16


def div3(p):
    return (p * 21846) >> 16


def pack_kernel(
    place_in, host_in, state_in, depth_in, open_in,
    out_ref, place_ref, host_ref, crowded_out,
    state_ref, depth_ref, open_ref, crowded_ref, sems,
):
    moves = [
        pltpu.make_async_copy(source, target, sems.at[i])
        for i, (source, target) in enumerate(
            (
                (place_in, place_ref), (host_in, host_ref),
                (state_in, state_ref), (depth_in, depth_ref), (open_in, open_ref),
            )
        )
    ]
    for move in moves:
        move.start()
    for move in moves[:2]:
        move.wait()
    tile = lax.broadcasted_iota(jnp.int32, (PEERS, NESTS), 0)
    hits = jnp.where(div6(place_ref[...]) == tile, 1.0, 0.0)
    most = jnp.max(jnp.sum(hits, axis=1, keepdims=True), axis=0, keepdims=True)
    crowded_ref[...] = jnp.where(most > FEW, 1, 0)
    report = pltpu.make_async_copy(crowded_ref, crowded_out, sems.at[len(moves)])
    report.start()
    for move in moves[2:]:
        move.wait()

    def channel(k, rows):
        if k < 3:
            return state_ref[0, k, rows, :]
        if k < 5:
            return depth_ref[0, k - 3, rows, :]
        return open_ref[0, k - 5, rows, :].astype(jnp.float32)

    first = lax.broadcasted_iota(jnp.int32, (8, COLS), 0) < HALO
    rims = [
        jnp.where(first, channel(k, pl.ds(0, 8)), channel(k, pl.ds(ROWS - 8, 8)))
        for k in range(CHAN)
    ]
    rims = jnp.concatenate(rims + [jnp.zeros((8, COLS), jnp.float32)], axis=0)
    left = lax.broadcasted_iota(jnp.int32, (FR, COLS), 1) < HALF
    for b in range(K):
        rows = pl.ds(b * FR, FR)
        for g in range(2):
            base = g * FR * 8 + b * UNIT
            for c in range(PART):
                out_ref[pl.ds(base + c, FR, stride=8), :] = channel(PART * g + c, rows)
            half = channel(LAST, rows)
            rim = rims[g * FR : (g + 1) * FR]
            if g == 1:
                half = pltpu.roll(half, HALF, 1)
            if b == 0:
                rim = pltpu.roll(rim, HALF, 1)
            out_ref[pl.ds(base + PART, FR, stride=8), :] = jnp.where(left, half, rim)
    report.wait()


def clear_table(table_ref, first, count, value=-1):
    for i in range(count):
        table_ref[first + i] = value


def compact_tiles_kernel(units, place_ref, host_ref, own_ref, other_ref, out_ref, table_ref):
    block = UNIT * units
    me = lax.axis_index("row") * lax.axis_size("nest") + lax.axis_index("nest")
    sub = lax.broadcasted_iota(jnp.int32, (8, COLS), 0)
    sub_lane = lax.broadcasted_iota(jnp.int32, (8, COLS), 1)
    used = (sub_lane < HALF) | ((sub & (UNIT - 1)) < PART)
    half_of = jnp.where(used, jnp.where(sub < UNIT, 0, 1), 2)

    out_ref[...] = jnp.zeros_like(out_ref)
    clear_table(table_ref, 0, PEERS, 0)

    def place_one(n, carry):
        h = host_ref[0, n]
        t = div6(place_ref[0, n])
        u = table_ref[t]
        table_ref[t] = u + 1
        piece = other_ref[pl.ds(pl.multiple_of((h >> 1) * 8, 8), 8), :]
        piece = jnp.where((h & 1) != (u & 1), pltpu.roll(piece, UNIT, 0), piece)
        spot = pl.ds(pl.multiple_of(t * block + (u >> 1) * 8, 8), 8)
        pltpu.store(out_ref.at[spot, :], piece, mask=half_of == (u & 1))
        return carry

    lax.fori_loop(0, NESTS, place_one, 0, unroll=8)

    tile = lax.broadcasted_iota(jnp.int32, (PEERS, COLS), 0)
    lane = lax.broadcasted_iota(jnp.int32, (PEERS, COLS), 1)
    tile_col = tile & 7
    has_right, has_left = tile_col < 7, tile_col > 0
    lower_half = me < FR
    to_above = ((me >> 2) & 1) == 0

    def right_of(x):
        return pltpu.roll(x, PEERS - 1, 0)

    def left_of(x):
        return pltpu.roll(x, 1, 0)

    def row_of(i):
        return own_ref[pl.ds(i, PEERS, stride=8), :]

    packed = jnp.zeros((PEERS, COLS), jnp.float32)
    rims = []
    for b in range(K):
        for c in range(PART):
            x = row_of(UNIT * b + c)
            side = jnp.where(
                has_right & (lane < HALO),
                right_of(x),
                jnp.where(has_left & (lane >= COLS - HALO), left_of(x), 0.0),
            )
            packed += pltpu.roll(side, HALF + HALO + 8 * (PART * b + c), 1)
        x = row_of(UNIT * b + PART)
        right = jnp.where(has_right & (lane < HALO), right_of(x), 0.0)
        left = jnp.where(has_left & (lane >= HALF - HALO) & (lane < HALF), left_of(x), 0.0)
        spot = HALF + 8 * PART * K + HALO * b
        packed += jnp.where(
            lower_half, pltpu.roll(right, spot, 1), pltpu.roll(left, spot - HALF + HALO, 1)
        )
        rims.append(
            jnp.where(
                to_above,
                jnp.where(tile < PEERS - 8, pltpu.roll(x, PEERS - 8, 0), 0.0),
                jnp.where(tile >= 8, pltpu.roll(x, 8, 0), 0.0),
            )
        )
    right = jnp.where(has_right & (lane >= HALF) & (lane < HALF + HALO), right_of(rims[0]), 0.0)
    left = jnp.where(has_left & (lane >= COLS - HALO), left_of(rims[1]), 0.0)
    packed += pltpu.roll(right, HALF - HALO, 1) + pltpu.roll(left, COLS - HALO, 1)
    for u, value in enumerate([packed] + rims):
        spot = pl.ds(UNIT * u + PART, PEERS, stride=block)
        out_ref[spot, :] = jnp.where(lane >= HALF, value, out_ref[spot, :])


def compact_slots_kernel(place_ref, host_ref, own_ref, other_ref, out_ref, table_ref):
    me = lax.axis_index("row") * lax.axis_size("nest") + lax.axis_index("nest")
    sub = lax.broadcasted_iota(jnp.int32, (8, COLS), 0)
    lane = lax.broadcasted_iota(jnp.int32, (8, COLS), 1)
    whole = (sub & (UNIT - 1)) < PART
    half_of = jnp.where(sub < UNIT, 0, 1)
    is_outer = jnp.where(whole, jnp.where((lane >= PW) & (lane < COLS - PW), 1, 0), 0)
    is_outer = jnp.where(whole | (lane < HALF), is_outer, 1)
    is_east = jnp.where(whole, jnp.where(lane < HALF, 1, 0), jnp.where(me < FR, 1, 0))

    def unit(source_ref, i):
        piece = source_ref[pl.ds(pl.multiple_of((i >> 1) * 8, 8), 8), :]
        return jnp.where(half_of == (i & 1), piece, pltpu.roll(piece, UNIT, 0))

    def clear(n, carry):
        clear_table(table_ref, 3 * div3(place_ref[0, n]), SPOTS, 0)
        return carry

    def note(n, carry):
        table_ref[place_ref[0, n]] = host_ref[0, n]
        return carry

    def gather_band(n, carry):
        p = place_ref[0, n]
        h = host_ref[0, n]
        band = div3(p)
        j = p - 3 * band
        west = unit(own_ref, table_ref[3 * band + jnp.where(j == 0, 0, j - 1)])
        east = unit(own_ref, table_ref[3 * band + jnp.where(j == SPOTS - 1, SPOTS - 1, j + 1)])
        outer = unit(other_ref, band)
        moved = jnp.where(
            j == 0, pltpu.roll(outer, PW, 1), jnp.where(j == 1, outer, pltpu.roll(outer, COLS - PW, 1))
        )
        outer = jnp.where(whole, moved, pltpu.roll(outer, HALF, 1))
        value = jnp.where(is_outer == 1, outer, jnp.where(is_east == 1, east, west))
        spot = pl.ds(pl.multiple_of((h >> 1) * 8, 8), 8)
        pltpu.store(out_ref.at[spot, :], value, mask=half_of == (h & 1))
        return carry

    out_ref[...] = jnp.zeros_like(out_ref)
    lax.fori_loop(0, NESTS, clear, 0, unroll=8)
    lax.fori_loop(0, NESTS, note, 0, unroll=8)
    lax.fori_loop(0, NESTS, gather_band, 0, unroll=4)


class Nest(NamedTuple):
    row: int | jax.Array
    west: jax.Array
    east: jax.Array
    spread: jax.Array
    gather: jax.Array
    covers: jax.Array


def window_kernel(
    tile_side, units, place_ref, host_ref, state_ref, depth_ref, open_ref, got_ref, out_ref,
    outer_ref, fine_ref, rep_ref, table_ref,
):
    row = lax.axis_index("row")
    col = lax.axis_index("nest")
    row_count = lax.axis_size("row")
    col_count = lax.axis_size("nest")
    me = row * col_count + col
    block = UNIT * units
    lane = lax.broadcasted_iota(jnp.int32, (FR, COLS), 1)
    small_row = lax.broadcasted_iota(jnp.int32, (PH, COLS), 0)
    small_lane = lax.broadcasted_iota(jnp.int32, (PH, COLS), 1)

    def own(k, rows):
        if k < 3:
            return state_ref[0, k, rows, :]
        if k < 5:
            return depth_ref[0, k - 3, rows, :]
        return open_ref[0, k - 5, rows, :].astype(jnp.float32)

    def rows_of(peer, row, count):
        return got_ref[pl.ds(peer * block + row, count, stride=block), :]

    def got(k, unit):
        if k < LAST:
            return rows_of((k // PART) * FR, UNIT * unit + k % PART, FR)
        left, right = (rows_of(g * FR, UNIT * unit + PART, FR) for g in range(2))
        return jnp.where(lane < HALF, left, pltpu.roll(right, HALF, 1))

    def set_fine(nest, values):
        level, east_flux, south_flux, depth_east, depth_south, open_east, open_south = values
        fine_ref[nest, 0] = level
        fine_ref[nest, 1] = COURANT * east_flux
        fine_ref[nest, 2] = COURANT * south_flux
        fine_ref[nest, 3] = (COURANT * COURANT) * open_east * depth_east
        fine_ref[nest, 4] = (COURANT * COURANT) * open_south * depth_south
        fine_ref[nest, 5] = HALF_SQUARE * open_east
        fine_ref[nest, 6] = HALF_SQUARE * open_south

    if tile_side:

        def find(n, count):
            p = place_ref[0, n]
            table_ref[count] = p - 6 * me
            return count + jnp.where(div6(p) == me, 1, 0)

        count = lax.fori_loop(0, NESTS, find, 0, unroll=16)
        nests = []
        for u in range(units):
            p = jnp.where(u < count, table_ref[u], 0)
            b = jnp.where(p >= SPOTS, 1, 0)
            c0 = LEFT + PW * (p - SPOTS * b)
            offset = small_lane - c0
            nests.append(
                Nest(
                    HALO + TOP + FR * b,
                    c0 - 1,
                    c0 + PW,
                    c0 + (small_lane >> 2),
                    jnp.clip(RR * offset, 0, COLS - RR),
                    (offset >= 0) & (offset < PW) & (u < count),
                )
            )
        keep = (lane < HALO) | (lane >= COLS - HALO)
        small_keep = (small_lane < HALO) | (small_lane >= COLS - HALO)
        beside = [rows_of(g * FR, PART, FR) for g in range(2)]
        for k in range(CHAN):
            for b in range(K):
                rows = pl.ds(HALO + b * FR, FR)
                outer_ref[k, rows, 0:COLS] = own(k, pl.ds(b * FR, FR))
                if k < LAST:
                    shift = HALF + HALO + 8 * (PART * b + k % PART)
                    side = pltpu.roll(beside[k // PART], COLS - shift, 1)
                else:
                    shift = HALF + 8 * PART * K + HALO * b
                    side = jnp.where(
                        lane < HALO,
                        pltpu.roll(beside[0], COLS - shift, 1),
                        pltpu.roll(beside[1], COLS - HALO - shift, 1),
                    )
                outer_ref[k, rows, COLS : 2 * COLS] = jnp.where(keep, side, 0.0)
            rim = jnp.where(
                small_lane < HALF,
                pltpu.roll(rows_of(8 * k, UNIT + PART, 8), HALF, 1),
                rows_of(8 * k, 2 * UNIT + PART, 8),
            )
            corner = jnp.where(small_keep, pltpu.roll(rows_of(8 * k, PART, 8), HALO, 1), 0.0)
            for columns, value in ((pl.ds(0, COLS), rim), (pl.ds(COLS, COLS), corner)):
                outer_ref[k, EXT - HALO : EXT, columns] = value[:HALO]
                outer_ref[k, 0:HALO, columns] = value[HALO:]
        for u in range(units):
            set_fine(u, [got(k, u) for k in range(CHAN)])
    else:

        def note_host(n, carry):
            table_ref[host_ref[0, n]] = place_ref[0, n]
            return carry

        def note_place(n, carry):
            table_ref[place_ref[0, n]] = 1
            return carry

        clear_table(table_ref, K * me, K)
        lax.fori_loop(0, NESTS, note_host, 0, unroll=16)
        at = [table_ref[K * me + s] for s in range(K)]
        live = [p >= 0 for p in at]
        bands = [3 * div3(jnp.where(live[s], at[s], 0)) for s in range(K)]
        spots = [jnp.where(live[s], at[s] - bands[s], 0) for s in range(K)]
        for s in range(K):
            clear_table(table_ref, bands[s], SPOTS)
        lax.fori_loop(0, NESTS, note_place, 0, unroll=16)
        nests = []
        for s in range(K):
            j = spots[s]
            r0 = HALO + TOP + FR * s
            c0 = LEFT + PW * j
            offset = small_lane - c0
            west = (j > 0) & (table_ref[bands[s] + jnp.where(j > 0, j - 1, 0)] == 1)
            last = SPOTS - 1
            east = (j < last) & (table_ref[bands[s] + jnp.where(j < last, j + 1, last)] == 1)
            nests.append(
                Nest(
                    r0,
                    c0 - 1,
                    c0 + PW,
                    c0 + (small_lane >> 2),
                    jnp.clip(RR * offset, 0, COLS - RR),
                    (offset >= 0) & (offset < PW) & live[s],
                )
            )
            around = c0 + jnp.where(small_lane < HALF, PW, -PW) + (small_lane >> 2)
            nests.append(
                Nest(
                    r0,
                    c0 + PW - 1,
                    c0,
                    jnp.clip(around, 0, COLS - 1),
                    jnp.clip(RR * jnp.where(offset < 0, offset + PW, offset - PW), 0, COLS - RR),
                    ((offset >= -PH) & (offset < 0) & west)
                    | ((offset >= PW) & (offset < PW + PH) & east),
                )
            )
            set_fine(2 * s, [own(k, pl.ds(s * FR, FR)) for k in range(CHAN)])
            ends = [got(k, s) for k in range(CHAN)]
            set_fine(2 * s + 1, ends)
            for k in range(LAST):
                outer_ref[k, pl.ds(HALO + s * FR, FR), 0:COLS] = jnp.where(
                    j == 0,
                    pltpu.roll(ends[k], COLS - PW, 1),
                    jnp.where(j == 1, ends[k], pltpu.roll(ends[k], PW, 1)),
                )
            left, right = (rows_of(g * FR, UNIT * s + PART, FR) for g in range(2))
            outer_ref[LAST, pl.ds(HALO + s * FR, FR), 0:COLS] = jnp.where(
                lane < HALF, pltpu.roll(left, HALF, 1), right
            )
        for k in range(CHAN):
            outer_ref[k, 0:HALO, 0:COLS] = jnp.zeros((HALO, COLS), jnp.float32)
            outer_ref[k, EXT - HALO : EXT, 0:COLS] = jnp.zeros((HALO, COLS), jnp.float32)
            outer_ref[k, :, COLS : 2 * COLS] = jnp.zeros((EXT, COLS), jnp.float32)

    for flux in (1, 2):
        outer_ref[flux] = COURANT * outer_ref[flux]
        outer_ref[flux + 2] = (COURANT * COURANT) * outer_ref[flux + 4] * outer_ref[flux + 2]

    inside = None
    if tile_side:
        ext_row = lax.broadcasted_iota(jnp.int32, (EXT, 2 * COLS), 0)
        ext_lane = lax.broadcasted_iota(jnp.int32, (EXT, 2 * COLS), 1)
        row_low = jnp.where(row == 0, HALO, 0)
        row_high = jnp.where(row == row_count - 1, EXT - HALO, EXT)
        right_end = jnp.where(col < col_count - 1, COLS + HALO, COLS)
        left_start = jnp.where(col > 0, 2 * COLS - HALO, 2 * COLS)
        inside = (
            (ext_row >= row_low)
            & (ext_row < row_high)
            & ((ext_lane < right_end) | (ext_lane >= left_start))
        )


    def take(x, index):
        return jnp.take_along_axis(x, index, axis=1, mode="promise_in_bounds")

    def block_of(k, start):
        return outer_ref[k, pl.ds(pl.multiple_of(start, 8), PH), 0:COLS]

    def ghosts(slot):
        ends = []
        for i, nest in enumerate(nests):
            west = pltpu.roll(block_of(1, nest.row), COLS - nest.west, 1)
            east = pltpu.roll(block_of(0, nest.row), COLS - 1 - nest.east, 1)
            side = jnp.where(small_lane == 0, west, east)
            for m in range(RR):
                rep_ref[slot, i, pl.ds(m, PH, stride=RR), :] = side
            north = block_of(2, nest.row - PH)[PH - 1 :]
            south = block_of(0, nest.row + PH)[:1]
            ends.append(
                tuple(
                    take(jnp.broadcast_to(edge, (PH, COLS)), nest.spread)
                    for edge in (north, south)
                )
            )
        return ends

    def above(x, edge):
        x = pltpu.roll(x, 1, 0)
        return jnp.concatenate([jnp.where(small_row == 0, edge, x[:PH]), x[PH:]], axis=0)

    def below(x, edge):
        x = pltpu.roll(x, FR - 1, 0)
        end = jnp.where(small_row == PH - 1, edge, x[FR - PH :])
        return jnp.concatenate([x[: FR - PH], end], axis=0)

    old_ends = ghosts(0)
    for step in range(STEPS):
        old, new = step % 2, (step + 1) % 2
        surface, eastward, southward = outer_ref[0], outer_ref[1], outer_ref[2]
        flow = (eastward - pltpu.roll(eastward, 1, 1)) + (southward - pltpu.roll(southward, 1, 0))
        surface = surface - flow
        if inside is not None:
            surface = jnp.where(inside, surface, 0.0)
        to_east = pltpu.roll(surface, 2 * COLS - 1, 1)
        to_south = pltpu.roll(surface, EXT - 1, 0)
        eastward = outer_ref[5] * (
            eastward - HALF_SQUARE * (surface + to_east) * (to_east - surface)
        ) - outer_ref[3] * (to_east - surface)
        southward = outer_ref[6] * (
            southward - HALF_SQUARE * (surface + to_south) * (to_south - surface)
        ) - outer_ref[4] * (to_south - surface)
        outer_ref[0] = surface
        outer_ref[1] = eastward
        outer_ref[2] = southward
        new_ends = ghosts(new)
        for i, spot in enumerate(nests):
            level, east_flux, south_flux = (fine_ref[i, k] for k in range(3))
            old_side, new_side = rep_ref[old, i], rep_ref[new, i]
            (old_north, old_south), (new_north, new_south) = old_ends[i], new_ends[i]
            for m in range(1, RR + 1):
                part = m / RR
                side = old_side + part * (new_side - old_side)
                north = old_north + part * (new_north - old_north)
                south = old_south + part * (new_south - old_south)
                west_of = jnp.where(lane == 0, side, pltpu.roll(east_flux, 1, 1))
                north_of = above(south_flux, north)
                level = level - ((east_flux - west_of) + (south_flux - north_of))
                east_of = jnp.where(lane == COLS - 1, side, pltpu.roll(level, COLS - 1, 1))
                south_of = below(level, south)
                half_east, half_south = fine_ref[i, 5], fine_ref[i, 6]
                if step == 0 and m == 1:
                    east_flux = jnp.where(half_east == 0.0, 0.0, east_flux)
                    south_flux = jnp.where(half_south == 0.0, 0.0, south_flux)
                east_flux = east_flux - (fine_ref[i, 3] + half_east * (level + east_of)) * (
                    east_of - level
                )
                south_flux = south_flux - (fine_ref[i, 4] + half_south * (level + south_of)) * (
                    south_of - level
                )
            for k, value in enumerate((level, east_flux, south_flux)):
                fine_ref[i, k] = value

            def every(k, m):
                return fine_ref[i, k, pl.ds(m, PH, stride=RR), :]

            def quads(x):
                parts = [take(x, spot.gather + m) for m in range(RR)]
                return (parts[0] + parts[1]) + (parts[2] + parts[3])

            sum_level = (every(0, 0) + every(0, 1)) + (every(0, 2) + every(0, 3))
            sum_east = (every(1, 0) + every(1, 1)) + (every(1, 2) + every(1, 3))
            back = (
                quads(sum_level) * (1.0 / (RR * RR)),
                take(sum_east, spot.gather + (RR - 1)) * (1.0 / RR),
                quads(every(2, RR - 1)) * (1.0 / RR),
            )
            rows = pl.ds(pl.multiple_of(spot.row, 8), PH)
            for k in range(3):
                pltpu.store(outer_ref.at[k, rows, 0:COLS], back[k], mask=spot.covers)
        old_ends = new_ends

    for k in range(3):
        scale = 1.0 if k == 0 else 1.0 / COURANT
        if tile_side:
            out_ref[0, k] = outer_ref[k, HALO : HALO + ROWS, 0:COLS] * scale
        else:
            for s in range(K):
                rows = pl.ds(s * FR, FR)
                out_ref[0, k, rows, :] = jnp.where(
                    live[s], fine_ref[2 * s, k] * scale, state_ref[0, k, rows, :]
                )


def window(tile_side, units, place, host, pieces, others, state, depth, opening):
    block = UNIT * units
    nests = units if tile_side else K * 2
    table = pltpu.SMEM((PEERS * K * SPOTS,), jnp.int32)
    blocks = pl.pallas_call(
        functools.partial(compact_tiles_kernel, units) if tile_side else compact_slots_kernel,
        out_shape=jax.ShapeDtypeStruct((PEERS * block, COLS), jnp.float32),
        in_specs=[SMEM, SMEM, VMEM, VMEM],
        out_specs=VMEM,
        scratch_shapes=[table],
        compiler_params=pltpu.CompilerParams(vmem_limit_bytes=8 * 1024 * 1024),
        name="compact_tiles" if tile_side else "compact_slots",
    )(place, host, pieces.reshape(-1, COLS), others.reshape(-1, COLS))
    got = lax.all_to_all(
        blocks.reshape(PEERS, block, COLS),
        ("row", "nest"),
        split_axis=0,
        concat_axis=0,
        tiled=True,
    )
    return pl.pallas_call(
        functools.partial(window_kernel, tile_side, units),
        out_shape=jax.ShapeDtypeStruct(state.shape, jnp.float32),
        in_specs=[SMEM, SMEM, VMEM, VMEM, VMEM, VMEM],
        out_specs=VMEM,
        scratch_shapes=[
            pltpu.VMEM((CHAN, EXT, 2 * COLS), jnp.float32),
            pltpu.VMEM((nests, CHAN, FR, COLS), jnp.float32),
            pltpu.VMEM((2, nests, FR, COLS), jnp.float32),
            table,
        ],
        compiler_params=pltpu.CompilerParams(vmem_limit_bytes=32 * 1024 * 1024),
        name="window_tiles" if tile_side else "window_slots",
    )(place, host, state, depth, opening, got.reshape(-1, COLS))


def on_device(ocean_state, face_depth, face_open, nest_place, nest_host):
    tiles = ("row", "nest")
    packed, place, host, crowded = pl.pallas_call(
        pack_kernel,
        out_shape=(
            jax.ShapeDtypeStruct((PEERS * 8, COLS), jnp.float32),
            jax.ShapeDtypeStruct((1, NESTS), jnp.int32),
            jax.ShapeDtypeStruct((1, NESTS), jnp.int32),
            jax.ShapeDtypeStruct((1, 1), jnp.int32),
        ),
        in_specs=[pl.BlockSpec(memory_space=pltpu.HBM)] * 5,
        out_specs=(VMEM, VMEM, VMEM, pl.BlockSpec(memory_space=pltpu.HBM)),
        scratch_shapes=[
            pltpu.VMEM(ocean_state.shape, jnp.float32),
            pltpu.VMEM(face_depth.shape, jnp.float32),
            pltpu.VMEM(face_open.shape, jnp.int32),
            pltpu.VMEM((1, 1), jnp.int32),
            pltpu.SemaphoreType.DMA((6,)),
        ],
        compiler_params=pltpu.CompilerParams(vmem_limit_bytes=4 * 1024 * 1024),
        name="pack",
    )(*(
        pltpu.with_memory_space_constraint(x, pltpu.HBM)
        for x in (nest_place.reshape(1, NESTS), nest_host.reshape(1, NESTS), ocean_state, face_depth, face_open)
    ))
    pieces = lax.all_to_all(
        packed.reshape(PEERS, 8, COLS), tiles, split_axis=0, concat_axis=0, tiled=True
    )
    others = lax.ppermute(pieces, "sec", [(0, 1), (1, 0)])
    which = jnp.where(lax.axis_index("sec") == 0, crowded[0, 0], 2)
    return lax.switch(
        which,
        [
            functools.partial(window, True, FEW),
            functools.partial(window, True, MANY),
            functools.partial(window, False, SLOT_UNITS),
        ],
        place, host, pieces, others, ocean_state, face_depth, face_open,
    )


def solution(mesh):
    placed = (
        P("sec", None, "row", "nest"),
        P("sec", None, "row", "nest"),
        P("sec", None, "row", "nest"),
        P(),
        P(),
    )
    return jax.shard_map(
        on_device,
        mesh=mesh,
        in_specs=placed,
        out_specs=P("sec", None, "row", "nest"),
        check_vma=False,
    )
```

```python
import functools
from typing import NamedTuple

import jax
import jax.numpy as jnp
from jax import lax
from jax.experimental import pallas as pl
from jax.experimental.pallas import tpu as pltpu
from jax.sharding import PartitionSpec as P

PH = 8
PW = 32
RR = 4
K = 2
STEPS = 4
NESTS = 64
COURANT = 0.3

ROWS = 64
COLS = 128
FR = RR * PH
SPOTS = RR - 1
PEERS = 64
HALO = 4
EXT = ROWS + 2 * HALO
TOP = (RR - 1) * PH // 2
LEFT = PW // 2
CHAN = 7
UNIT = 4
FEW = 4
MANY = K * SPOTS
SLOT_UNITS = K
HALF = COLS // 2
LAST = CHAN - 1
PART = LAST // 2
HALF_SQUARE = 0.5 * COURANT * COURANT

VMEM = pl.BlockSpec(memory_space=pltpu.VMEM)
SMEM = pl.BlockSpec(memory_space=pltpu.SMEM)


def div6(p):
    return (p * 10923) >> 16


def div3(p):
    return (p * 21846) >> 16


def pack_kernel(
    place_in, host_in, state_in, depth_in, open_in,
    out_ref, place_ref, host_ref, state_ref, depth_ref, open_ref, sems,
):
    moves = [
        pltpu.make_async_copy(source, target, sems.at[i])
        for i, (source, target) in enumerate(
            (
                (place_in, place_ref), (host_in, host_ref),
                (state_in, state_ref), (depth_in, depth_ref), (open_in, open_ref),
            )
        )
    ]
    for move in moves:
        move.start()
    for move in moves:
        move.wait()

    def channel(k, rows):
        if k < 3:
            return state_ref[0, k, rows, :]
        if k < 5:
            return depth_ref[0, k - 3, rows, :]
        return open_ref[0, k - 5, rows, :].astype(jnp.float32)

    first = lax.broadcasted_iota(jnp.int32, (8, COLS), 0) < HALO
    rims = [
        jnp.where(first, channel(k, pl.ds(0, 8)), channel(k, pl.ds(ROWS - 8, 8)))
        for k in range(CHAN)
    ]
    rims = jnp.concatenate(rims + [jnp.zeros((8, COLS), jnp.float32)], axis=0)
    left = lax.broadcasted_iota(jnp.int32, (FR, COLS), 1) < HALF
    for b in range(K):
        rows = pl.ds(b * FR, FR)
        for g in range(2):
            base = g * FR * 8 + b * UNIT
            for c in range(PART):
                out_ref[pl.ds(base + c, FR, stride=8), :] = channel(PART * g + c, rows)
            half = channel(LAST, rows)
            rim = rims[g * FR : (g + 1) * FR]
            if g == 1:
                half = pltpu.roll(half, HALF, 1)
            if b == 0:
                rim = pltpu.roll(rim, HALF, 1)
            out_ref[pl.ds(base + PART, FR, stride=8), :] = jnp.where(left, half, rim)


def count_kernel(place_ref, pieces_ref, crowded_ref):
    tile = lax.broadcasted_iota(jnp.int32, (PEERS, NESTS), 0)
    hits = jnp.where(div6(place_ref[...]) == tile, 1.0, 0.0)
    most = jnp.max(jnp.sum(hits, axis=1, keepdims=True), axis=0, keepdims=True)
    crowded_ref[...] = jnp.where(most > FEW, 1, 0)


def clear_table(table_ref, first, count, value=-1):
    for i in range(count):
        table_ref[first + i] = value


def compact_tiles_kernel(units, place_ref, host_ref, own_ref, other_ref, out_ref, table_ref):
    block = UNIT * units
    me = lax.axis_index("row") * lax.axis_size("nest") + lax.axis_index("nest")
    used = (lax.broadcasted_iota(jnp.int32, (UNIT, COLS), 1) < HALF) | (
        lax.broadcasted_iota(jnp.int32, (UNIT, COLS), 0) < PART
    )

    out_ref[...] = jnp.zeros_like(out_ref)
    clear_table(table_ref, 0, PEERS, 0)

    def place_one(n, carry):
        h = host_ref[0, n]
        t = div6(place_ref[0, n])
        u = table_ref[t]
        table_ref[t] = u + 1
        piece = other_ref[pl.ds(pl.multiple_of(h * UNIT, UNIT), UNIT), :]
        spot = pl.ds(pl.multiple_of(t * block + u * UNIT, UNIT), UNIT)
        pltpu.store(out_ref.at[spot, :], piece, mask=used)
        return carry

    lax.fori_loop(0, NESTS, place_one, 0, unroll=16)

    tile = lax.broadcasted_iota(jnp.int32, (PEERS, COLS), 0)
    lane = lax.broadcasted_iota(jnp.int32, (PEERS, COLS), 1)
    tile_col = tile & 7
    has_right, has_left = tile_col < 7, tile_col > 0
    lower_half = me < FR
    to_above = ((me >> 2) & 1) == 0

    def right_of(x):
        return pltpu.roll(x, PEERS - 1, 0)

    def left_of(x):
        return pltpu.roll(x, 1, 0)

    def row_of(i):
        return own_ref[pl.ds(i, PEERS, stride=8), :]

    packed = jnp.zeros((PEERS, COLS), jnp.float32)
    rims = []
    for b in range(K):
        for c in range(PART):
            x = row_of(UNIT * b + c)
            side = jnp.where(
                has_right & (lane < HALO),
                right_of(x),
                jnp.where(has_left & (lane >= COLS - HALO), left_of(x), 0.0),
            )
            packed += pltpu.roll(side, HALF + HALO + 8 * (PART * b + c), 1)
        x = row_of(UNIT * b + PART)
        right = jnp.where(has_right & (lane < HALO), right_of(x), 0.0)
        left = jnp.where(has_left & (lane >= HALF - HALO) & (lane < HALF), left_of(x), 0.0)
        spot = HALF + 8 * PART * K + HALO * b
        packed += jnp.where(
            lower_half, pltpu.roll(right, spot, 1), pltpu.roll(left, spot - HALF + HALO, 1)
        )
        rims.append(
            jnp.where(
                to_above,
                jnp.where(tile < PEERS - 8, pltpu.roll(x, PEERS - 8, 0), 0.0),
                jnp.where(tile >= 8, pltpu.roll(x, 8, 0), 0.0),
            )
        )
    right = jnp.where(has_right & (lane >= HALF) & (lane < HALF + HALO), right_of(rims[0]), 0.0)
    left = jnp.where(has_left & (lane >= COLS - HALO), left_of(rims[1]), 0.0)
    packed += pltpu.roll(right, HALF - HALO, 1) + pltpu.roll(left, COLS - HALO, 1)
    for u, value in enumerate([packed] + rims):
        spot = pl.ds(UNIT * u + PART, PEERS, stride=block)
        out_ref[spot, :] = jnp.where(lane >= HALF, value, out_ref[spot, :])


def compact_slots_kernel(place_ref, host_ref, own_ref, other_ref, out_ref, table_ref):
    me = lax.axis_index("row") * lax.axis_size("nest") + lax.axis_index("nest")
    lane = lax.broadcasted_iota(jnp.int32, (UNIT, COLS), 1)
    whole = lax.broadcasted_iota(jnp.int32, (UNIT, COLS), 0) < PART
    is_outer = jnp.where(whole, jnp.where((lane >= PW) & (lane < COLS - PW), 1, 0), 0)
    is_outer = jnp.where(whole | (lane < HALF), is_outer, 1)
    is_east = jnp.where(whole, jnp.where(lane < HALF, 1, 0), jnp.where(me < FR, 1, 0))

    def unit(source_ref, i):
        return source_ref[pl.ds(pl.multiple_of(i * UNIT, UNIT), UNIT), :]

    def clear(n, carry):
        clear_table(table_ref, 3 * div3(place_ref[0, n]), SPOTS, 0)
        return carry

    def note(n, carry):
        table_ref[place_ref[0, n]] = host_ref[0, n]
        return carry

    def gather_band(n, carry):
        p = place_ref[0, n]
        h = host_ref[0, n]
        band = div3(p)
        j = p - 3 * band
        west = unit(own_ref, table_ref[3 * band + jnp.where(j == 0, 0, j - 1)])
        east = unit(own_ref, table_ref[3 * band + jnp.where(j == SPOTS - 1, SPOTS - 1, j + 1)])
        outer = unit(other_ref, band)
        moved = jnp.where(
            j == 0, pltpu.roll(outer, PW, 1), jnp.where(j == 1, outer, pltpu.roll(outer, COLS - PW, 1))
        )
        outer = jnp.where(whole, moved, pltpu.roll(outer, HALF, 1))
        value = jnp.where(is_outer == 1, outer, jnp.where(is_east == 1, east, west))
        out_ref[pl.ds(pl.multiple_of(h * UNIT, UNIT), UNIT), :] = value
        return carry

    out_ref[...] = jnp.zeros_like(out_ref)
    lax.fori_loop(0, NESTS, clear, 0, unroll=8)
    lax.fori_loop(0, NESTS, note, 0, unroll=8)
    lax.fori_loop(0, NESTS, gather_band, 0, unroll=8)


class Nest(NamedTuple):
    row: int | jax.Array
    west: jax.Array
    east: jax.Array
    spread: jax.Array
    gather: jax.Array
    covers: jax.Array


def window_kernel(
    tile_side, units, place_ref, host_ref, state_ref, depth_ref, open_ref, got_ref, out_ref,
    outer_ref, fine_ref, rep_ref, table_ref,
):
    row = lax.axis_index("row")
    col = lax.axis_index("nest")
    row_count = lax.axis_size("row")
    col_count = lax.axis_size("nest")
    me = row * col_count + col
    block = UNIT * units
    lane = lax.broadcasted_iota(jnp.int32, (FR, COLS), 1)
    small_row = lax.broadcasted_iota(jnp.int32, (PH, COLS), 0)
    small_lane = lax.broadcasted_iota(jnp.int32, (PH, COLS), 1)

    def own(k, rows):
        if k < 3:
            return state_ref[0, k, rows, :]
        if k < 5:
            return depth_ref[0, k - 3, rows, :]
        return open_ref[0, k - 5, rows, :].astype(jnp.float32)

    def rows_of(peer, row, count):
        return got_ref[pl.ds(peer * block + row, count, stride=block), :]

    def got(k, unit):
        if k < LAST:
            return rows_of((k // PART) * FR, UNIT * unit + k % PART, FR)
        left, right = (rows_of(g * FR, UNIT * unit + PART, FR) for g in range(2))
        return jnp.where(lane < HALF, left, pltpu.roll(right, HALF, 1))

    def set_fine(nest, values):
        level, east_flux, south_flux, depth_east, depth_south, open_east, open_south = values
        fine_ref[nest, 0] = level
        fine_ref[nest, 1] = COURANT * east_flux
        fine_ref[nest, 2] = COURANT * south_flux
        fine_ref[nest, 3] = (COURANT * COURANT) * open_east * depth_east
        fine_ref[nest, 4] = (COURANT * COURANT) * open_south * depth_south
        fine_ref[nest, 5] = HALF_SQUARE * open_east
        fine_ref[nest, 6] = HALF_SQUARE * open_south

    if tile_side:

        def find(n, count):
            p = place_ref[0, n]
            table_ref[count] = p - 6 * me
            return count + jnp.where(div6(p) == me, 1, 0)

        count = lax.fori_loop(0, NESTS, find, 0, unroll=16)
        nests = []
        for u in range(units):
            p = jnp.where(u < count, table_ref[u], 0)
            b = jnp.where(p >= SPOTS, 1, 0)
            c0 = LEFT + PW * (p - SPOTS * b)
            offset = small_lane - c0
            nests.append(
                Nest(
                    HALO + TOP + FR * b,
                    c0 - 1,
                    c0 + PW,
                    c0 + (small_lane >> 2),
                    jnp.clip(RR * offset, 0, COLS - RR),
                    (offset >= 0) & (offset < PW) & (u < count),
                )
            )
        keep = (lane < HALO) | (lane >= COLS - HALO)
        small_keep = (small_lane < HALO) | (small_lane >= COLS - HALO)
        beside = [rows_of(g * FR, PART, FR) for g in range(2)]
        for k in range(CHAN):
            for b in range(K):
                rows = pl.ds(HALO + b * FR, FR)
                outer_ref[k, rows, 0:COLS] = own(k, pl.ds(b * FR, FR))
                if k < LAST:
                    shift = HALF + HALO + 8 * (PART * b + k % PART)
                    side = pltpu.roll(beside[k // PART], COLS - shift, 1)
                else:
                    shift = HALF + 8 * PART * K + HALO * b
                    side = jnp.where(
                        lane < HALO,
                        pltpu.roll(beside[0], COLS - shift, 1),
                        pltpu.roll(beside[1], COLS - HALO - shift, 1),
                    )
                outer_ref[k, rows, COLS : 2 * COLS] = jnp.where(keep, side, 0.0)
            rim = jnp.where(
                small_lane < HALF,
                pltpu.roll(rows_of(8 * k, UNIT + PART, 8), HALF, 1),
                rows_of(8 * k, 2 * UNIT + PART, 8),
            )
            corner = jnp.where(small_keep, pltpu.roll(rows_of(8 * k, PART, 8), HALO, 1), 0.0)
            for columns, value in ((pl.ds(0, COLS), rim), (pl.ds(COLS, COLS), corner)):
                outer_ref[k, EXT - HALO : EXT, columns] = value[:HALO]
                outer_ref[k, 0:HALO, columns] = value[HALO:]
        for u in range(units):
            set_fine(u, [got(k, u) for k in range(CHAN)])
    else:

        def note_host(n, carry):
            table_ref[host_ref[0, n]] = place_ref[0, n]
            return carry

        def note_place(n, carry):
            table_ref[place_ref[0, n]] = 1
            return carry

        clear_table(table_ref, K * me, K)
        lax.fori_loop(0, NESTS, note_host, 0, unroll=16)
        at = [table_ref[K * me + s] for s in range(K)]
        live = [p >= 0 for p in at]
        bands = [3 * div3(jnp.where(live[s], at[s], 0)) for s in range(K)]
        spots = [jnp.where(live[s], at[s] - bands[s], 0) for s in range(K)]
        for s in range(K):
            clear_table(table_ref, bands[s], SPOTS)
        lax.fori_loop(0, NESTS, note_place, 0, unroll=16)
        nests = []
        for s in range(K):
            j = spots[s]
            r0 = HALO + TOP + FR * s
            c0 = LEFT + PW * j
            offset = small_lane - c0
            west = (j > 0) & (table_ref[bands[s] + jnp.where(j > 0, j - 1, 0)] == 1)
            last = SPOTS - 1
            east = (j < last) & (table_ref[bands[s] + jnp.where(j < last, j + 1, last)] == 1)
            nests.append(
                Nest(
                    r0,
                    c0 - 1,
                    c0 + PW,
                    c0 + (small_lane >> 2),
                    jnp.clip(RR * offset, 0, COLS - RR),
                    (offset >= 0) & (offset < PW) & live[s],
                )
            )
            around = c0 + jnp.where(small_lane < HALF, PW, -PW) + (small_lane >> 2)
            nests.append(
                Nest(
                    r0,
                    c0 + PW - 1,
                    c0,
                    jnp.clip(around, 0, COLS - 1),
                    jnp.clip(RR * jnp.where(offset < 0, offset + PW, offset - PW), 0, COLS - RR),
                    ((offset >= -PH) & (offset < 0) & west)
                    | ((offset >= PW) & (offset < PW + PH) & east),
                )
            )
            set_fine(2 * s, [own(k, pl.ds(s * FR, FR)) for k in range(CHAN)])
            ends = [got(k, s) for k in range(CHAN)]
            set_fine(2 * s + 1, ends)
            for k in range(LAST):
                outer_ref[k, pl.ds(HALO + s * FR, FR), 0:COLS] = jnp.where(
                    j == 0,
                    pltpu.roll(ends[k], COLS - PW, 1),
                    jnp.where(j == 1, ends[k], pltpu.roll(ends[k], PW, 1)),
                )
            left, right = (rows_of(g * FR, UNIT * s + PART, FR) for g in range(2))
            outer_ref[LAST, pl.ds(HALO + s * FR, FR), 0:COLS] = jnp.where(
                lane < HALF, pltpu.roll(left, HALF, 1), right
            )
        for k in range(CHAN):
            outer_ref[k, 0:HALO, 0:COLS] = jnp.zeros((HALO, COLS), jnp.float32)
            outer_ref[k, EXT - HALO : EXT, 0:COLS] = jnp.zeros((HALO, COLS), jnp.float32)
            outer_ref[k, :, COLS : 2 * COLS] = jnp.zeros((EXT, COLS), jnp.float32)

    for flux in (1, 2):
        outer_ref[flux] = COURANT * outer_ref[flux]
        outer_ref[flux + 2] = (COURANT * COURANT) * outer_ref[flux + 4] * outer_ref[flux + 2]

    inside = None
    if tile_side:
        ext_row = lax.broadcasted_iota(jnp.int32, (EXT, 2 * COLS), 0)
        ext_lane = lax.broadcasted_iota(jnp.int32, (EXT, 2 * COLS), 1)
        row_low = jnp.where(row == 0, HALO, 0)
        row_high = jnp.where(row == row_count - 1, EXT - HALO, EXT)
        right_end = jnp.where(col < col_count - 1, COLS + HALO, COLS)
        left_start = jnp.where(col > 0, 2 * COLS - HALO, 2 * COLS)
        inside = (
            (ext_row >= row_low)
            & (ext_row < row_high)
            & ((ext_lane < right_end) | (ext_lane >= left_start))
        )


    def take(x, index):
        return jnp.take_along_axis(x, index, axis=1, mode="promise_in_bounds")

    def block_of(k, start):
        return outer_ref[k, pl.ds(pl.multiple_of(start, 8), PH), 0:COLS]

    def ghosts(slot):
        ends = []
        for i, nest in enumerate(nests):
            west = pltpu.roll(block_of(1, nest.row), COLS - nest.west, 1)
            east = pltpu.roll(block_of(0, nest.row), COLS - 1 - nest.east, 1)
            side = jnp.where(small_lane == 0, west, east)
            for m in range(RR):
                rep_ref[slot, i, pl.ds(m, PH, stride=RR), :] = side
            north = block_of(2, nest.row - PH)[PH - 1 :]
            south = block_of(0, nest.row + PH)[:1]
            ends.append(
                tuple(
                    take(jnp.broadcast_to(edge, (PH, COLS)), nest.spread)
                    for edge in (north, south)
                )
            )
        return ends

    def above(x, edge):
        x = pltpu.roll(x, 1, 0)
        return jnp.concatenate([jnp.where(small_row == 0, edge, x[:PH]), x[PH:]], axis=0)

    def below(x, edge):
        x = pltpu.roll(x, FR - 1, 0)
        end = jnp.where(small_row == PH - 1, edge, x[FR - PH :])
        return jnp.concatenate([x[: FR - PH], end], axis=0)

    old_ends = ghosts(0)
    for step in range(STEPS):
        old, new = step % 2, (step + 1) % 2
        surface, eastward, southward = outer_ref[0], outer_ref[1], outer_ref[2]
        flow = (eastward - pltpu.roll(eastward, 1, 1)) + (southward - pltpu.roll(southward, 1, 0))
        surface = surface - flow
        if inside is not None:
            surface = jnp.where(inside, surface, 0.0)
        to_east = pltpu.roll(surface, 2 * COLS - 1, 1)
        to_south = pltpu.roll(surface, EXT - 1, 0)
        eastward = outer_ref[5] * (
            eastward - HALF_SQUARE * (surface + to_east) * (to_east - surface)
        ) - outer_ref[3] * (to_east - surface)
        southward = outer_ref[6] * (
            southward - HALF_SQUARE * (surface + to_south) * (to_south - surface)
        ) - outer_ref[4] * (to_south - surface)
        outer_ref[0] = surface
        outer_ref[1] = eastward
        outer_ref[2] = southward
        new_ends = ghosts(new)
        for i, spot in enumerate(nests):
            level, east_flux, south_flux = (fine_ref[i, k] for k in range(3))
            old_side, new_side = rep_ref[old, i], rep_ref[new, i]
            (old_north, old_south), (new_north, new_south) = old_ends[i], new_ends[i]
            for m in range(1, RR + 1):
                part = m / RR
                side = old_side + part * (new_side - old_side)
                north = old_north + part * (new_north - old_north)
                south = old_south + part * (new_south - old_south)
                west_of = jnp.where(lane == 0, side, pltpu.roll(east_flux, 1, 1))
                north_of = above(south_flux, north)
                level = level - ((east_flux - west_of) + (south_flux - north_of))
                east_of = jnp.where(lane == COLS - 1, side, pltpu.roll(level, COLS - 1, 1))
                south_of = below(level, south)
                half_east, half_south = fine_ref[i, 5], fine_ref[i, 6]
                if step == 0 and m == 1:
                    east_flux = jnp.where(half_east == 0.0, 0.0, east_flux)
                    south_flux = jnp.where(half_south == 0.0, 0.0, south_flux)
                east_flux = east_flux - (fine_ref[i, 3] + half_east * (level + east_of)) * (
                    east_of - level
                )
                south_flux = south_flux - (fine_ref[i, 4] + half_south * (level + south_of)) * (
                    south_of - level
                )
            for k, value in enumerate((level, east_flux, south_flux)):
                fine_ref[i, k] = value

            def every(k, m):
                return fine_ref[i, k, pl.ds(m, PH, stride=RR), :]

            def quads(x):
                parts = [take(x, spot.gather + m) for m in range(RR)]
                return (parts[0] + parts[1]) + (parts[2] + parts[3])

            sum_level = (every(0, 0) + every(0, 1)) + (every(0, 2) + every(0, 3))
            sum_east = (every(1, 0) + every(1, 1)) + (every(1, 2) + every(1, 3))
            back = (
                quads(sum_level) * (1.0 / (RR * RR)),
                take(sum_east, spot.gather + (RR - 1)) * (1.0 / RR),
                quads(every(2, RR - 1)) * (1.0 / RR),
            )
            rows = pl.ds(pl.multiple_of(spot.row, 8), PH)
            for k in range(3):
                pltpu.store(outer_ref.at[k, rows, 0:COLS], back[k], mask=spot.covers)
        old_ends = new_ends

    for k in range(3):
        scale = 1.0 if k == 0 else 1.0 / COURANT
        if tile_side:
            out_ref[0, k] = outer_ref[k, HALO : HALO + ROWS, 0:COLS] * scale
        else:
            for s in range(K):
                rows = pl.ds(s * FR, FR)
                out_ref[0, k, rows, :] = jnp.where(
                    live[s], fine_ref[2 * s, k] * scale, state_ref[0, k, rows, :]
                )


def window(tile_side, units, place, host, pieces, others, state, depth, opening):
    block = UNIT * units
    nests = units if tile_side else K * 2
    table = pltpu.SMEM((PEERS * K * SPOTS,), jnp.int32)
    blocks = pl.pallas_call(
        functools.partial(compact_tiles_kernel, units) if tile_side else compact_slots_kernel,
        out_shape=jax.ShapeDtypeStruct((PEERS * block, COLS), jnp.float32),
        in_specs=[SMEM, SMEM, VMEM, VMEM],
        out_specs=VMEM,
        scratch_shapes=[table],
        compiler_params=pltpu.CompilerParams(vmem_limit_bytes=8 * 1024 * 1024),
        name="compact_tiles" if tile_side else "compact_slots",
    )(place, host, pieces.reshape(-1, COLS), others.reshape(-1, COLS))
    got = lax.all_to_all(
        blocks.reshape(PEERS, block, COLS),
        ("row", "nest"),
        split_axis=0,
        concat_axis=0,
        tiled=True,
    )
    return pl.pallas_call(
        functools.partial(window_kernel, tile_side, units),
        out_shape=jax.ShapeDtypeStruct(state.shape, jnp.float32),
        in_specs=[SMEM, SMEM, VMEM, VMEM, VMEM, VMEM],
        out_specs=VMEM,
        scratch_shapes=[
            pltpu.VMEM((CHAN, EXT, 2 * COLS), jnp.float32),
            pltpu.VMEM((nests, CHAN, FR, COLS), jnp.float32),
            pltpu.VMEM((2, nests, FR, COLS), jnp.float32),
            table,
        ],
        compiler_params=pltpu.CompilerParams(vmem_limit_bytes=32 * 1024 * 1024),
        name="window_tiles" if tile_side else "window_slots",
    )(place, host, state, depth, opening, got.reshape(-1, COLS))


def on_device(ocean_state, face_depth, face_open, nest_place, nest_host):
    tiles = ("row", "nest")
    packed, place, host = pl.pallas_call(
        pack_kernel,
        out_shape=(
            jax.ShapeDtypeStruct((PEERS * 8, COLS), jnp.float32),
            jax.ShapeDtypeStruct((1, NESTS), jnp.int32),
            jax.ShapeDtypeStruct((1, NESTS), jnp.int32),
        ),
        in_specs=[pl.BlockSpec(memory_space=pltpu.HBM)] * 5,
        out_specs=(VMEM, VMEM, VMEM),
        scratch_shapes=[
            pltpu.VMEM(ocean_state.shape, jnp.float32),
            pltpu.VMEM(face_depth.shape, jnp.float32),
            pltpu.VMEM(face_open.shape, jnp.int32),
            pltpu.SemaphoreType.DMA((5,)),
        ],
        compiler_params=pltpu.CompilerParams(vmem_limit_bytes=4 * 1024 * 1024),
        name="pack",
    )(*(
        pltpu.with_memory_space_constraint(x, pltpu.HBM)
        for x in (nest_place.reshape(1, NESTS), nest_host.reshape(1, NESTS), ocean_state, face_depth, face_open)
    ))
    pieces = lax.all_to_all(
        packed.reshape(PEERS, 8, COLS), tiles, split_axis=0, concat_axis=0, tiled=True
    )
    others = lax.ppermute(pieces, "sec", [(0, 1), (1, 0)])
    crowded = pl.pallas_call(
        count_kernel,
        out_shape=jax.ShapeDtypeStruct((1, 1), jnp.int32),
        in_specs=[VMEM, pl.BlockSpec(memory_space=pl.ANY)],
        out_specs=VMEM,
        compiler_params=pltpu.CompilerParams(vmem_limit_bytes=4 * 1024 * 1024),
        name="count",
    )(place, pieces)
    which = jnp.where(lax.axis_index("sec") == 0, crowded[0, 0], 2)
    return lax.switch(
        which,
        [
            functools.partial(window, True, FEW),
            functools.partial(window, True, MANY),
            functools.partial(window, False, SLOT_UNITS),
        ],
        place, host, pieces, others, ocean_state, face_depth, face_open,
    )


def solution(mesh):
    placed = (
        P("sec", None, "row", "nest"),
        P("sec", None, "row", "nest"),
        P("sec", None, "row", "nest"),
        P(),
        P(),
    )
    return jax.shard_map(
        on_device,
        mesh=mesh,
        in_specs=placed,
        out_specs=P("sec", None, "row", "nest"),
        check_vma=False,
    )
```

```python
import functools
from typing import NamedTuple

import jax
import jax.numpy as jnp
from jax import lax
from jax.experimental import pallas as pl
from jax.experimental.pallas import tpu as pltpu
from jax.sharding import PartitionSpec as P

PH = 8
PW = 32
RR = 4
K = 2
STEPS = 4
NESTS = 64
COURANT = 0.3

ROWS = 64
COLS = 128
FR = RR * PH
SPOTS = RR - 1
PEERS = 64
HALO = 4
EXT = ROWS + 2 * HALO
TOP = (RR - 1) * PH // 2
LEFT = PW // 2
CHAN = 7
UNIT = 4
FEW = 4
MANY = K * SPOTS
SLOT_UNITS = K
HALF = COLS // 2
LAST = CHAN - 1
PART = LAST // 2
HALF_SQUARE = 0.5 * COURANT * COURANT

VMEM = pl.BlockSpec(memory_space=pltpu.VMEM)
SMEM = pl.BlockSpec(memory_space=pltpu.SMEM)


def div6(p):
    return (p * 10923) >> 16


def div3(p):
    return (p * 21846) >> 16


def pack_kernel(
    place_in, host_in, state_in, depth_in, open_in,
    out_ref, place_ref, host_ref, state_ref, depth_ref, open_ref, sems,
):
    moves = [
        pltpu.make_async_copy(source, target, sems.at[i])
        for i, (source, target) in enumerate(
            (
                (place_in, place_ref), (host_in, host_ref),
                (state_in, state_ref), (depth_in, depth_ref), (open_in, open_ref),
            )
        )
    ]
    for move in moves:
        move.start()
    for move in moves:
        move.wait()

    def channel(k, rows):
        if k < 3:
            return state_ref[0, k, rows, :]
        if k < 5:
            return depth_ref[0, k - 3, rows, :]
        return open_ref[0, k - 5, rows, :].astype(jnp.float32)

    first = lax.broadcasted_iota(jnp.int32, (8, COLS), 0) < HALO
    rims = [
        jnp.where(first, channel(k, pl.ds(0, 8)), channel(k, pl.ds(ROWS - 8, 8)))
        for k in range(CHAN)
    ]
    rims = jnp.concatenate(rims + [jnp.zeros((8, COLS), jnp.float32)], axis=0)
    left = lax.broadcasted_iota(jnp.int32, (FR, COLS), 1) < HALF
    for b in range(K):
        rows = pl.ds(b * FR, FR)
        for g in range(2):
            base = g * FR * 8 + b * UNIT
            for c in range(PART):
                out_ref[pl.ds(base + c, FR, stride=8), :] = channel(PART * g + c, rows)
            half = channel(LAST, rows)
            rim = rims[g * FR : (g + 1) * FR]
            if g == 1:
                half = pltpu.roll(half, HALF, 1)
            if b == 0:
                rim = pltpu.roll(rim, HALF, 1)
            out_ref[pl.ds(base + PART, FR, stride=8), :] = jnp.where(left, half, rim)


def prepare_kernel(place_ref, own_ref, crowded_ref, halo_ref):
    me = lax.axis_index("row") * lax.axis_size("nest") + lax.axis_index("nest")
    hit_tile = lax.broadcasted_iota(jnp.int32, (PEERS, NESTS), 0)
    hits = jnp.where(div6(place_ref[...]) == hit_tile, 1.0, 0.0)
    most = jnp.max(jnp.sum(hits, axis=1, keepdims=True), axis=0, keepdims=True)
    crowded_ref[...] = jnp.where(most > FEW, 1, 0)

    tile = lax.broadcasted_iota(jnp.int32, (PEERS, COLS), 0)
    lane = lax.broadcasted_iota(jnp.int32, (PEERS, COLS), 1)
    tile_col = tile & 7
    has_right, has_left = tile_col < 7, tile_col > 0
    lower_half = me < FR
    to_above = ((me >> 2) & 1) == 0

    def right_of(x):
        return pltpu.roll(x, PEERS - 1, 0)

    def left_of(x):
        return pltpu.roll(x, 1, 0)

    def row_of(i):
        return own_ref[pl.ds(i, PEERS, stride=8), :]

    packed = jnp.zeros((PEERS, COLS), jnp.float32)
    rims = []
    for b in range(K):
        for c in range(PART):
            x = row_of(UNIT * b + c)
            side = jnp.where(
                has_right & (lane < HALO),
                right_of(x),
                jnp.where(has_left & (lane >= COLS - HALO), left_of(x), 0.0),
            )
            packed += pltpu.roll(side, HALF + HALO + 8 * (PART * b + c), 1)
        x = row_of(UNIT * b + PART)
        right = jnp.where(has_right & (lane < HALO), right_of(x), 0.0)
        left = jnp.where(has_left & (lane >= HALF - HALO) & (lane < HALF), left_of(x), 0.0)
        spot = HALF + 8 * PART * K + HALO * b
        packed += jnp.where(
            lower_half, pltpu.roll(right, spot, 1), pltpu.roll(left, spot - HALF + HALO, 1)
        )
        rims.append(
            jnp.where(
                to_above,
                jnp.where(tile < PEERS - 8, pltpu.roll(x, PEERS - 8, 0), 0.0),
                jnp.where(tile >= 8, pltpu.roll(x, 8, 0), 0.0),
            )
        )
    right = jnp.where(has_right & (lane >= HALF) & (lane < HALF + HALO), right_of(rims[0]), 0.0)
    left = jnp.where(has_left & (lane >= COLS - HALO), left_of(rims[1]), 0.0)
    packed += pltpu.roll(right, HALF - HALO, 1) + pltpu.roll(left, COLS - HALO, 1)
    for u, value in enumerate([packed] + rims):
        halo_ref[u] = value


def clear_table(table_ref, first, count, value=-1):
    for i in range(count):
        table_ref[first + i] = value


def compact_tiles_kernel(units, place_ref, host_ref, halo_ref, other_ref, out_ref, table_ref):
    block = UNIT * units
    used = (lax.broadcasted_iota(jnp.int32, (UNIT, COLS), 1) < HALF) | (
        lax.broadcasted_iota(jnp.int32, (UNIT, COLS), 0) < PART
    )

    out_ref[...] = jnp.zeros_like(out_ref)
    clear_table(table_ref, 0, PEERS, 0)

    def place_one(n, carry):
        h = host_ref[0, n]
        t = div6(place_ref[0, n])
        u = table_ref[t]
        table_ref[t] = u + 1
        piece = other_ref[pl.ds(pl.multiple_of(h * UNIT, UNIT), UNIT), :]
        spot = pl.ds(pl.multiple_of(t * block + u * UNIT, UNIT), UNIT)
        pltpu.store(out_ref.at[spot, :], piece, mask=used)
        return carry

    lax.fori_loop(0, NESTS, place_one, 0, unroll=True)

    lane = lax.broadcasted_iota(jnp.int32, (PEERS, COLS), 1)
    for u in range(SPOTS):
        spot = pl.ds(UNIT * u + PART, PEERS, stride=block)
        out_ref[spot, :] = jnp.where(lane >= HALF, halo_ref[u], out_ref[spot, :])


def compact_slots_kernel(place_ref, host_ref, own_ref, other_ref, out_ref, table_ref):
    me = lax.axis_index("row") * lax.axis_size("nest") + lax.axis_index("nest")
    lane = lax.broadcasted_iota(jnp.int32, (UNIT, COLS), 1)
    whole = lax.broadcasted_iota(jnp.int32, (UNIT, COLS), 0) < PART
    is_outer = jnp.where(whole, jnp.where((lane >= PW) & (lane < COLS - PW), 1, 0), 0)
    is_outer = jnp.where(whole | (lane < HALF), is_outer, 1)
    is_east = jnp.where(whole, jnp.where(lane < HALF, 1, 0), jnp.where(me < FR, 1, 0))

    def unit(source_ref, i):
        return source_ref[pl.ds(pl.multiple_of(i * UNIT, UNIT), UNIT), :]

    def clear(n, carry):
        clear_table(table_ref, 3 * div3(place_ref[0, n]), SPOTS, 0)
        return carry

    def note(n, carry):
        table_ref[place_ref[0, n]] = host_ref[0, n]
        return carry

    def gather_band(n, carry):
        p = place_ref[0, n]
        h = host_ref[0, n]
        band = div3(p)
        j = p - 3 * band
        west = unit(own_ref, table_ref[3 * band + jnp.where(j == 0, 0, j - 1)])
        east = unit(own_ref, table_ref[3 * band + jnp.where(j == SPOTS - 1, SPOTS - 1, j + 1)])
        outer = unit(other_ref, band)
        moved = jnp.where(
            j == 0, pltpu.roll(outer, PW, 1), jnp.where(j == 1, outer, pltpu.roll(outer, COLS - PW, 1))
        )
        outer = jnp.where(whole, moved, pltpu.roll(outer, HALF, 1))
        value = jnp.where(is_outer == 1, outer, jnp.where(is_east == 1, east, west))
        out_ref[pl.ds(pl.multiple_of(h * UNIT, UNIT), UNIT), :] = value
        return carry

    out_ref[...] = jnp.zeros_like(out_ref)
    lax.fori_loop(0, NESTS, clear, 0, unroll=8)
    lax.fori_loop(0, NESTS, note, 0, unroll=8)
    lax.fori_loop(0, NESTS, gather_band, 0, unroll=8)


class Nest(NamedTuple):
    row: int | jax.Array
    west: jax.Array
    east: jax.Array
    spread: jax.Array
    gather: jax.Array
    covers: jax.Array


def window_kernel(
    tile_side, units, place_ref, host_ref, state_ref, depth_ref, open_ref, got_ref, out_ref,
    outer_ref, fine_ref, rep_ref, table_ref,
):
    row = lax.axis_index("row")
    col = lax.axis_index("nest")
    row_count = lax.axis_size("row")
    col_count = lax.axis_size("nest")
    me = row * col_count + col
    block = UNIT * units
    lane = lax.broadcasted_iota(jnp.int32, (FR, COLS), 1)
    small_row = lax.broadcasted_iota(jnp.int32, (PH, COLS), 0)
    small_lane = lax.broadcasted_iota(jnp.int32, (PH, COLS), 1)

    def own(k, rows):
        if k < 3:
            return state_ref[0, k, rows, :]
        if k < 5:
            return depth_ref[0, k - 3, rows, :]
        return open_ref[0, k - 5, rows, :].astype(jnp.float32)

    def rows_of(peer, row, count):
        return got_ref[pl.ds(peer * block + row, count, stride=block), :]

    def got(k, unit):
        if k < LAST:
            return rows_of((k // PART) * FR, UNIT * unit + k % PART, FR)
        left, right = (rows_of(g * FR, UNIT * unit + PART, FR) for g in range(2))
        return jnp.where(lane < HALF, left, pltpu.roll(right, HALF, 1))

    def set_fine(nest, values):
        level, east_flux, south_flux, depth_east, depth_south, open_east, open_south = values
        fine_ref[nest, 0] = level
        fine_ref[nest, 1] = COURANT * east_flux
        fine_ref[nest, 2] = COURANT * south_flux
        fine_ref[nest, 3] = (COURANT * COURANT) * open_east * depth_east
        fine_ref[nest, 4] = (COURANT * COURANT) * open_south * depth_south
        fine_ref[nest, 5] = HALF_SQUARE * open_east
        fine_ref[nest, 6] = HALF_SQUARE * open_south

    if tile_side:

        def find(n, count):
            p = place_ref[0, n]
            table_ref[count] = p - 6 * me
            return count + jnp.where(div6(p) == me, 1, 0)

        count = lax.fori_loop(0, NESTS, find, 0, unroll=True)
        nests = []
        for u in range(units):
            p = jnp.where(u < count, table_ref[u], 0)
            b = jnp.where(p >= SPOTS, 1, 0)
            c0 = LEFT + PW * (p - SPOTS * b)
            offset = small_lane - c0
            nests.append(
                Nest(
                    HALO + TOP + FR * b,
                    c0 - 1,
                    c0 + PW,
                    c0 + (small_lane >> 2),
                    jnp.clip(RR * offset, 0, COLS - RR),
                    (offset >= 0) & (offset < PW) & (u < count),
                )
            )
        keep = (lane < HALO) | (lane >= COLS - HALO)
        small_keep = (small_lane < HALO) | (small_lane >= COLS - HALO)
        beside = [rows_of(g * FR, PART, FR) for g in range(2)]
        for k in range(CHAN):
            for b in range(K):
                rows = pl.ds(HALO + b * FR, FR)
                outer_ref[k, rows, 0:COLS] = own(k, pl.ds(b * FR, FR))
                if k < LAST:
                    shift = HALF + HALO + 8 * (PART * b + k % PART)
                    side = pltpu.roll(beside[k // PART], COLS - shift, 1)
                else:
                    shift = HALF + 8 * PART * K + HALO * b
                    side = jnp.where(
                        lane < HALO,
                        pltpu.roll(beside[0], COLS - shift, 1),
                        pltpu.roll(beside[1], COLS - HALO - shift, 1),
                    )
                outer_ref[k, rows, COLS : 2 * COLS] = jnp.where(keep, side, 0.0)
            rim = jnp.where(
                small_lane < HALF,
                pltpu.roll(rows_of(8 * k, UNIT + PART, 8), HALF, 1),
                rows_of(8 * k, 2 * UNIT + PART, 8),
            )
            corner = jnp.where(small_keep, pltpu.roll(rows_of(8 * k, PART, 8), HALO, 1), 0.0)
            for columns, value in ((pl.ds(0, COLS), rim), (pl.ds(COLS, COLS), corner)):
                outer_ref[k, EXT - HALO : EXT, columns] = value[:HALO]
                outer_ref[k, 0:HALO, columns] = value[HALO:]
        for u in range(units):
            set_fine(u, [got(k, u) for k in range(CHAN)])
    else:

        def note_host(n, carry):
            table_ref[host_ref[0, n]] = place_ref[0, n]
            return carry

        def note_place(n, carry):
            table_ref[place_ref[0, n]] = 1
            return carry

        clear_table(table_ref, K * me, K)
        lax.fori_loop(0, NESTS, note_host, 0, unroll=16)
        at = [table_ref[K * me + s] for s in range(K)]
        live = [p >= 0 for p in at]
        bands = [3 * div3(jnp.where(live[s], at[s], 0)) for s in range(K)]
        spots = [jnp.where(live[s], at[s] - bands[s], 0) for s in range(K)]
        for s in range(K):
            clear_table(table_ref, bands[s], SPOTS)
        lax.fori_loop(0, NESTS, note_place, 0, unroll=16)
        nests = []
        for s in range(K):
            j = spots[s]
            r0 = HALO + TOP + FR * s
            c0 = LEFT + PW * j
            offset = small_lane - c0
            west = (j > 0) & (table_ref[bands[s] + jnp.where(j > 0, j - 1, 0)] == 1)
            last = SPOTS - 1
            east = (j < last) & (table_ref[bands[s] + jnp.where(j < last, j + 1, last)] == 1)
            nests.append(
                Nest(
                    r0,
                    c0 - 1,
                    c0 + PW,
                    c0 + (small_lane >> 2),
                    jnp.clip(RR * offset, 0, COLS - RR),
                    (offset >= 0) & (offset < PW) & live[s],
                )
            )
            around = c0 + jnp.where(small_lane < HALF, PW, -PW) + (small_lane >> 2)
            nests.append(
                Nest(
                    r0,
                    c0 + PW - 1,
                    c0,
                    jnp.clip(around, 0, COLS - 1),
                    jnp.clip(RR * jnp.where(offset < 0, offset + PW, offset - PW), 0, COLS - RR),
                    ((offset >= -PH) & (offset < 0) & west)
                    | ((offset >= PW) & (offset < PW + PH) & east),
                )
            )
            set_fine(2 * s, [own(k, pl.ds(s * FR, FR)) for k in range(CHAN)])
            ends = [got(k, s) for k in range(CHAN)]
            set_fine(2 * s + 1, ends)
            for k in range(LAST):
                outer_ref[k, pl.ds(HALO + s * FR, FR), 0:COLS] = jnp.where(
                    j == 0,
                    pltpu.roll(ends[k], COLS - PW, 1),
                    jnp.where(j == 1, ends[k], pltpu.roll(ends[k], PW, 1)),
                )
            left, right = (rows_of(g * FR, UNIT * s + PART, FR) for g in range(2))
            outer_ref[LAST, pl.ds(HALO + s * FR, FR), 0:COLS] = jnp.where(
                lane < HALF, pltpu.roll(left, HALF, 1), right
            )
        for k in range(CHAN):
            outer_ref[k, 0:HALO, 0:COLS] = jnp.zeros((HALO, COLS), jnp.float32)
            outer_ref[k, EXT - HALO : EXT, 0:COLS] = jnp.zeros((HALO, COLS), jnp.float32)
            outer_ref[k, :, COLS : 2 * COLS] = jnp.zeros((EXT, COLS), jnp.float32)

    for flux in (1, 2):
        outer_ref[flux] = COURANT * outer_ref[flux]
        outer_ref[flux + 2] = (COURANT * COURANT) * outer_ref[flux + 4] * outer_ref[flux + 2]

    inside = None
    if tile_side:
        ext_row = lax.broadcasted_iota(jnp.int32, (EXT, 2 * COLS), 0)
        ext_lane = lax.broadcasted_iota(jnp.int32, (EXT, 2 * COLS), 1)
        row_low = jnp.where(row == 0, HALO, 0)
        row_high = jnp.where(row == row_count - 1, EXT - HALO, EXT)
        right_end = jnp.where(col < col_count - 1, COLS + HALO, COLS)
        left_start = jnp.where(col > 0, 2 * COLS - HALO, 2 * COLS)
        inside = (
            (ext_row >= row_low)
            & (ext_row < row_high)
            & ((ext_lane < right_end) | (ext_lane >= left_start))
        )


    def take(x, index):
        return jnp.take_along_axis(x, index, axis=1, mode="promise_in_bounds")

    def block_of(k, start):
        return outer_ref[k, pl.ds(pl.multiple_of(start, 8), PH), 0:COLS]

    def ghosts(slot):
        ends = []
        for i, nest in enumerate(nests):
            west = pltpu.roll(block_of(1, nest.row), COLS - nest.west, 1)
            east = pltpu.roll(block_of(0, nest.row), COLS - 1 - nest.east, 1)
            side = jnp.where(small_lane == 0, west, east)
            for m in range(RR):
                rep_ref[slot, i, pl.ds(m, PH, stride=RR), :] = side
            north = block_of(2, nest.row - PH)[PH - 1 :]
            south = block_of(0, nest.row + PH)[:1]
            ends.append(
                tuple(
                    take(jnp.broadcast_to(edge, (PH, COLS)), nest.spread)
                    for edge in (north, south)
                )
            )
        return ends

    def above(x, edge):
        x = pltpu.roll(x, 1, 0)
        return jnp.concatenate([jnp.where(small_row == 0, edge, x[:PH]), x[PH:]], axis=0)

    def below(x, edge):
        x = pltpu.roll(x, FR - 1, 0)
        end = jnp.where(small_row == PH - 1, edge, x[FR - PH :])
        return jnp.concatenate([x[: FR - PH], end], axis=0)

    old_ends = ghosts(0)
    for step in range(STEPS):
        old, new = step % 2, (step + 1) % 2
        surface, eastward, southward = outer_ref[0], outer_ref[1], outer_ref[2]
        flow = (eastward - pltpu.roll(eastward, 1, 1)) + (southward - pltpu.roll(southward, 1, 0))
        surface = surface - flow
        if inside is not None:
            surface = jnp.where(inside, surface, 0.0)
        to_east = pltpu.roll(surface, 2 * COLS - 1, 1)
        to_south = pltpu.roll(surface, EXT - 1, 0)
        eastward = outer_ref[5] * (
            eastward - HALF_SQUARE * (surface + to_east) * (to_east - surface)
        ) - outer_ref[3] * (to_east - surface)
        southward = outer_ref[6] * (
            southward - HALF_SQUARE * (surface + to_south) * (to_south - surface)
        ) - outer_ref[4] * (to_south - surface)
        outer_ref[0] = surface
        outer_ref[1] = eastward
        outer_ref[2] = southward
        new_ends = ghosts(new)
        for i, spot in enumerate(nests):
            level, east_flux, south_flux = (fine_ref[i, k] for k in range(3))
            old_side, new_side = rep_ref[old, i], rep_ref[new, i]
            (old_north, old_south), (new_north, new_south) = old_ends[i], new_ends[i]
            for m in range(1, RR + 1):
                part = m / RR
                side = old_side + part * (new_side - old_side)
                north = old_north + part * (new_north - old_north)
                south = old_south + part * (new_south - old_south)
                west_of = jnp.where(lane == 0, side, pltpu.roll(east_flux, 1, 1))
                north_of = above(south_flux, north)
                level = level - ((east_flux - west_of) + (south_flux - north_of))
                east_of = jnp.where(lane == COLS - 1, side, pltpu.roll(level, COLS - 1, 1))
                south_of = below(level, south)
                half_east, half_south = fine_ref[i, 5], fine_ref[i, 6]
                if step == 0 and m == 1:
                    east_flux = jnp.where(half_east == 0.0, 0.0, east_flux)
                    south_flux = jnp.where(half_south == 0.0, 0.0, south_flux)
                east_flux = east_flux - (fine_ref[i, 3] + half_east * (level + east_of)) * (
                    east_of - level
                )
                south_flux = south_flux - (fine_ref[i, 4] + half_south * (level + south_of)) * (
                    south_of - level
                )
            for k, value in enumerate((level, east_flux, south_flux)):
                fine_ref[i, k] = value

            def every(k, m):
                return fine_ref[i, k, pl.ds(m, PH, stride=RR), :]

            def quads(x):
                parts = [take(x, spot.gather + m) for m in range(RR)]
                return (parts[0] + parts[1]) + (parts[2] + parts[3])

            sum_level = (every(0, 0) + every(0, 1)) + (every(0, 2) + every(0, 3))
            sum_east = (every(1, 0) + every(1, 1)) + (every(1, 2) + every(1, 3))
            back = (
                quads(sum_level) * (1.0 / (RR * RR)),
                take(sum_east, spot.gather + (RR - 1)) * (1.0 / RR),
                quads(every(2, RR - 1)) * (1.0 / RR),
            )
            rows = pl.ds(pl.multiple_of(spot.row, 8), PH)
            for k in range(3):
                pltpu.store(outer_ref.at[k, rows, 0:COLS], back[k], mask=spot.covers)
        old_ends = new_ends

    for k in range(3):
        scale = 1.0 if k == 0 else 1.0 / COURANT
        if tile_side:
            out_ref[0, k] = outer_ref[k, HALO : HALO + ROWS, 0:COLS] * scale
        else:
            for s in range(K):
                rows = pl.ds(s * FR, FR)
                out_ref[0, k, rows, :] = jnp.where(
                    live[s], fine_ref[2 * s, k] * scale, state_ref[0, k, rows, :]
                )


def window(tile_side, units, place, host, pieces, halos, others, state, depth, opening):
    block = UNIT * units
    nests = units if tile_side else K * 2
    table = pltpu.SMEM((PEERS * K * SPOTS,), jnp.int32)
    blocks = pl.pallas_call(
        functools.partial(compact_tiles_kernel, units) if tile_side else compact_slots_kernel,
        out_shape=jax.ShapeDtypeStruct((PEERS * block, COLS), jnp.float32),
        in_specs=[SMEM, SMEM, VMEM, VMEM],
        out_specs=VMEM,
        scratch_shapes=[table],
        compiler_params=pltpu.CompilerParams(vmem_limit_bytes=8 * 1024 * 1024),
        name="compact_tiles" if tile_side else "compact_slots",
    )(place, host, halos if tile_side else pieces.reshape(-1, COLS), others.reshape(-1, COLS))
    got = lax.all_to_all(
        blocks.reshape(PEERS, block, COLS),
        ("row", "nest"),
        split_axis=0,
        concat_axis=0,
        tiled=True,
    )
    return pl.pallas_call(
        functools.partial(window_kernel, tile_side, units),
        out_shape=jax.ShapeDtypeStruct(state.shape, jnp.float32),
        in_specs=[SMEM, SMEM, VMEM, VMEM, VMEM, VMEM],
        out_specs=VMEM,
        scratch_shapes=[
            pltpu.VMEM((CHAN, EXT, 2 * COLS), jnp.float32),
            pltpu.VMEM((nests, CHAN, FR, COLS), jnp.float32),
            pltpu.VMEM((2, nests, FR, COLS), jnp.float32),
            table,
        ],
        compiler_params=pltpu.CompilerParams(vmem_limit_bytes=32 * 1024 * 1024),
        name="window_tiles" if tile_side else "window_slots",
    )(place, host, state, depth, opening, got.reshape(-1, COLS))


def on_device(ocean_state, face_depth, face_open, nest_place, nest_host):
    tiles = ("row", "nest")
    packed, place, host = pl.pallas_call(
        pack_kernel,
        out_shape=(
            jax.ShapeDtypeStruct((PEERS * 8, COLS), jnp.float32),
            jax.ShapeDtypeStruct((1, NESTS), jnp.int32),
            jax.ShapeDtypeStruct((1, NESTS), jnp.int32),
        ),
        in_specs=[pl.BlockSpec(memory_space=pltpu.HBM)] * 5,
        out_specs=(VMEM, VMEM, VMEM),
        scratch_shapes=[
            pltpu.VMEM(ocean_state.shape, jnp.float32),
            pltpu.VMEM(face_depth.shape, jnp.float32),
            pltpu.VMEM(face_open.shape, jnp.int32),
            pltpu.SemaphoreType.DMA((5,)),
        ],
        compiler_params=pltpu.CompilerParams(vmem_limit_bytes=4 * 1024 * 1024),
        name="pack",
    )(*(
        pltpu.with_memory_space_constraint(x, pltpu.HBM)
        for x in (nest_place.reshape(1, NESTS), nest_host.reshape(1, NESTS), ocean_state, face_depth, face_open)
    ))
    pieces = lax.all_to_all(
        packed.reshape(PEERS, 8, COLS), tiles, split_axis=0, concat_axis=0, tiled=True
    )
    others = lax.ppermute(pieces, "sec", [(0, 1), (1, 0)])
    crowded, halos = pl.pallas_call(
        prepare_kernel,
        out_shape=(
            jax.ShapeDtypeStruct((1, 1), jnp.int32),
            jax.ShapeDtypeStruct((SPOTS, PEERS, COLS), jnp.float32),
        ),
        in_specs=[VMEM, VMEM],
        out_specs=(VMEM, VMEM),
        compiler_params=pltpu.CompilerParams(vmem_limit_bytes=4 * 1024 * 1024),
        name="prepare",
    )(place, pieces.reshape(-1, COLS))
    which = jnp.where(lax.axis_index("sec") == 0, crowded[0, 0], 2)
    return lax.switch(
        which,
        [
            functools.partial(window, True, FEW),
            functools.partial(window, True, MANY),
            functools.partial(window, False, SLOT_UNITS),
        ],
        place, host, pieces, halos, others, ocean_state, face_depth, face_open,
    )


def solution(mesh):
    placed = (
        P("sec", None, "row", "nest"),
        P("sec", None, "row", "nest"),
        P("sec", None, "row", "nest"),
        P(),
        P(),
    )
    return jax.shard_map(
        on_device,
        mesh=mesh,
        in_specs=placed,
        out_specs=P("sec", None, "row", "nest"),
        check_vma=False,
    )
```

```python
import functools
from typing import NamedTuple

import jax
import jax.numpy as jnp
from jax import lax
from jax.experimental import pallas as pl
from jax.experimental.pallas import tpu as pltpu
from jax.sharding import PartitionSpec as P

PH = 8
PW = 32
RR = 4
K = 2
STEPS = 4
NESTS = 64
COURANT = 0.3

ROWS = 64
COLS = 128
FR = RR * PH
SPOTS = RR - 1
PEERS = 64
HALO = 4
EXT = ROWS + 2 * HALO
TOP = (RR - 1) * PH // 2
LEFT = PW // 2
CHAN = 7
UNIT = 4
FEW = 4
MANY = K * SPOTS
SLOT_UNITS = K
HALF = COLS // 2
LAST = CHAN - 1
PART = LAST // 2
HALF_SQUARE = 0.5 * COURANT * COURANT

VMEM = pl.BlockSpec(memory_space=pltpu.VMEM)
SMEM = pl.BlockSpec(memory_space=pltpu.SMEM)


def div6(p):
    return (p * 10923) >> 16


def div3(p):
    return (p * 21846) >> 16


def pack_kernel(
    place_in, host_in, state_in, depth_in, open_in,
    out_ref, place_ref, host_ref, state_ref, depth_ref, open_ref, sems,
):
    moves = [
        pltpu.make_async_copy(source, target, sems.at[i])
        for i, (source, target) in enumerate(
            (
                (place_in, place_ref), (host_in, host_ref),
                (state_in, state_ref), (depth_in, depth_ref), (open_in, open_ref),
            )
        )
    ]
    for move in moves:
        move.start()
    for move in moves:
        move.wait()

    def channel(k, rows):
        if k < 3:
            return state_ref[0, k, rows, :]
        if k < 5:
            return depth_ref[0, k - 3, rows, :]
        return open_ref[0, k - 5, rows, :].astype(jnp.float32)

    first = lax.broadcasted_iota(jnp.int32, (8, COLS), 0) < HALO
    rims = [
        jnp.where(first, channel(k, pl.ds(0, 8)), channel(k, pl.ds(ROWS - 8, 8)))
        for k in range(CHAN)
    ]
    rims = jnp.concatenate(rims + [jnp.zeros((8, COLS), jnp.float32)], axis=0)
    left = lax.broadcasted_iota(jnp.int32, (FR, COLS), 1) < HALF
    for b in range(K):
        rows = pl.ds(b * FR, FR)
        for g in range(2):
            base = g * FR * 8 + b * UNIT
            for c in range(PART):
                out_ref[pl.ds(base + c, FR, stride=8), :] = channel(PART * g + c, rows)
            half = channel(LAST, rows)
            rim = rims[g * FR : (g + 1) * FR]
            if g == 1:
                half = pltpu.roll(half, HALF, 1)
            if b == 0:
                rim = pltpu.roll(rim, HALF, 1)
            out_ref[pl.ds(base + PART, FR, stride=8), :] = jnp.where(left, half, rim)


def prepare_kernel(place_ref, own_ref, crowded_ref, halo_ref):
    me = lax.axis_index("row") * lax.axis_size("nest") + lax.axis_index("nest")
    hit_tile = lax.broadcasted_iota(jnp.int32, (PEERS, NESTS), 0)
    hits = jnp.where(div6(place_ref[...]) == hit_tile, 1.0, 0.0)
    most = jnp.max(jnp.sum(hits, axis=1, keepdims=True), axis=0, keepdims=True)
    crowded_ref[...] = jnp.where(most > FEW, 1, 0)

    tile = lax.broadcasted_iota(jnp.int32, (PEERS, COLS), 0)
    lane = lax.broadcasted_iota(jnp.int32, (PEERS, COLS), 1)
    tile_col = tile & 7
    has_right, has_left = tile_col < 7, tile_col > 0
    lower_half = me < FR
    to_above = ((me >> 2) & 1) == 0

    def right_of(x):
        return pltpu.roll(x, PEERS - 1, 0)

    def left_of(x):
        return pltpu.roll(x, 1, 0)

    def row_of(i):
        return own_ref[pl.ds(i, PEERS, stride=8), :]

    packed = jnp.zeros((PEERS, COLS), jnp.float32)
    rims = []
    for b in range(K):
        for c in range(PART):
            x = row_of(UNIT * b + c)
            side = jnp.where(
                has_right & (lane < HALO),
                right_of(x),
                jnp.where(has_left & (lane >= COLS - HALO), left_of(x), 0.0),
            )
            packed += pltpu.roll(side, HALF + HALO + 8 * (PART * b + c), 1)
        x = row_of(UNIT * b + PART)
        right = jnp.where(has_right & (lane < HALO), right_of(x), 0.0)
        left = jnp.where(has_left & (lane >= HALF - HALO) & (lane < HALF), left_of(x), 0.0)
        spot = HALF + 8 * PART * K + HALO * b
        packed += jnp.where(
            lower_half, pltpu.roll(right, spot, 1), pltpu.roll(left, spot - HALF + HALO, 1)
        )
        rims.append(
            jnp.where(
                to_above,
                jnp.where(tile < PEERS - 8, pltpu.roll(x, PEERS - 8, 0), 0.0),
                jnp.where(tile >= 8, pltpu.roll(x, 8, 0), 0.0),
            )
        )
    right = jnp.where(has_right & (lane >= HALF) & (lane < HALF + HALO), right_of(rims[0]), 0.0)
    left = jnp.where(has_left & (lane >= COLS - HALO), left_of(rims[1]), 0.0)
    packed += pltpu.roll(right, HALF - HALO, 1) + pltpu.roll(left, COLS - HALO, 1)
    for u, value in enumerate([packed] + rims):
        halo_ref[u] = value


def clear_table(table_ref, first, count, value=-1):
    for i in range(count):
        table_ref[first + i] = value


def compact_tiles_kernel(units, place_ref, host_ref, halo_ref, other_ref, out_ref, table_ref):
    block = UNIT * units
    used = (lax.broadcasted_iota(jnp.int32, (UNIT, COLS), 1) < HALF) | (
        lax.broadcasted_iota(jnp.int32, (UNIT, COLS), 0) < PART
    )

    out_ref[...] = jnp.zeros_like(out_ref)
    lane = lax.broadcasted_iota(jnp.int32, (PEERS, COLS), 1)
    for u in range(SPOTS):
        spot = pl.ds(UNIT * u + PART, PEERS, stride=block)
        out_ref[spot, :] = jnp.where(lane >= HALF, halo_ref[u], 0.0)
    clear_table(table_ref, 0, PEERS, 0)

    def place_one(n, carry):
        h = host_ref[0, n]
        t = div6(place_ref[0, n])
        u = table_ref[t]
        table_ref[t] = u + 1
        piece = other_ref[pl.ds(pl.multiple_of(h * UNIT, UNIT), UNIT), :]
        spot = pl.ds(pl.multiple_of(t * block + u * UNIT, UNIT), UNIT)
        pltpu.store(out_ref.at[spot, :], piece, mask=used)
        return carry

    lax.fori_loop(0, NESTS, place_one, 0, unroll=True)


def compact_slots_kernel(place_ref, host_ref, own_ref, other_ref, out_ref, table_ref):
    me = lax.axis_index("row") * lax.axis_size("nest") + lax.axis_index("nest")
    lane = lax.broadcasted_iota(jnp.int32, (UNIT, COLS), 1)
    whole = lax.broadcasted_iota(jnp.int32, (UNIT, COLS), 0) < PART
    is_outer = jnp.where(whole, jnp.where((lane >= PW) & (lane < COLS - PW), 1, 0), 0)
    is_outer = jnp.where(whole | (lane < HALF), is_outer, 1)
    is_east = jnp.where(whole, jnp.where(lane < HALF, 1, 0), jnp.where(me < FR, 1, 0))

    def unit(source_ref, i):
        return source_ref[pl.ds(pl.multiple_of(i * UNIT, UNIT), UNIT), :]

    def clear(n, carry):
        clear_table(table_ref, 3 * div3(place_ref[0, n]), SPOTS, 0)
        return carry

    def note(n, carry):
        table_ref[place_ref[0, n]] = host_ref[0, n]
        return carry

    def gather_band(n, carry):
        p = place_ref[0, n]
        h = host_ref[0, n]
        band = div3(p)
        j = p - 3 * band
        west = unit(own_ref, table_ref[3 * band + jnp.where(j == 0, 0, j - 1)])
        east = unit(own_ref, table_ref[3 * band + jnp.where(j == SPOTS - 1, SPOTS - 1, j + 1)])
        outer = unit(other_ref, band)
        moved = jnp.where(
            j == 0, pltpu.roll(outer, PW, 1), jnp.where(j == 1, outer, pltpu.roll(outer, COLS - PW, 1))
        )
        outer = jnp.where(whole, moved, pltpu.roll(outer, HALF, 1))
        value = jnp.where(is_outer == 1, outer, jnp.where(is_east == 1, east, west))
        out_ref[pl.ds(pl.multiple_of(h * UNIT, UNIT), UNIT), :] = value
        return carry

    out_ref[...] = jnp.zeros_like(out_ref)
    lax.fori_loop(0, NESTS, clear, 0, unroll=True)
    lax.fori_loop(0, NESTS, note, 0, unroll=True)
    lax.fori_loop(0, NESTS, gather_band, 0, unroll=8)


class Nest(NamedTuple):
    row: int | jax.Array
    west: jax.Array
    east: jax.Array
    spread: jax.Array
    gather: jax.Array
    covers: jax.Array


def window_kernel(
    tile_side, units, place_ref, host_ref, state_ref, depth_ref, open_ref, got_ref, out_ref,
    outer_ref, fine_ref, rep_ref, table_ref,
):
    row = lax.axis_index("row")
    col = lax.axis_index("nest")
    row_count = lax.axis_size("row")
    col_count = lax.axis_size("nest")
    me = row * col_count + col
    block = UNIT * units
    lane = lax.broadcasted_iota(jnp.int32, (FR, COLS), 1)
    small_row = lax.broadcasted_iota(jnp.int32, (PH, COLS), 0)
    small_lane = lax.broadcasted_iota(jnp.int32, (PH, COLS), 1)

    def own(k, rows):
        if k < 3:
            return state_ref[0, k, rows, :]
        if k < 5:
            return depth_ref[0, k - 3, rows, :]
        return open_ref[0, k - 5, rows, :].astype(jnp.float32)

    def rows_of(peer, row, count):
        return got_ref[pl.ds(peer * block + row, count, stride=block), :]

    def got(k, unit):
        if k < LAST:
            return rows_of((k // PART) * FR, UNIT * unit + k % PART, FR)
        left, right = (rows_of(g * FR, UNIT * unit + PART, FR) for g in range(2))
        return jnp.where(lane < HALF, left, pltpu.roll(right, HALF, 1))

    def set_fine(nest, values):
        level, east_flux, south_flux, depth_east, depth_south, open_east, open_south = values
        fine_ref[nest, 0] = level
        fine_ref[nest, 1] = COURANT * east_flux
        fine_ref[nest, 2] = COURANT * south_flux
        fine_ref[nest, 3] = (COURANT * COURANT) * open_east * depth_east
        fine_ref[nest, 4] = (COURANT * COURANT) * open_south * depth_south
        fine_ref[nest, 5] = HALF_SQUARE * open_east
        fine_ref[nest, 6] = HALF_SQUARE * open_south

    if tile_side:

        def find(n, count):
            p = place_ref[0, n]
            table_ref[count] = p - 6 * me
            return count + jnp.where(div6(p) == me, 1, 0)

        count = lax.fori_loop(0, NESTS, find, 0, unroll=True)
        nests = []
        for u in range(units):
            p = jnp.where(u < count, table_ref[u], 0)
            b = jnp.where(p >= SPOTS, 1, 0)
            c0 = LEFT + PW * (p - SPOTS * b)
            offset = small_lane - c0
            nests.append(
                Nest(
                    HALO + TOP + FR * b,
                    c0 - 1,
                    c0 + PW,
                    c0 + (small_lane >> 2),
                    jnp.clip(RR * offset, 0, COLS - RR),
                    (offset >= 0) & (offset < PW) & (u < count),
                )
            )
        keep = (lane < HALO) | (lane >= COLS - HALO)
        small_keep = (small_lane < HALO) | (small_lane >= COLS - HALO)
        beside = [rows_of(g * FR, PART, FR) for g in range(2)]
        for k in range(CHAN):
            for b in range(K):
                rows = pl.ds(HALO + b * FR, FR)
                outer_ref[k, rows, 0:COLS] = own(k, pl.ds(b * FR, FR))
                if k < LAST:
                    shift = HALF + HALO + 8 * (PART * b + k % PART)
                    side = pltpu.roll(beside[k // PART], COLS - shift, 1)
                else:
                    shift = HALF + 8 * PART * K + HALO * b
                    side = jnp.where(
                        lane < HALO,
                        pltpu.roll(beside[0], COLS - shift, 1),
                        pltpu.roll(beside[1], COLS - HALO - shift, 1),
                    )
                outer_ref[k, rows, COLS : 2 * COLS] = jnp.where(keep, side, 0.0)
            rim = jnp.where(
                small_lane < HALF,
                pltpu.roll(rows_of(8 * k, UNIT + PART, 8), HALF, 1),
                rows_of(8 * k, 2 * UNIT + PART, 8),
            )
            corner = jnp.where(small_keep, pltpu.roll(rows_of(8 * k, PART, 8), HALO, 1), 0.0)
            for columns, value in ((pl.ds(0, COLS), rim), (pl.ds(COLS, COLS), corner)):
                outer_ref[k, EXT - HALO : EXT, columns] = value[:HALO]
                outer_ref[k, 0:HALO, columns] = value[HALO:]
        for u in range(units):
            set_fine(u, [got(k, u) for k in range(CHAN)])
    else:

        def note_host(n, carry):
            table_ref[host_ref[0, n]] = place_ref[0, n]
            return carry

        def note_place(n, carry):
            table_ref[place_ref[0, n]] = 1
            return carry

        clear_table(table_ref, K * me, K)
        lax.fori_loop(0, NESTS, note_host, 0, unroll=True)
        at = [table_ref[K * me + s] for s in range(K)]
        live = [p >= 0 for p in at]
        bands = [3 * div3(jnp.where(live[s], at[s], 0)) for s in range(K)]
        spots = [jnp.where(live[s], at[s] - bands[s], 0) for s in range(K)]
        for s in range(K):
            clear_table(table_ref, bands[s], SPOTS)
        lax.fori_loop(0, NESTS, note_place, 0, unroll=True)
        nests = []
        for s in range(K):
            j = spots[s]
            r0 = HALO + TOP + FR * s
            c0 = LEFT + PW * j
            offset = small_lane - c0
            west = (j > 0) & (table_ref[bands[s] + jnp.where(j > 0, j - 1, 0)] == 1)
            last = SPOTS - 1
            east = (j < last) & (table_ref[bands[s] + jnp.where(j < last, j + 1, last)] == 1)
            nests.append(
                Nest(
                    r0,
                    c0 - 1,
                    c0 + PW,
                    c0 + (small_lane >> 2),
                    jnp.clip(RR * offset, 0, COLS - RR),
                    (offset >= 0) & (offset < PW) & live[s],
                )
            )
            around = c0 + jnp.where(small_lane < HALF, PW, -PW) + (small_lane >> 2)
            nests.append(
                Nest(
                    r0,
                    c0 + PW - 1,
                    c0,
                    jnp.clip(around, 0, COLS - 1),
                    jnp.clip(RR * jnp.where(offset < 0, offset + PW, offset - PW), 0, COLS - RR),
                    ((offset >= -PH) & (offset < 0) & west)
                    | ((offset >= PW) & (offset < PW + PH) & east),
                )
            )
            set_fine(2 * s, [own(k, pl.ds(s * FR, FR)) for k in range(CHAN)])
            ends = [got(k, s) for k in range(CHAN)]
            set_fine(2 * s + 1, ends)
            for k in range(LAST):
                outer_ref[k, pl.ds(HALO + s * FR, FR), 0:COLS] = jnp.where(
                    j == 0,
                    pltpu.roll(ends[k], COLS - PW, 1),
                    jnp.where(j == 1, ends[k], pltpu.roll(ends[k], PW, 1)),
                )
            left, right = (rows_of(g * FR, UNIT * s + PART, FR) for g in range(2))
            outer_ref[LAST, pl.ds(HALO + s * FR, FR), 0:COLS] = jnp.where(
                lane < HALF, pltpu.roll(left, HALF, 1), right
            )
        for k in range(CHAN):
            outer_ref[k, 0:HALO, 0:COLS] = jnp.zeros((HALO, COLS), jnp.float32)
            outer_ref[k, EXT - HALO : EXT, 0:COLS] = jnp.zeros((HALO, COLS), jnp.float32)
            outer_ref[k, :, COLS : 2 * COLS] = jnp.zeros((EXT, COLS), jnp.float32)

    for flux in (1, 2):
        outer_ref[flux] = COURANT * outer_ref[flux]
        outer_ref[flux + 2] = (COURANT * COURANT) * outer_ref[flux + 4] * outer_ref[flux + 2]

    inside = None
    if tile_side:
        ext_row = lax.broadcasted_iota(jnp.int32, (EXT, 2 * COLS), 0)
        ext_lane = lax.broadcasted_iota(jnp.int32, (EXT, 2 * COLS), 1)
        row_low = jnp.where(row == 0, HALO, 0)
        row_high = jnp.where(row == row_count - 1, EXT - HALO, EXT)
        right_end = jnp.where(col < col_count - 1, COLS + HALO, COLS)
        left_start = jnp.where(col > 0, 2 * COLS - HALO, 2 * COLS)
        inside = (
            (ext_row >= row_low)
            & (ext_row < row_high)
            & ((ext_lane < right_end) | (ext_lane >= left_start))
        )


    def take(x, index):
        return jnp.take_along_axis(x, index, axis=1, mode="promise_in_bounds")

    def block_of(k, start):
        return outer_ref[k, pl.ds(pl.multiple_of(start, 8), PH), 0:COLS]

    def ghosts(slot):
        ends = []
        for i, nest in enumerate(nests):
            west = pltpu.roll(block_of(1, nest.row), COLS - nest.west, 1)
            east = pltpu.roll(block_of(0, nest.row), COLS - 1 - nest.east, 1)
            side = jnp.where(small_lane == 0, west, east)
            for m in range(RR):
                rep_ref[slot, i, pl.ds(m, PH, stride=RR), :] = side
            north = block_of(2, nest.row - PH)[PH - 1 :]
            south = block_of(0, nest.row + PH)[:1]
            ends.append(
                tuple(
                    take(jnp.broadcast_to(edge, (PH, COLS)), nest.spread)
                    for edge in (north, south)
                )
            )
        return ends

    def above(x, edge):
        x = pltpu.roll(x, 1, 0)
        return jnp.concatenate([jnp.where(small_row == 0, edge, x[:PH]), x[PH:]], axis=0)

    def below(x, edge):
        x = pltpu.roll(x, FR - 1, 0)
        end = jnp.where(small_row == PH - 1, edge, x[FR - PH :])
        return jnp.concatenate([x[: FR - PH], end], axis=0)

    old_ends = ghosts(0)
    for step in range(STEPS):
        old, new = step % 2, (step + 1) % 2
        surface, eastward, southward = outer_ref[0], outer_ref[1], outer_ref[2]
        flow = (eastward - pltpu.roll(eastward, 1, 1)) + (southward - pltpu.roll(southward, 1, 0))
        surface = surface - flow
        if inside is not None:
            surface = jnp.where(inside, surface, 0.0)
        to_east = pltpu.roll(surface, 2 * COLS - 1, 1)
        to_south = pltpu.roll(surface, EXT - 1, 0)
        eastward = outer_ref[5] * (
            eastward - HALF_SQUARE * (surface + to_east) * (to_east - surface)
        ) - outer_ref[3] * (to_east - surface)
        southward = outer_ref[6] * (
            southward - HALF_SQUARE * (surface + to_south) * (to_south - surface)
        ) - outer_ref[4] * (to_south - surface)
        outer_ref[0] = surface
        outer_ref[1] = eastward
        outer_ref[2] = southward
        new_ends = ghosts(new)
        for i, spot in enumerate(nests):
            level, east_flux, south_flux = (fine_ref[i, k] for k in range(3))
            old_side, new_side = rep_ref[old, i], rep_ref[new, i]
            (old_north, old_south), (new_north, new_south) = old_ends[i], new_ends[i]
            for m in range(1, RR + 1):
                part = m / RR
                side = old_side + part * (new_side - old_side)
                north = old_north + part * (new_north - old_north)
                south = old_south + part * (new_south - old_south)
                west_of = jnp.where(lane == 0, side, pltpu.roll(east_flux, 1, 1))
                north_of = above(south_flux, north)
                level = level - ((east_flux - west_of) + (south_flux - north_of))
                east_of = jnp.where(lane == COLS - 1, side, pltpu.roll(level, COLS - 1, 1))
                south_of = below(level, south)
                half_east, half_south = fine_ref[i, 5], fine_ref[i, 6]
                if step == 0 and m == 1:
                    east_flux = jnp.where(half_east == 0.0, 0.0, east_flux)
                    south_flux = jnp.where(half_south == 0.0, 0.0, south_flux)
                east_flux = east_flux - (fine_ref[i, 3] + half_east * (level + east_of)) * (
                    east_of - level
                )
                south_flux = south_flux - (fine_ref[i, 4] + half_south * (level + south_of)) * (
                    south_of - level
                )
            for k, value in enumerate((level, east_flux, south_flux)):
                fine_ref[i, k] = value

            def every(k, m):
                return fine_ref[i, k, pl.ds(m, PH, stride=RR), :]

            def quads(x):
                parts = [take(x, spot.gather + m) for m in range(RR)]
                return (parts[0] + parts[1]) + (parts[2] + parts[3])

            sum_level = (every(0, 0) + every(0, 1)) + (every(0, 2) + every(0, 3))
            sum_east = (every(1, 0) + every(1, 1)) + (every(1, 2) + every(1, 3))
            back = (
                quads(sum_level) * (1.0 / (RR * RR)),
                take(sum_east, spot.gather + (RR - 1)) * (1.0 / RR),
                quads(every(2, RR - 1)) * (1.0 / RR),
            )
            rows = pl.ds(pl.multiple_of(spot.row, 8), PH)
            for k in range(3):
                pltpu.store(outer_ref.at[k, rows, 0:COLS], back[k], mask=spot.covers)
        old_ends = new_ends

    for k in range(3):
        scale = 1.0 if k == 0 else 1.0 / COURANT
        if tile_side:
            out_ref[0, k] = outer_ref[k, HALO : HALO + ROWS, 0:COLS] * scale
        else:
            for s in range(K):
                rows = pl.ds(s * FR, FR)
                out_ref[0, k, rows, :] = jnp.where(
                    live[s], fine_ref[2 * s, k] * scale, state_ref[0, k, rows, :]
                )


def window(tile_side, units, place, host, pieces, halos, others, state, depth, opening):
    block = UNIT * units
    nests = units if tile_side else K * 2
    table = pltpu.SMEM((PEERS * K * SPOTS,), jnp.int32)
    blocks = pl.pallas_call(
        functools.partial(compact_tiles_kernel, units) if tile_side else compact_slots_kernel,
        out_shape=jax.ShapeDtypeStruct((PEERS * block, COLS), jnp.float32),
        in_specs=[SMEM, SMEM, VMEM, VMEM],
        out_specs=VMEM,
        scratch_shapes=[table],
        compiler_params=pltpu.CompilerParams(vmem_limit_bytes=8 * 1024 * 1024),
        name="compact_tiles" if tile_side else "compact_slots",
    )(place, host, halos if tile_side else pieces.reshape(-1, COLS), others.reshape(-1, COLS))
    got = lax.all_to_all(
        blocks.reshape(PEERS, block, COLS),
        ("row", "nest"),
        split_axis=0,
        concat_axis=0,
        tiled=True,
    )
    return pl.pallas_call(
        functools.partial(window_kernel, tile_side, units),
        out_shape=jax.ShapeDtypeStruct(state.shape, jnp.float32),
        in_specs=[SMEM, SMEM, VMEM, VMEM, VMEM, VMEM],
        out_specs=VMEM,
        scratch_shapes=[
            pltpu.VMEM((CHAN, EXT, 2 * COLS), jnp.float32),
            pltpu.VMEM((nests, CHAN, FR, COLS), jnp.float32),
            pltpu.VMEM((2, nests, FR, COLS), jnp.float32),
            table,
        ],
        compiler_params=pltpu.CompilerParams(vmem_limit_bytes=32 * 1024 * 1024),
        name="window_tiles" if tile_side else "window_slots",
    )(place, host, state, depth, opening, got.reshape(-1, COLS))


def on_device(ocean_state, face_depth, face_open, nest_place, nest_host):
    tiles = ("row", "nest")
    packed, place, host = pl.pallas_call(
        pack_kernel,
        out_shape=(
            jax.ShapeDtypeStruct((PEERS * 8, COLS), jnp.float32),
            jax.ShapeDtypeStruct((1, NESTS), jnp.int32),
            jax.ShapeDtypeStruct((1, NESTS), jnp.int32),
        ),
        in_specs=[pl.BlockSpec(memory_space=pltpu.HBM)] * 5,
        out_specs=(VMEM, VMEM, VMEM),
        scratch_shapes=[
            pltpu.VMEM(ocean_state.shape, jnp.float32),
            pltpu.VMEM(face_depth.shape, jnp.float32),
            pltpu.VMEM(face_open.shape, jnp.int32),
            pltpu.SemaphoreType.DMA((5,)),
        ],
        compiler_params=pltpu.CompilerParams(vmem_limit_bytes=4 * 1024 * 1024),
        name="pack",
    )(*(
        pltpu.with_memory_space_constraint(x, pltpu.HBM)
        for x in (nest_place.reshape(1, NESTS), nest_host.reshape(1, NESTS), ocean_state, face_depth, face_open)
    ))
    pieces = lax.all_to_all(
        packed.reshape(PEERS, 8, COLS), tiles, split_axis=0, concat_axis=0, tiled=True
    )
    others = lax.ppermute(pieces, "sec", [(0, 1), (1, 0)])
    crowded, halos = pl.pallas_call(
        prepare_kernel,
        out_shape=(
            jax.ShapeDtypeStruct((1, 1), jnp.int32),
            jax.ShapeDtypeStruct((SPOTS, PEERS, COLS), jnp.float32),
        ),
        in_specs=[VMEM, VMEM],
        out_specs=(VMEM, VMEM),
        compiler_params=pltpu.CompilerParams(vmem_limit_bytes=4 * 1024 * 1024),
        name="prepare",
    )(place, pieces.reshape(-1, COLS))
    which = jnp.where(lax.axis_index("sec") == 0, crowded[0, 0], 2)
    return lax.switch(
        which,
        [
            functools.partial(window, True, FEW),
            functools.partial(window, True, MANY),
            functools.partial(window, False, SLOT_UNITS),
        ],
        place, host, pieces, halos, others, ocean_state, face_depth, face_open,
    )


def solution(mesh):
    placed = (
        P("sec", None, "row", "nest"),
        P("sec", None, "row", "nest"),
        P("sec", None, "row", "nest"),
        P(),
        P(),
    )
    return jax.shard_map(
        on_device,
        mesh=mesh,
        in_specs=placed,
        out_specs=P("sec", None, "row", "nest"),
        check_vma=False,
    )
```

```python
import functools
from typing import NamedTuple

import jax
import jax.numpy as jnp
from jax import lax
from jax.experimental import pallas as pl
from jax.experimental.pallas import tpu as pltpu
from jax.sharding import PartitionSpec as P

PH = 8
PW = 32
RR = 4
K = 2
STEPS = 4
NESTS = 64
COURANT = 0.3

ROWS = 64
COLS = 128
FR = RR * PH
SPOTS = RR - 1
PEERS = 64
HALO = 4
EXT = ROWS + 2 * HALO
TOP = (RR - 1) * PH // 2
LEFT = PW // 2
CHAN = 7
UNIT = 4
FEW = 4
MANY = K * SPOTS
SLOT_UNITS = K
HALF = COLS // 2
LAST = CHAN - 1
PART = LAST // 2
HALF_SQUARE = 0.5 * COURANT * COURANT

VMEM = pl.BlockSpec(memory_space=pltpu.VMEM)
SMEM = pl.BlockSpec(memory_space=pltpu.SMEM)


def div6(p):
    return (p * 10923) >> 16


def div3(p):
    return (p * 21846) >> 16


def pack_kernel(
    place_in, host_in, state_in, depth_in, open_in,
    out_ref, place_ref, host_ref, state_ref, depth_ref, open_ref, sems,
):
    moves = [
        pltpu.make_async_copy(source, target, sems.at[i])
        for i, (source, target) in enumerate(
            (
                (state_in, state_ref), (depth_in, depth_ref), (open_in, open_ref),
                (place_in, place_ref), (host_in, host_ref),
            )
        )
    ]
    for move in moves:
        move.start()
    for move in moves:
        move.wait()

    def channel(k, rows):
        if k < 3:
            return state_ref[0, k, rows, :]
        if k < 5:
            return depth_ref[0, k - 3, rows, :]
        return open_ref[0, k - 5, rows, :].astype(jnp.float32)

    first = lax.broadcasted_iota(jnp.int32, (8, COLS), 0) < HALO
    rims = [
        jnp.where(first, channel(k, pl.ds(0, 8)), channel(k, pl.ds(ROWS - 8, 8)))
        for k in range(CHAN)
    ]
    rims = jnp.concatenate(rims + [jnp.zeros((8, COLS), jnp.float32)], axis=0)
    left = lax.broadcasted_iota(jnp.int32, (FR, COLS), 1) < HALF
    for b in range(K):
        rows = pl.ds(b * FR, FR)
        for g in range(2):
            base = g * FR * 8 + b * UNIT
            for c in range(PART):
                out_ref[pl.ds(base + c, FR, stride=8), :] = channel(PART * g + c, rows)
            half = channel(LAST, rows)
            rim = rims[g * FR : (g + 1) * FR]
            if g == 1:
                half = pltpu.roll(half, HALF, 1)
            if b == 0:
                rim = pltpu.roll(rim, HALF, 1)
            out_ref[pl.ds(base + PART, FR, stride=8), :] = jnp.where(left, half, rim)


def prepare_kernel(place_ref, own_ref, crowded_ref, halo_ref):
    me = lax.axis_index("row") * lax.axis_size("nest") + lax.axis_index("nest")
    hit_tile = lax.broadcasted_iota(jnp.int32, (PEERS, NESTS), 0)
    hits = jnp.where(div6(place_ref[...]) == hit_tile, 1.0, 0.0)
    most = jnp.max(jnp.sum(hits, axis=1, keepdims=True), axis=0, keepdims=True)
    crowded_ref[...] = jnp.where(most > FEW, 1, 0)

    tile = lax.broadcasted_iota(jnp.int32, (PEERS, COLS), 0)
    lane = lax.broadcasted_iota(jnp.int32, (PEERS, COLS), 1)
    tile_col = tile & 7
    has_right, has_left = tile_col < 7, tile_col > 0
    lower_half = me < FR
    to_above = ((me >> 2) & 1) == 0

    def right_of(x):
        return pltpu.roll(x, PEERS - 1, 0)

    def left_of(x):
        return pltpu.roll(x, 1, 0)

    def row_of(i):
        return own_ref[pl.ds(i, PEERS, stride=8), :]

    packed = jnp.zeros((PEERS, COLS), jnp.float32)
    rims = []
    for b in range(K):
        for c in range(PART):
            x = row_of(UNIT * b + c)
            side = jnp.where(
                has_right & (lane < HALO),
                right_of(x),
                jnp.where(has_left & (lane >= COLS - HALO), left_of(x), 0.0),
            )
            packed += pltpu.roll(side, HALF + HALO + 8 * (PART * b + c), 1)
        x = row_of(UNIT * b + PART)
        right = jnp.where(has_right & (lane < HALO), right_of(x), 0.0)
        left = jnp.where(has_left & (lane >= HALF - HALO) & (lane < HALF), left_of(x), 0.0)
        spot = HALF + 8 * PART * K + HALO * b
        packed += jnp.where(
            lower_half, pltpu.roll(right, spot, 1), pltpu.roll(left, spot - HALF + HALO, 1)
        )
        rims.append(
            jnp.where(
                to_above,
                jnp.where(tile < PEERS - 8, pltpu.roll(x, PEERS - 8, 0), 0.0),
                jnp.where(tile >= 8, pltpu.roll(x, 8, 0), 0.0),
            )
        )
    right = jnp.where(has_right & (lane >= HALF) & (lane < HALF + HALO), right_of(rims[0]), 0.0)
    left = jnp.where(has_left & (lane >= COLS - HALO), left_of(rims[1]), 0.0)
    packed += pltpu.roll(right, HALF - HALO, 1) + pltpu.roll(left, COLS - HALO, 1)
    for u, value in enumerate([packed] + rims):
        halo_ref[u] = value


def clear_table(table_ref, first, count, value=-1):
    for i in range(count):
        table_ref[first + i] = value


def compact_tiles_kernel(units, place_ref, host_ref, halo_ref, other_ref, out_ref, table_ref):
    block = UNIT * units
    used = (lax.broadcasted_iota(jnp.int32, (UNIT, COLS), 1) < HALF) | (
        lax.broadcasted_iota(jnp.int32, (UNIT, COLS), 0) < PART
    )

    out_ref[...] = jnp.zeros_like(out_ref)
    lane = lax.broadcasted_iota(jnp.int32, (PEERS, COLS), 1)
    for u in range(SPOTS):
        spot = pl.ds(UNIT * u + PART, PEERS, stride=block)
        out_ref[spot, :] = jnp.where(lane >= HALF, halo_ref[u], 0.0)
    clear_table(table_ref, 0, PEERS, 0)

    def place_one(n, carry):
        h = host_ref[0, n]
        t = div6(place_ref[0, n])
        u = table_ref[t]
        table_ref[t] = u + 1
        piece = other_ref[pl.ds(pl.multiple_of(h * UNIT, UNIT), UNIT), :]
        spot = pl.ds(pl.multiple_of(t * block + u * UNIT, UNIT), UNIT)
        pltpu.store(out_ref.at[spot, :], piece, mask=used)
        return carry

    lax.fori_loop(0, NESTS, place_one, 0, unroll=True)


def compact_slots_kernel(place_ref, host_ref, own_ref, other_ref, out_ref, table_ref):
    me = lax.axis_index("row") * lax.axis_size("nest") + lax.axis_index("nest")
    lane = lax.broadcasted_iota(jnp.int32, (UNIT, COLS), 1)
    whole = lax.broadcasted_iota(jnp.int32, (UNIT, COLS), 0) < PART
    is_outer = jnp.where(whole, jnp.where((lane >= PW) & (lane < COLS - PW), 1, 0), 0)
    is_outer = jnp.where(whole | (lane < HALF), is_outer, 1)
    is_east = jnp.where(whole, jnp.where(lane < HALF, 1, 0), jnp.where(me < FR, 1, 0))

    def unit(source_ref, i):
        return source_ref[pl.ds(pl.multiple_of(i * UNIT, UNIT), UNIT), :]

    def clear(n, carry):
        clear_table(table_ref, 3 * div3(place_ref[0, n]), SPOTS, 0)
        return carry

    def note(n, carry):
        table_ref[place_ref[0, n]] = host_ref[0, n]
        return carry

    def gather_band(n, carry):
        p = place_ref[0, n]
        h = host_ref[0, n]
        band = div3(p)
        j = p - 3 * band
        west = unit(own_ref, table_ref[3 * band + jnp.where(j == 0, 0, j - 1)])
        east = unit(own_ref, table_ref[3 * band + jnp.where(j == SPOTS - 1, SPOTS - 1, j + 1)])
        outer = unit(other_ref, band)
        moved = jnp.where(
            j == 0, pltpu.roll(outer, PW, 1), jnp.where(j == 1, outer, pltpu.roll(outer, COLS - PW, 1))
        )
        outer = jnp.where(whole, moved, pltpu.roll(outer, HALF, 1))
        value = jnp.where(is_outer == 1, outer, jnp.where(is_east == 1, east, west))
        out_ref[pl.ds(pl.multiple_of(h * UNIT, UNIT), UNIT), :] = value
        return carry

    out_ref[...] = jnp.zeros_like(out_ref)
    lax.fori_loop(0, NESTS, clear, 0, unroll=True)
    lax.fori_loop(0, NESTS, note, 0, unroll=True)
    lax.fori_loop(0, NESTS, gather_band, 0, unroll=8)


class Nest(NamedTuple):
    row: int | jax.Array
    west: jax.Array
    east: jax.Array
    spread: jax.Array
    gather: jax.Array
    covers: jax.Array


def window_kernel(
    tile_side, units, place_ref, host_ref, state_ref, depth_ref, open_ref, got_ref, out_ref,
    outer_ref, fine_ref, rep_ref, table_ref,
):
    row = lax.axis_index("row")
    col = lax.axis_index("nest")
    row_count = lax.axis_size("row")
    col_count = lax.axis_size("nest")
    me = row * col_count + col
    block = UNIT * units
    lane = lax.broadcasted_iota(jnp.int32, (FR, COLS), 1)
    small_row = lax.broadcasted_iota(jnp.int32, (PH, COLS), 0)
    small_lane = lax.broadcasted_iota(jnp.int32, (PH, COLS), 1)

    def own(k, rows):
        if k < 3:
            return state_ref[0, k, rows, :]
        if k < 5:
            return depth_ref[0, k - 3, rows, :]
        return open_ref[0, k - 5, rows, :].astype(jnp.float32)

    def rows_of(peer, row, count):
        return got_ref[pl.ds(peer * block + row, count, stride=block), :]

    def got(k, unit):
        if k < LAST:
            return rows_of((k // PART) * FR, UNIT * unit + k % PART, FR)
        left, right = (rows_of(g * FR, UNIT * unit + PART, FR) for g in range(2))
        return jnp.where(lane < HALF, left, pltpu.roll(right, HALF, 1))

    def set_fine(nest, values):
        level, east_flux, south_flux, depth_east, depth_south, open_east, open_south = values
        fine_ref[nest, 0] = level
        fine_ref[nest, 1] = COURANT * east_flux
        fine_ref[nest, 2] = COURANT * south_flux
        fine_ref[nest, 3] = (COURANT * COURANT) * open_east * depth_east
        fine_ref[nest, 4] = (COURANT * COURANT) * open_south * depth_south
        fine_ref[nest, 5] = HALF_SQUARE * open_east
        fine_ref[nest, 6] = HALF_SQUARE * open_south

    if tile_side:

        def find(n, count):
            p = place_ref[0, n]
            table_ref[count] = p - 6 * me
            return count + jnp.where(div6(p) == me, 1, 0)

        count = lax.fori_loop(0, NESTS, find, 0, unroll=True)
        nests = []
        for u in range(units):
            p = jnp.where(u < count, table_ref[u], 0)
            b = jnp.where(p >= SPOTS, 1, 0)
            c0 = LEFT + PW * (p - SPOTS * b)
            offset = small_lane - c0
            nests.append(
                Nest(
                    HALO + TOP + FR * b,
                    c0 - 1,
                    c0 + PW,
                    c0 + (small_lane >> 2),
                    jnp.clip(RR * offset, 0, COLS - RR),
                    (offset >= 0) & (offset < PW) & (u < count),
                )
            )
        keep = (lane < HALO) | (lane >= COLS - HALO)
        small_keep = (small_lane < HALO) | (small_lane >= COLS - HALO)
        beside = [rows_of(g * FR, PART, FR) for g in range(2)]
        for k in range(CHAN):
            for b in range(K):
                rows = pl.ds(HALO + b * FR, FR)
                outer_ref[k, rows, 0:COLS] = own(k, pl.ds(b * FR, FR))
                if k < LAST:
                    shift = HALF + HALO + 8 * (PART * b + k % PART)
                    side = pltpu.roll(beside[k // PART], COLS - shift, 1)
                else:
                    shift = HALF + 8 * PART * K + HALO * b
                    side = jnp.where(
                        lane < HALO,
                        pltpu.roll(beside[0], COLS - shift, 1),
                        pltpu.roll(beside[1], COLS - HALO - shift, 1),
                    )
                outer_ref[k, rows, COLS : 2 * COLS] = jnp.where(keep, side, 0.0)
            rim = jnp.where(
                small_lane < HALF,
                pltpu.roll(rows_of(8 * k, UNIT + PART, 8), HALF, 1),
                rows_of(8 * k, 2 * UNIT + PART, 8),
            )
            corner = jnp.where(small_keep, pltpu.roll(rows_of(8 * k, PART, 8), HALO, 1), 0.0)
            for columns, value in ((pl.ds(0, COLS), rim), (pl.ds(COLS, COLS), corner)):
                outer_ref[k, EXT - HALO : EXT, columns] = value[:HALO]
                outer_ref[k, 0:HALO, columns] = value[HALO:]
        for u in range(units):
            set_fine(u, [got(k, u) for k in range(CHAN)])
    else:

        def note_host(n, carry):
            table_ref[host_ref[0, n]] = place_ref[0, n]
            return carry

        def note_place(n, carry):
            table_ref[place_ref[0, n]] = 1
            return carry

        clear_table(table_ref, K * me, K)
        lax.fori_loop(0, NESTS, note_host, 0, unroll=True)
        at = [table_ref[K * me + s] for s in range(K)]
        live = [p >= 0 for p in at]
        bands = [3 * div3(jnp.where(live[s], at[s], 0)) for s in range(K)]
        spots = [jnp.where(live[s], at[s] - bands[s], 0) for s in range(K)]
        for s in range(K):
            clear_table(table_ref, bands[s], SPOTS)
        lax.fori_loop(0, NESTS, note_place, 0, unroll=True)
        nests = []
        for s in range(K):
            j = spots[s]
            r0 = HALO + TOP + FR * s
            c0 = LEFT + PW * j
            offset = small_lane - c0
            west = (j > 0) & (table_ref[bands[s] + jnp.where(j > 0, j - 1, 0)] == 1)
            last = SPOTS - 1
            east = (j < last) & (table_ref[bands[s] + jnp.where(j < last, j + 1, last)] == 1)
            nests.append(
                Nest(
                    r0,
                    c0 - 1,
                    c0 + PW,
                    c0 + (small_lane >> 2),
                    jnp.clip(RR * offset, 0, COLS - RR),
                    (offset >= 0) & (offset < PW) & live[s],
                )
            )
            around = c0 + jnp.where(small_lane < HALF, PW, -PW) + (small_lane >> 2)
            nests.append(
                Nest(
                    r0,
                    c0 + PW - 1,
                    c0,
                    jnp.clip(around, 0, COLS - 1),
                    jnp.clip(RR * jnp.where(offset < 0, offset + PW, offset - PW), 0, COLS - RR),
                    ((offset >= -PH) & (offset < 0) & west)
                    | ((offset >= PW) & (offset < PW + PH) & east),
                )
            )
            set_fine(2 * s, [own(k, pl.ds(s * FR, FR)) for k in range(CHAN)])
            ends = [got(k, s) for k in range(CHAN)]
            set_fine(2 * s + 1, ends)
            for k in range(LAST):
                outer_ref[k, pl.ds(HALO + s * FR, FR), 0:COLS] = jnp.where(
                    j == 0,
                    pltpu.roll(ends[k], COLS - PW, 1),
                    jnp.where(j == 1, ends[k], pltpu.roll(ends[k], PW, 1)),
                )
            left, right = (rows_of(g * FR, UNIT * s + PART, FR) for g in range(2))
            outer_ref[LAST, pl.ds(HALO + s * FR, FR), 0:COLS] = jnp.where(
                lane < HALF, pltpu.roll(left, HALF, 1), right
            )
        for k in range(CHAN):
            outer_ref[k, 0:HALO, 0:COLS] = jnp.zeros((HALO, COLS), jnp.float32)
            outer_ref[k, EXT - HALO : EXT, 0:COLS] = jnp.zeros((HALO, COLS), jnp.float32)
            outer_ref[k, :, COLS : 2 * COLS] = jnp.zeros((EXT, COLS), jnp.float32)

    for flux in (1, 2):
        outer_ref[flux] = COURANT * outer_ref[flux]
        outer_ref[flux + 2] = (COURANT * COURANT) * outer_ref[flux + 4] * outer_ref[flux + 2]

    inside = None
    if tile_side:
        ext_row = lax.broadcasted_iota(jnp.int32, (EXT, 2 * COLS), 0)
        ext_lane = lax.broadcasted_iota(jnp.int32, (EXT, 2 * COLS), 1)
        row_low = jnp.where(row == 0, HALO, 0)
        row_high = jnp.where(row == row_count - 1, EXT - HALO, EXT)
        right_end = jnp.where(col < col_count - 1, COLS + HALO, COLS)
        left_start = jnp.where(col > 0, 2 * COLS - HALO, 2 * COLS)
        inside = (
            (ext_row >= row_low)
            & (ext_row < row_high)
            & ((ext_lane < right_end) | (ext_lane >= left_start))
        )


    def take(x, index):
        return jnp.take_along_axis(x, index, axis=1, mode="promise_in_bounds")

    def block_of(k, start):
        return outer_ref[k, pl.ds(pl.multiple_of(start, 8), PH), 0:COLS]

    def ghosts(slot):
        ends = []
        for i, nest in enumerate(nests):
            west = pltpu.roll(block_of(1, nest.row), COLS - nest.west, 1)
            east = pltpu.roll(block_of(0, nest.row), COLS - 1 - nest.east, 1)
            side = jnp.where(small_lane == 0, west, east)
            for m in range(RR):
                rep_ref[slot, i, pl.ds(m, PH, stride=RR), :] = side
            north = block_of(2, nest.row - PH)[PH - 1 :]
            south = block_of(0, nest.row + PH)[:1]
            ends.append(
                tuple(
                    take(jnp.broadcast_to(edge, (PH, COLS)), nest.spread)
                    for edge in (north, south)
                )
            )
        return ends

    def above(x, edge):
        x = pltpu.roll(x, 1, 0)
        return jnp.concatenate([jnp.where(small_row == 0, edge, x[:PH]), x[PH:]], axis=0)

    def below(x, edge):
        x = pltpu.roll(x, FR - 1, 0)
        end = jnp.where(small_row == PH - 1, edge, x[FR - PH :])
        return jnp.concatenate([x[: FR - PH], end], axis=0)

    old_ends = ghosts(0)
    for step in range(STEPS):
        old, new = step % 2, (step + 1) % 2
        surface, eastward, southward = outer_ref[0], outer_ref[1], outer_ref[2]
        flow = (eastward - pltpu.roll(eastward, 1, 1)) + (southward - pltpu.roll(southward, 1, 0))
        surface = surface - flow
        if inside is not None:
            surface = jnp.where(inside, surface, 0.0)
        to_east = pltpu.roll(surface, 2 * COLS - 1, 1)
        to_south = pltpu.roll(surface, EXT - 1, 0)
        eastward = outer_ref[5] * (
            eastward - HALF_SQUARE * (surface + to_east) * (to_east - surface)
        ) - outer_ref[3] * (to_east - surface)
        southward = outer_ref[6] * (
            southward - HALF_SQUARE * (surface + to_south) * (to_south - surface)
        ) - outer_ref[4] * (to_south - surface)
        outer_ref[0] = surface
        outer_ref[1] = eastward
        outer_ref[2] = southward
        new_ends = ghosts(new)
        for i, spot in enumerate(nests):
            level, east_flux, south_flux = (fine_ref[i, k] for k in range(3))
            old_side, new_side = rep_ref[old, i], rep_ref[new, i]
            (old_north, old_south), (new_north, new_south) = old_ends[i], new_ends[i]
            for m in range(1, RR + 1):
                part = m / RR
                side = old_side + part * (new_side - old_side)
                north = old_north + part * (new_north - old_north)
                south = old_south + part * (new_south - old_south)
                west_of = jnp.where(lane == 0, side, pltpu.roll(east_flux, 1, 1))
                north_of = above(south_flux, north)
                level = level - ((east_flux - west_of) + (south_flux - north_of))
                east_of = jnp.where(lane == COLS - 1, side, pltpu.roll(level, COLS - 1, 1))
                south_of = below(level, south)
                half_east, half_south = fine_ref[i, 5], fine_ref[i, 6]
                if step == 0 and m == 1:
                    east_flux = jnp.where(half_east == 0.0, 0.0, east_flux)
                    south_flux = jnp.where(half_south == 0.0, 0.0, south_flux)
                east_flux = east_flux - (fine_ref[i, 3] + half_east * (level + east_of)) * (
                    east_of - level
                )
                south_flux = south_flux - (fine_ref[i, 4] + half_south * (level + south_of)) * (
                    south_of - level
                )
            for k, value in enumerate((level, east_flux, south_flux)):
                fine_ref[i, k] = value

            def every(k, m):
                return fine_ref[i, k, pl.ds(m, PH, stride=RR), :]

            def quads(x):
                parts = [take(x, spot.gather + m) for m in range(RR)]
                return (parts[0] + parts[1]) + (parts[2] + parts[3])

            sum_level = (every(0, 0) + every(0, 1)) + (every(0, 2) + every(0, 3))
            sum_east = (every(1, 0) + every(1, 1)) + (every(1, 2) + every(1, 3))
            back = (
                quads(sum_level) * (1.0 / (RR * RR)),
                take(sum_east, spot.gather + (RR - 1)) * (1.0 / RR),
                quads(every(2, RR - 1)) * (1.0 / RR),
            )
            rows = pl.ds(pl.multiple_of(spot.row, 8), PH)
            for k in range(3):
                pltpu.store(outer_ref.at[k, rows, 0:COLS], back[k], mask=spot.covers)
        old_ends = new_ends

    for k in range(3):
        scale = 1.0 if k == 0 else 1.0 / COURANT
        if tile_side:
            out_ref[0, k] = outer_ref[k, HALO : HALO + ROWS, 0:COLS] * scale
        else:
            for s in range(K):
                rows = pl.ds(s * FR, FR)
                out_ref[0, k, rows, :] = jnp.where(
                    live[s], fine_ref[2 * s, k] * scale, state_ref[0, k, rows, :]
                )


def window(tile_side, units, place, host, pieces, halos, others, state, depth, opening):
    block = UNIT * units
    nests = units if tile_side else K * 2
    table = pltpu.SMEM((PEERS * K * SPOTS,), jnp.int32)
    blocks = pl.pallas_call(
        functools.partial(compact_tiles_kernel, units) if tile_side else compact_slots_kernel,
        out_shape=jax.ShapeDtypeStruct((PEERS * block, COLS), jnp.float32),
        in_specs=[SMEM, SMEM, VMEM, VMEM],
        out_specs=VMEM,
        scratch_shapes=[table],
        compiler_params=pltpu.CompilerParams(vmem_limit_bytes=8 * 1024 * 1024),
        name="compact_tiles" if tile_side else "compact_slots",
    )(place, host, halos if tile_side else pieces.reshape(-1, COLS), others.reshape(-1, COLS))
    got = lax.all_to_all(
        blocks.reshape(PEERS, block, COLS),
        ("row", "nest"),
        split_axis=0,
        concat_axis=0,
        tiled=True,
    )
    return pl.pallas_call(
        functools.partial(window_kernel, tile_side, units),
        out_shape=jax.ShapeDtypeStruct(state.shape, jnp.float32),
        in_specs=[SMEM, SMEM, VMEM, VMEM, VMEM, VMEM],
        out_specs=VMEM,
        scratch_shapes=[
            pltpu.VMEM((CHAN, EXT, 2 * COLS), jnp.float32),
            pltpu.VMEM((nests, CHAN, FR, COLS), jnp.float32),
            pltpu.VMEM((2, nests, FR, COLS), jnp.float32),
            table,
        ],
        compiler_params=pltpu.CompilerParams(vmem_limit_bytes=32 * 1024 * 1024),
        name="window_tiles" if tile_side else "window_slots",
    )(place, host, state, depth, opening, got.reshape(-1, COLS))


def on_device(ocean_state, face_depth, face_open, nest_place, nest_host):
    tiles = ("row", "nest")
    packed, place, host = pl.pallas_call(
        pack_kernel,
        out_shape=(
            jax.ShapeDtypeStruct((PEERS * 8, COLS), jnp.float32),
            jax.ShapeDtypeStruct((1, NESTS), jnp.int32),
            jax.ShapeDtypeStruct((1, NESTS), jnp.int32),
        ),
        in_specs=[pl.BlockSpec(memory_space=pltpu.HBM)] * 5,
        out_specs=(VMEM, VMEM, VMEM),
        scratch_shapes=[
            pltpu.VMEM(ocean_state.shape, jnp.float32),
            pltpu.VMEM(face_depth.shape, jnp.float32),
            pltpu.VMEM(face_open.shape, jnp.int32),
            pltpu.SemaphoreType.DMA((5,)),
        ],
        compiler_params=pltpu.CompilerParams(vmem_limit_bytes=4 * 1024 * 1024),
        name="pack",
    )(*(
        pltpu.with_memory_space_constraint(x, pltpu.HBM)
        for x in (nest_place.reshape(1, NESTS), nest_host.reshape(1, NESTS), ocean_state, face_depth, face_open)
    ))
    pieces = lax.all_to_all(
        packed.reshape(PEERS, 8, COLS), tiles, split_axis=0, concat_axis=0, tiled=True
    )
    others = lax.ppermute(pieces, "sec", [(0, 1), (1, 0)])
    crowded, halos = pl.pallas_call(
        prepare_kernel,
        out_shape=(
            jax.ShapeDtypeStruct((1, 1), jnp.int32),
            jax.ShapeDtypeStruct((SPOTS, PEERS, COLS), jnp.float32),
        ),
        in_specs=[VMEM, VMEM],
        out_specs=(VMEM, VMEM),
        compiler_params=pltpu.CompilerParams(vmem_limit_bytes=4 * 1024 * 1024),
        name="prepare",
    )(place, pieces.reshape(-1, COLS))
    which = jnp.where(lax.axis_index("sec") == 0, crowded[0, 0], 2)
    return lax.switch(
        which,
        [
            functools.partial(window, True, FEW),
            functools.partial(window, True, MANY),
            functools.partial(window, False, SLOT_UNITS),
        ],
        place, host, pieces, halos, others, ocean_state, face_depth, face_open,
    )


def solution(mesh):
    placed = (
        P("sec", None, "row", "nest"),
        P("sec", None, "row", "nest"),
        P("sec", None, "row", "nest"),
        P(),
        P(),
    )
    return jax.shard_map(
        on_device,
        mesh=mesh,
        in_specs=placed,
        out_specs=P("sec", None, "row", "nest"),
        check_vma=False,
    )
```
